32 devices in a mesh: seq: 8 (over z, x), rows: 4 (over y, core).
Axes of the slice: x: 2, y: 2, z: 4, core: 2. Of those that a mesh axis runs over, the one named last changes fastest.
Arguments:
- tokens: bfloat16 [8, 1024, 768], P('rows', 'seq'), may hold values from -12 to 12
- query_weight: bfloat16 [768, 768], P(('seq', 'rows')), may hold values from -0.21875 to 0.21875
- query_bias: bfloat16 [768], P(('seq', 'rows')), may hold values from -1 to 1
- key_weight: bfloat16 [768, 768], P(('seq', 'rows')), may hold values from -0.21875 to 0.21875
- key_bias: bfloat16 [768], P(('seq', 'rows')), may hold values from -1 to 1
- value_weight: bfloat16 [768, 768], P(('seq', 'rows')), may hold values from -0.21875 to 0.21875
- value_bias: bfloat16 [768], P(('seq', 'rows')), may hold values from -0.25 to 0.25
- output_weight: bfloat16 [768, 768], P(('seq', 'rows')), may hold values from -1.75 to 1.75
- output_bias: bfloat16 [768], P(('seq', 'rows')), may hold values from -1 to 1
- first_gain: bfloat16 [768], P(('seq', 'rows')), may hold values from 0.25 to 1.75
- first_shift: bfloat16 [768], P(('seq', 'rows')), may hold values from -1.5 to 1.5
- up_weight: bfloat16 [768, 3072], P(('seq', 'rows')), may hold values from -0.21875 to 0.21875
- up_bias: bfloat16 [3072], P(('seq', 'rows')), may hold values from -1 to 1
- down_weight: bfloat16 [3072, 768], P(('seq', 'rows')), may hold values from -0.109375 to 0.109375
- down_bias: bfloat16 [768], P(('seq', 'rows')), may hold values from -1 to 1
- second_gain: bfloat16 [768], P(('seq', 'rows')), may hold values from 0.25 to 1.75
- second_shift: bfloat16 [768], P(('seq', 'rows')), may hold values from -1.5 to 1.5
- position_bias: float32 [12, 129], replicated, may hold values from -1 to 3
- feature_matrix: float32 [12, 64, 64], replicated, may hold values from -4 to 4
- cotangent: bfloat16 [8, 1024, 768], P('rows', 'seq'), may hold values from -6 to 6
Outputs:
- layer_output: float32 [8, 1024, 768], P('rows', 'seq')
- token_grads: float32 [8, 1024, 768], P('rows', 'seq')
- query_weight_grad: float32 [768, 768], P(('seq', 'rows'))
- query_bias_grad: float32 [768], P(('seq', 'rows'))
- key_weight_grad: float32 [768, 768], P(('seq', 'rows'))
- key_bias_grad: float32 [768], P(('seq', 'rows'))
- value_weight_grad: float32 [768, 768], P(('seq', 'rows'))
- value_bias_grad: float32 [768], P(('seq', 'rows'))
- output_weight_grad: float32 [768, 768], P(('seq', 'rows'))
- output_bias_grad: float32 [768], P(('seq', 'rows'))
- first_gain_grad: float32 [768], P(('seq', 'rows'))
- first_shift_grad: float32 [768], P(('seq', 'rows'))
- up_weight_grad: float32 [768, 3072], P(('seq', 'rows'))
- up_bias_grad: float32 [3072], P(('seq', 'rows'))
- down_weight_grad: float32 [3072, 768], P(('seq', 'rows'))
- down_bias_grad: float32 [768], P(('seq', 'rows'))
- second_gain_grad: float32 [768], P(('seq', 'rows'))
- second_shift_grad: float32 [768], P(('seq', 'rows'))
- position_bias_grad: float32 [12, 129], replicated
The draws below stay inside these ranges and needn't reach their ends.
All inputs are finite; a program needn't handle non-finite values.
Results may differ from the reference program's by a relative error of at most 0.029.
Values may be sent and summed in bfloat16 or wider, within the bound.
No kernel may reach another device: no remote copies, remote signals or barrier semaphores. Data moves between devices by JAX's collectives and lax.ppermute only.
A program may use at most 256 MiB of HBM per device.

```python
import math
import jax
import jax.numpy as jnp
from jax import lax

D = 768
H = 12
FF = 3072
DH = 64
M = 64
R = 128
S = 128
ROWS = 8
LEN = 1024


def draw_tokens(key, part):
    key = jax.random.fold_in(key, 11)
    key_cols, key_vals = jax.random.split(key)
    column_scale = jnp.exp(jax.random.uniform(key_cols, (D,), jnp.float32, math.log(0.3), math.log(3.0)))
    base = jax.random.truncated_normal(key_vals, -4.0, 4.0, (ROWS, LEN, D), jnp.float32)
    return (base * column_scale).astype(jnp.bfloat16)


def draw_position_bias(key, part):
    key = jax.random.fold_in(key, 23)
    key_near, key_far = jax.random.split(key)
    near_bias = jax.random.uniform(key_near, (H, R), jnp.float32, 0.5, 2.5)
    far_bias = jax.random.uniform(key_far, (H, 1), jnp.float32, -0.5, 0.5)
    return jnp.concatenate([near_bias, far_bias], axis=1)


def with_spikes(values, stream_key, source, target, shards_of, factor):
    owner, partner = [(jnp.arange(values.shape[dim]) // (values.shape[dim] // shards_of)).reshape([-1 if axis == dim else 1 for axis in range(values.ndim)]) for dim in (source, target)]
    chosen = jax.random.permutation(stream_key, shards_of)[partner]
    strong = (owner == chosen) | (owner == (partner + shards_of // 2) % shards_of)
    return jnp.where(strong, factor * values, values)


def steps_of(stream_key, dims, cuts, smallest, high):
    def one(position, shards_of):
        draws = jax.random.uniform(jax.random.fold_in(jax.random.fold_in(stream_key, 6), position), (shards_of,), jnp.float32, smallest / len(cuts), high / len(cuts))
        return jnp.repeat(jnp.exp(draws), dims[position] // shards_of).reshape((-1,) + (1,) * (len(dims) - position - 1))

    level = one(*cuts[0])
    for cut in cuts[1:]:
        level = level * one(*cut)
    return level


def noise(own_key, extent, scale, bound, cuts=(), kind=jnp.bfloat16):
    array = jax.random.normal(own_key, extent, jnp.float32) * scale
    if len(cuts) > 0:
        array = steps_of(own_key, extent, cuts, -0.22, 0.18) * array
    return jnp.clip(array, min=-bound, max=bound).astype(kind)


def gaussian_with(stream_key, dims, width, limit, cuts, heavy, kind=jnp.bfloat16):
    result = width * jax.random.normal(stream_key, dims, jnp.float32)
    if cuts:
        result = result * steps_of(stream_key, dims, cuts, -0.22, 0.18)
    return jnp.clip(with_spikes(result, jax.random.fold_in(stream_key, 3), *heavy), -limit, limit).astype(kind)


def setup_inputs(seed: int = 0) -> dict:
    seeds = jax.random.split(jax.random.key(seed), 21)
    return {
        "tokens": draw_tokens(jax.random.fold_in(seeds[20], 71), 0),
        "query_weight": noise(seeds[1], (D, D), D ** -0.5, 0.21875, ((0, 32),)),
        "query_bias": noise(seeds[2], (D,), 0.2, 1.0, ((0, 32),)),
        "key_weight": noise(seeds[3], (D, D), D ** -0.5, 0.21875, ((0, 32),)),
        "key_bias": noise(seeds[4], (D,), 0.2, 1.0, ((0, 32),)),
        "value_weight": noise(seeds[5], (D, D), D ** -0.5, 0.21875, ((0, 32),)),
        "value_bias": noise(seeds[6], (D,), 0.05, 0.25, ((0, 32),)),
        "output_weight": noise(seeds[7], (D, D), (D // 64) ** -0.5, 1.75, ((0, 32),)),
        "output_bias": noise(seeds[8], (D,), 0.2, 1.0, ((0, 32),)),
        "first_gain": jnp.clip(1.0 + 0.15 * jax.random.normal(seeds[9], (D,), jnp.float32), 0.25, 1.75).astype(jnp.bfloat16),
        "first_shift": noise(seeds[10], (D,), 0.3, 1.5, ((0, 32),)),
        "up_weight": noise(seeds[11], (D, FF), D ** -0.5, 0.21875, ((0, 32),)),
        "up_bias": noise(seeds[12], (FF,), 0.2, 1.0, ((0, 32),)),
        "down_weight": noise(seeds[13], (FF, D), FF ** -0.5, 0.109375, ((0, 32),)),
        "down_bias": noise(seeds[14], (D,), 0.2, 1.0, ((0, 32),)),
        "second_gain": jnp.clip(1.0 + 0.15 * jax.random.normal(seeds[15], (D,), jnp.float32), 0.25, 1.75).astype(jnp.bfloat16),
        "second_shift": noise(seeds[16], (D,), 0.3, 1.5, ((0, 32),)),
        "position_bias": draw_position_bias(jax.random.fold_in(seeds[20], 71), 0),
        "feature_matrix": noise(seeds[18], (H, DH, M), 1.0, 4.0, (), jnp.float32),
        "cotangent": gaussian_with(seeds[19], (ROWS, LEN, D), 1.0, 6.0, ((0, 4), (1, 8)), (1, 2, 8, 2.0)),
    }


epsilon = 1e-06

@jax.custom_vjp
def low(v):
    return lax.optimization_barrier(v.astype(jnp.bfloat16)).astype(jnp.float32)

@jax.custom_vjp
def low_back(v):
    return v

def low_keep(v):
    return (low(v), None)

def low_pass(kept, grad):
    return (grad,)

def back_keep(v):
    return (v, None)

def back_low(kept, grad):
    return (low(grad),)
low.defvjp(low_keep, low_pass)
low_back.defvjp(back_keep, back_low)

def hi_dot(left_arg, right_arg):
    return jnp.dot(left_arg, right_arg, precision=lax.Precision.HIGHEST, preferred_element_type=jnp.float32)

def layer_norm(values, gain_vec, offset):
    row_mean = lax.optimization_barrier(jnp.mean(values, axis=-1, keepdims=True))
    centred = values - row_mean
    spread = lax.optimization_barrier(jnp.mean(centred * centred, axis=-1, keepdims=True))
    return centred * lax.rsqrt(spread + epsilon) * gain_vec + offset

def gelu_exact(values):
    return 0.5 * values * (1.0 + lax.erf(values * 2.0 ** (-0.5)))

def feature_map(values, matrix):
    head_size = matrix.shape[1]
    feature_count = matrix.shape[2]
    scaled = values * head_size ** (-0.25)
    exponent = jnp.einsum('nhd,hdm->nhm', scaled, matrix, precision=lax.Precision.HIGHEST)
    exponent = exponent - 0.5 * lax.optimization_barrier(jnp.sum(scaled * scaled, axis=-1, keepdims=True))
    return jnp.exp(exponent) * feature_count ** (-0.5)

def window_weights(exp_bias):
    query_pos = jnp.arange(S, dtype=jnp.int32)[:, None]
    key_pos = jnp.arange(R + S, dtype=jnp.int32)[None, :]
    distance = query_pos + R - key_pos
    bucket = jnp.clip(distance, 0, R).astype(jnp.int32)
    near_part = jnp.where(distance[None] >= 0, exp_bias[:, bucket], 0.0)
    return near_part - jnp.where(key_pos[None] < R, exp_bias[:, R][:, None, None], 0.0)

def block_step(carried, pieces):
    running_state_sum, total_sum, weights, distant_weight = carried
    query_block_rows, key_block_rows, value_block_rows, halo_key, halo_value = pieces
    key_window = jnp.concatenate([halo_key, key_block_rows], axis=0)
    value_window = jnp.concatenate([halo_value, value_block_rows], axis=0)
    scores = low_back(jnp.einsum('shm,thm->hst', query_block_rows, key_window, precision=lax.Precision.HIGHEST))
    weighted = scores * weights
    numerator_sum = jnp.einsum('hst,thd->shd', low(weighted), value_window, precision=lax.Precision.HIGHEST)
    numerator_sum = numerator_sum + distant_weight[:, None] * jnp.einsum('lua,uap->lup', query_block_rows, running_state_sum, precision=lax.Precision.HIGHEST)
    denom = lax.optimization_barrier(jnp.sum(weighted, axis=-1)).T + distant_weight * jnp.einsum('shm,hm->sh', query_block_rows, total_sum, precision=lax.Precision.HIGHEST)
    attended_context = low(low_back(numerator_sum) / low_back(denom)[:, :, None])
    running_state_sum = running_state_sum + jnp.einsum('olp,olx->lpx', key_block_rows, value_block_rows, precision=lax.Precision.HIGHEST)
    total_sum = total_sum + lax.optimization_barrier(jnp.sum(key_block_rows, axis=0))
    return ((running_state_sum, total_sum, weights, distant_weight), attended_context)

def forward_row(params, row_tokens, feature_matrix):
    query_w, query_b, key_w, key_b, value_w, value_b, output_w, output_b, gain_first, offset_first, up_w, up_b, down_w, down_b, gain_second, offset_second, position_bias = params
    length = row_tokens.shape[0]
    blocks = length // S
    query_raw = low_back(hi_dot(row_tokens, query_w) + query_b)
    key_raw = low_back(hi_dot(row_tokens, key_w) + key_b)
    value_raw = low_back(hi_dot(row_tokens, value_w) + value_b)
    query_feat = low(feature_map(query_raw.reshape(length, H, DH), feature_matrix)).reshape(blocks, S, H, M)
    key_feat = low(feature_map(key_raw.reshape(length, H, DH), feature_matrix)).reshape(blocks, S, H, M)
    value_low = low(value_raw).reshape(blocks, S, H, DH)
    exp_bias = jnp.exp(position_bias)
    halo_keys = jnp.concatenate([jnp.zeros((1, R, H, M), jnp.float32), key_feat[:-1, S - R:]], axis=0)
    halo_values = jnp.concatenate([jnp.zeros((1, R, H, DH), jnp.float32), value_low[:-1, S - R:]], axis=0)
    start = (jnp.zeros((H, M, DH), jnp.float32), jnp.zeros((H, M), jnp.float32), window_weights(exp_bias), exp_bias[:, R])
    final_carry, contexts = lax.scan(jax.checkpoint(block_step), start, (query_feat, key_feat, value_low, halo_keys, halo_values))
    attended_context = contexts.reshape(length, H * DH)
    attn = low_back(hi_dot(attended_context, output_w) + output_b)
    hidden = layer_norm(row_tokens + attn, gain_first, offset_first)
    upper = low_back(hi_dot(low(hidden), up_w) + up_b)
    active = low(gelu_exact(upper))
    lower = low_back(hi_dot(active, down_w) + down_b)
    return layer_norm(hidden + lower, gain_second, offset_second)

def reference(tokens, query_weight, query_bias, key_weight, key_bias, value_weight, value_bias, output_weight, output_bias, first_gain, first_shift, up_weight, up_bias, down_weight, down_bias, second_gain, second_shift, position_bias, feature_matrix, cotangent):
    params = tuple((argument.astype(jnp.float32) for argument in (query_weight, query_bias, key_weight, key_bias, value_weight, value_bias, output_weight, output_bias, first_gain, first_shift, up_weight, up_bias, down_weight, down_bias, second_gain, second_shift, position_bias)))
    matrix = feature_matrix.astype(jnp.float32)

    def per_row(grad_sums, pieces):
        row_tokens, row_grad = pieces
        outputs, pullback = jax.vjp(lambda weights, inputs: forward_row(weights, inputs, matrix), params, row_tokens)
        weight_grads, token_grad = pullback(row_grad)
        return (jax.tree.map(jnp.add, grad_sums, weight_grads), (outputs, token_grad))
    zero_sums = jax.tree.map(jnp.zeros_like, params)
    grad_sums, (layer_output, token_grads) = lax.scan(per_row, zero_sums, (tokens.astype(jnp.float32), cotangent.astype(jnp.float32)))
    return (layer_output, token_grads, grad_sums[0], grad_sums[1], grad_sums[2], grad_sums[3], grad_sums[4], grad_sums[5], grad_sums[6], grad_sums[7], grad_sums[8], grad_sums[9], grad_sums[10], grad_sums[11], grad_sums[12], grad_sums[13], grad_sums[14], grad_sums[15], grad_sums[16])
```

```python
import jax
import jax.numpy as jnp
from jax import lax
from jax.sharding import PartitionSpec as P

BOTH = ("seq", "rows")
EPS = 1e-06
BF = jnp.bfloat16
F32 = jnp.float32


class Place:
    def __init__(self):
        self.seq = lax.axis_size("seq")
        self.rows = lax.axis_size("rows")
        self.n = self.seq * self.rows
        self.fast = self.seq == 8 and self.rows == 4
        me = lax.axis_index(BOTH)
        self.c = me % 2
        self.y = (me // 2) % 2
        self.x = (me // 4) % 2
        self.z = me // 8
        self.s = lax.axis_index("seq")

    def flip(self, a, stride):
        return lax.ppermute(a, BOTH, [(d, d ^ stride) for d in range(self.n)])

    def swap_c(self, a):
        return self.flip(a, 1)

    def swap_y(self, a):
        return self.flip(a, 2)

    def swap_x(self, a):
        return self.flip(a, 4)

    def turn_z(self, a, by):
        return lax.ppermute(a, BOTH, [(d, (d + 8 * by) % self.n) for d in range(self.n)])

    def along(self, a, by):
        pairs = [(i, i + by) for i in range(self.seq) if 0 <= i + by < self.seq]
        return lax.ppermute(a, "seq", pairs)


def ordered(first, mine, other, axis):
    return jnp.where(
        first, jnp.stack([mine, other], axis=axis), jnp.stack([other, mine], axis=axis)
    )


def gather_halves(at, left, right):
    r, half = left.shape
    if not at.fast:
        return (
            lax.all_gather(left, BOTH, axis=0, tiled=True),
            lax.all_gather(right, BOTH, axis=0, tiled=True),
        )
    c0 = at.c == 0
    got = at.swap_c(jnp.where(c0, right, left))
    piece = ordered(c0, jnp.where(c0, left, right), got, 0).reshape(2 * r, half)
    turned = [at.turn_z(piece, by) for by in (1, 2, 3)]
    rel = jnp.stack([piece, turned[2], turned[1], turned[0]])
    by_z = lax.dynamic_slice_in_dim(jnp.concatenate([rel, rel]), (4 - at.z) % 4, 4)
    low, high = by_z[:2], by_z[2:]
    low_x = ordered(at.x == 0, low, at.swap_x(low), 1)
    high_y = ordered(at.y == 0, high, at.swap_y(high), 1)
    low_xy = ordered(at.y == 0, low_x, at.swap_y(low_x), 2)
    high_xy = ordered(at.x == 0, high_y, at.swap_x(high_y), 1)
    mine = jnp.concatenate([low_xy, high_xy]).reshape(at.n * r, half)
    other = at.swap_c(mine)
    return jnp.where(c0, mine, other), jnp.where(c0, other, mine)


def half_at(a, index, axis):
    return lax.dynamic_index_in_dim(a, index, axis, keepdims=False)


def plus(kept, got):
    return (kept.astype(F32) + got.astype(F32)).astype(BF)


def scatter_halves(at, left, right):
    total, half = left.shape
    r = total // at.n
    if not at.fast:
        return (
            lax.psum_scatter(left, BOTH, scatter_dimension=0, tiled=True),
            lax.psum_scatter(right, BOTH, scatter_dimension=0, tiled=True),
        )
    c0 = at.c == 0
    got = at.swap_c(jnp.where(c0, right, left).astype(BF))
    mine = plus(jnp.where(c0, left, right), got).reshape(4, 2, 2, 2 * r, half)
    low, high = mine[:2], mine[2:]
    low = plus(half_at(low, at.y, 2), at.swap_y(half_at(low, 1 - at.y, 2)))
    high = plus(half_at(high, at.x, 1), at.swap_x(half_at(high, 1 - at.x, 1)))
    low = plus(half_at(low, at.x, 1), at.swap_x(half_at(low, 1 - at.x, 1)))
    high = plus(half_at(high, at.y, 1), at.swap_y(half_at(high, 1 - at.y, 1)))
    by_z = jnp.concatenate([low, high])
    got = [at.turn_z(half_at(by_z, (at.z + by) % 4, 0), by).astype(F32) for by in (1, 2, 3)]
    piece = (half_at(by_z, at.z, 0).astype(F32) + got[0] + got[1] + got[2]).reshape(2, r, half)
    keep = half_at(piece, at.c, 0)
    got = at.swap_c(half_at(piece, 1 - at.c, 0))
    return jnp.where(c0, keep, got), jnp.where(c0, got, keep)


def sum_before(at, a, reverse):
    if not at.fast:
        everything = lax.all_gather(a, "seq").astype(F32)
        index = jnp.arange(at.seq).reshape((-1,) + (1,) * a.ndim)
        reached = index > at.s if reverse else index < at.s
        return jnp.sum(jnp.where(reached, everything, 0.0), axis=0)
    beside = at.swap_x(a).astype(F32)
    pair = plus(a, beside)
    before = jnp.where((at.x == 0) if reverse else (at.x == 1), beside, 0.0)
    for by in (1, 2, 3):
        if reverse:
            got = lax.ppermute(pair, BOTH, [(d, d - 8 * by) for d in range(8 * by, at.n)])
        else:
            got = lax.ppermute(pair, BOTH, [(d, d + 8 * by) for d in range(at.n - 8 * by)])
        before = before + got.astype(F32)
    return before


def sum_everywhere(at, a):
    if not at.fast:
        return lax.psum(a, BOTH)
    a = a + at.swap_c(a)
    a = a + at.swap_y(a)
    a = a + at.swap_x(a)
    a = a + at.flip(a, 8)
    return a + at.flip(a, 16)


def layer_norm(values, gain_vec, offset):
    row_mean = jnp.mean(values, axis=-1, keepdims=True)
    centred = values - row_mean
    spread = jnp.mean(centred * centred, axis=-1, keepdims=True)
    return centred * lax.rsqrt(spread + EPS) * gain_vec + offset


def gelu_exact(values):
    return 0.5 * values * (1.0 + lax.erf(values * 2.0 ** (-0.5)))


def feature_map(values, matrix):
    head_size = matrix.shape[1]
    scaled = values * head_size ** (-0.25)
    exponent = jnp.einsum("nhd,hdm->nhm", scaled, matrix, precision=lax.Precision.HIGHEST)
    exponent = exponent - 0.5 * jnp.sum(scaled * scaled, axis=-1, keepdims=True)
    return jnp.exp(exponent) * matrix.shape[2] ** (-0.5)


def window_table(exp_bias, window, block_len):
    head_count = exp_bias.shape[0]
    key_span = window + block_len
    period = key_span + block_len
    far_column = exp_bias[:, window : window + 1]
    periodic = jnp.concatenate(
        [
            exp_bias[:, ::-1],
            jnp.zeros((head_count, block_len - 1), F32),
            jnp.broadcast_to(far_column, (head_count, block_len)),
        ],
        axis=1,
    )
    tiled_rows = jnp.tile(periodic, (1, block_len))
    table = tiled_rows[:, : block_len * (period - 1)].reshape(head_count, block_len, period - 1)[
        :, :, :key_span
    ]
    column = lax.broadcasted_iota(jnp.int32, (1, 1, key_span), 2)
    return table - jnp.where(column < window, far_column[:, :, None], 0.0)


def bucket_sums(pieces, window, block_len):
    head_count = pieces.shape[0]
    key_span = window + block_len
    period = key_span + block_len
    padded = jnp.pad(pieces, ((0, 0), (0, 0), (0, period - 1 - key_span)))
    flat_rows = padded.reshape(head_count, block_len * (period - 1))
    flat_rows = jnp.pad(flat_rows, ((0, 0), (0, block_len)))
    return jnp.sum(flat_rows.reshape(head_count, block_len, period), axis=1)


def tdot(a, b):
    return lax.dot_general(a, b, (((0,), (0,)), ((), ())), preferred_element_type=F32)


def dot_t(a, b):
    return lax.dot_general(a, b, (((1,), (1,)), ((), ())), preferred_element_type=F32)


def dot(a, b):
    return jnp.dot(a, b, preferred_element_type=F32)


def ein(spec, a, b):
    return jnp.einsum(spec, a, b, preferred_element_type=F32)


def on_device(
    tokens,
    query_weight,
    query_bias,
    key_weight,
    key_bias,
    value_weight,
    value_bias,
    output_weight,
    output_bias,
    first_gain,
    first_shift,
    up_weight,
    up_bias,
    down_weight,
    down_bias,
    second_gain,
    second_shift,
    position_bias,
    feature_matrix,
    cotangent,
):
    at = Place()
    rows, block, width = tokens.shape
    heads, size, feats = feature_matrix.shape
    window = position_bias.shape[1] - 1
    n = rows * block
    hw = width // 2
    ff = up_weight.shape[1]
    hf = ff // 2
    own = query_weight.shape[0]
    up_own = up_bias.shape[0] // own
    tok = tokens.reshape(n, width)

    vectors = (
        query_bias, key_bias, value_bias, output_bias, first_gain, first_shift,
        down_bias, second_gain, second_shift,
    )
    small = jnp.concatenate([v[:, None] for v in vectors] + [up_bias.reshape(own, up_own)], axis=1)
    small = jnp.pad(small, ((0, 0), (0, 128 - small.shape[1])))
    g1_left, g1_right = gather_halves(
        at,
        jnp.concatenate([query_weight[:, :hw], key_weight[:, :hw], value_weight[:, :hw], small], axis=1),
        jnp.concatenate([query_weight[:, hw:], key_weight[:, hw:], value_weight[:, hw:], small], axis=1),
    )
    wq = jnp.concatenate([g1_left[:, :hw], g1_right[:, :hw]], axis=1)
    wk = jnp.concatenate([g1_left[:, hw : 2 * hw], g1_right[:, hw : 2 * hw]], axis=1)
    wv = jnp.concatenate([g1_left[:, 2 * hw : 3 * hw], g1_right[:, 2 * hw : 3 * hw]], axis=1)
    small = g1_left[:, 3 * hw :]
    vecs = small[:, : len(vectors)].T.astype(F32)
    b_q, b_k, b_v, b_o, gain1, shift1, b_d, gain2, shift2 = [vecs[i] for i in range(len(vectors))]
    b_u = small[:, len(vectors) : len(vectors) + up_own].reshape(ff).astype(F32)
    g2_left, g2_right = gather_halves(
        at,
        jnp.concatenate([output_weight[:, :hw], up_weight[:, :hf]], axis=1),
        jnp.concatenate([output_weight[:, hw:], up_weight[:, hf:]], axis=1),
    )
    wo = jnp.concatenate([g2_left[:, :hw], g2_right[:, :hw]], axis=1)
    wu = jnp.concatenate([g2_left[:, hw:], g2_right[:, hw:]], axis=1)
    wd = jnp.concatenate(gather_halves(at, down_weight[:, :hw], down_weight[:, hw:]), axis=1)

    exp_bias = jnp.exp(position_bias)
    far = exp_bias[:, window]
    table = window_table(exp_bias, window, block)

    halo_tok = at.along(tok, 1)
    inner = at.s > 0

    def split(a, h=heads):
        return a.reshape(rows, block, h, a.shape[-1] // h)

    def phi(values):
        return feature_map(values.reshape(n, heads, size), feature_matrix)

    q_raw = dot(tok, wq) + b_q
    k_raw = dot(tok, wk) + b_k
    q_phi, q_back = jax.vjp(phi, q_raw)
    k_phi, k_back = jax.vjp(phi, k_raw)
    q_feat = split(q_phi.astype(BF).reshape(n, width))
    k_feat = split(k_phi.astype(BF).reshape(n, width))
    v_low = split((dot(tok, wv) + b_v).astype(BF))
    state = ein("rshm,rshd->rmhd", k_feat, v_low).reshape(rows, feats, width)
    total = jnp.sum(k_feat.astype(F32), axis=1).reshape(rows, 1, width)
    packed = jnp.concatenate([state, jnp.pad(total, ((0, 0), (0, 7), (0, 0)))], axis=1)
    before = sum_before(at, packed.astype(BF), False)
    q_next = at.along(q_feat.reshape(n, width), -1)
    halo_k = jnp.where(inner, split(phi(dot(halo_tok, wk) + b_k).astype(BF).reshape(n, width)), 0)
    halo_v = jnp.where(inner, split((dot(halo_tok, wv) + b_v).astype(BF)), 0)
    k_win = jnp.concatenate([halo_k, k_feat], axis=1)
    v_win = jnp.concatenate([halo_v, v_low], axis=1)
    state = before[:, :feats].reshape(rows, feats, heads, size).astype(BF)
    total = before[:, feats].reshape(rows, heads, feats).astype(BF)

    scores = ein("rshm,rthm->rhst", q_feat, k_win)
    weighted = scores * table
    w_low = weighted.astype(BF)
    state_num = ein("rshm,rmhd->rshd", q_feat, state)
    state_den = ein("rshm,rhm->rsh", q_feat, total)
    numer = ein("rhst,rthd->rshd", w_low, v_win) + far[:, None] * state_num
    denom = jnp.transpose(jnp.sum(weighted, axis=-1), (0, 2, 1)) + far * state_den
    ratio = numer / denom[..., None]
    context = ratio.astype(BF).reshape(n, width)

    resid = tok.astype(F32) + dot(context, wo) + b_o
    hidden, first_back = jax.vjp(layer_norm, resid, gain1, shift1)
    h_low = hidden.astype(BF)
    active, gelu_back = jax.vjp(gelu_exact, dot(h_low, wu) + b_u)
    a_low = active.astype(BF)
    out, second_back = jax.vjp(layer_norm, hidden + dot(a_low, wd) + b_d, gain2, shift2)
    d_lower, d_gain2, d_shift2 = second_back(cotangent.reshape(n, width).astype(F32))
    d_low = d_lower.astype(BF)
    g_wd = [tdot(a_low, d_low[:, :hw]), tdot(a_low, d_low[:, hw:])]
    s_wd = scatter_halves(at, *g_wd)
    d_upper = gelu_back(dot_t(d_low, wd))[0].astype(BF)
    g_wu = [tdot(h_low, d_upper[:, :hf]), tdot(h_low, d_upper[:, hf:])]
    d_resid, d_gain1, d_shift1 = first_back(d_lower + dot_t(d_upper, wu))
    d_attn = d_resid.astype(BF)
    g_wo = [tdot(context, d_attn[:, :hw]), tdot(context, d_attn[:, hw:])]
    s_uo = scatter_halves(
        at,
        jnp.concatenate([g_wo[0], g_wu[0]], axis=1),
        jnp.concatenate([g_wo[1], g_wu[1]], axis=1),
    )
    d_context = split(dot_t(d_attn, wo))
    d_numer = (d_context / denom[..., None]).astype(BF)
    d_denom = (-jnp.sum(d_context * ratio, axis=-1) / denom).astype(BF)

    later = far[:, None] * ein("rshm,rshd->rmhd", q_feat, d_numer)
    later_tot = far[:, None] * ein("rshm,rsh->rhm", q_feat, d_denom)
    packed = jnp.concatenate(
        [
            later.reshape(rows, feats, width),
            jnp.pad(later_tot.reshape(rows, 1, width), ((0, 0), (0, 7), (0, 0))),
        ],
        axis=1,
    )
    after = sum_before(at, packed.astype(BF), True)
    dn_next = split(at.along(d_numer.reshape(n, width), -1))
    dd_next = at.along(d_denom, -1)
    d_weighted = ein("rshd,rthd->rhst", d_numer, v_win)
    d_weighted = d_weighted + jnp.transpose(d_denom.astype(F32), (0, 2, 1))[..., None]
    pieces = jnp.sum(d_weighted * scores, axis=0)
    d_scores = (d_weighted * table).astype(BF)
    d_qfeat = ein("rhst,rthm->rshm", d_scores, k_win) + far[:, None] * (
        ein("rshd,rmhd->rshm", d_numer, state) + d_denom.astype(F32)[..., None] * total.astype(F32)[:, None]
    )
    d_query = q_back(d_qfeat.reshape(n, heads, feats))[0].reshape(n, width).astype(BF)
    bucketed = bucket_sums(pieces, window, block)
    near_grad = bucketed[:, window:0:-1]
    far_grad = (
        bucketed[:, 0]
        + jnp.sum(bucketed[:, window + block :], axis=1)
        - jnp.sum(pieces[:, :, :window], axis=(1, 2))
        + jnp.sum(d_numer.astype(F32) * state_num, axis=(0, 1, 3))
        + jnp.sum(d_denom.astype(F32) * state_den, axis=(0, 1))
    )
    position_grad = sum_everywhere(
        at,
        jnp.concatenate(
            [exp_bias[:, :window] * near_grad, (exp_bias[:, window] * far_grad)[:, None]], axis=1
        ),
    )

    qn = split(q_next)
    t_next = table[:, :, :window]
    w_next = (ein("rshm,rthm->rhst", qn, k_feat) * t_next).astype(BF)
    dw_next = ein("rshd,rthd->rhst", dn_next, v_low)
    dw_next = dw_next + jnp.transpose(dd_next.astype(F32), (0, 2, 1))[..., None]
    ds_next = (dw_next * t_next).astype(BF)
    later = after[:, :feats].reshape(rows, feats, heads, size).astype(BF)
    later_tot = after[:, feats].reshape(rows, heads, feats)
    d_kfeat = (
        ein("rhst,rshm->rthm", d_scores[..., window:], q_feat)
        + ein("rhst,rshm->rthm", ds_next, qn)
        + ein("rmhd,rshd->rshm", later, v_low)
        + later_tot[:, None]
    )
    d_value = (
        ein("rhst,rshd->rthd", w_low[..., window:], d_numer)
        + ein("rhst,rshd->rthd", w_next, dn_next)
        + ein("rmhd,rshm->rshd", later, k_feat)
    )
    d_key = k_back(d_kfeat.reshape(n, heads, feats))[0].reshape(n, width).astype(BF)
    d_value = d_value.reshape(n, width).astype(BF)
    d_tokens = d_resid + dot_t(d_query, wq) + dot_t(d_key, wk) + dot_t(d_value, wv)

    def cols(a):
        return jnp.sum(a.astype(F32), axis=0)

    g_small = jnp.stack(
        [cols(d_query), cols(d_key), cols(d_value), cols(d_attn), d_gain1, d_shift1, cols(d_low), d_gain2, d_shift2]
    ).T
    g_small = jnp.concatenate([g_small, cols(d_upper).reshape(width, up_own)], axis=1)
    g_small = jnp.pad(g_small, ((0, 0), (0, 128 - g_small.shape[1])))
    s_qkv = scatter_halves(
        at,
        *[
            jnp.concatenate(
                [tdot(tok, d_query[:, h]), tdot(tok, d_key[:, h]), tdot(tok, d_value[:, h]), g_small], axis=1
            )
            for h in (slice(0, hw), slice(hw, width))
        ],
    )

    def both(pair, start, size):
        return jnp.concatenate([pair[0][:, start : start + size], pair[1][:, start : start + size]], axis=1)

    s_small = s_qkv[0][:, 3 * hw :]
    sq, sk, sv, so, sg1, ss1, sd, sg2, ss2 = [s_small[:, i] for i in range(len(vectors))]
    su = s_small[:, len(vectors) : len(vectors) + up_own].reshape(-1)
    return (
        out.reshape(rows, block, width),
        d_tokens.reshape(rows, block, width),
        both(s_qkv, 0, hw),
        sq,
        both(s_qkv, hw, hw),
        sk,
        both(s_qkv, 2 * hw, hw),
        sv,
        both(s_uo, 0, hw),
        so,
        sg1,
        ss1,
        both(s_uo, hw, hf),
        su,
        both(s_wd, 0, hw),
        sd,
        sg2,
        ss2,
        position_grad,
    )


def solution(mesh):
    matrix, vector, split = P(BOTH, None), P(BOTH), P("rows", "seq", None)
    return jax.shard_map(
        on_device,
        mesh=mesh,
        in_specs=(split,)
        + (matrix, vector) * 4
        + (vector, vector)
        + (matrix, vector) * 2
        + (vector, vector)
        + (P(), P(), split),
        out_specs=(split, split)
        + (matrix, vector) * 4
        + (vector, vector)
        + (matrix, vector) * 2
        + (vector, vector)
        + (P(),),
        check_vma=False,
    )
```

```python
import math

import jax
import jax.numpy as jnp
from jax import lax
from jax.experimental import pallas as pl
from jax.experimental.pallas import tpu as pltpu
from jax.sharding import PartitionSpec as P

BOTH = ("seq", "rows")
EPS = 1e-06
BF = jnp.bfloat16
F32 = jnp.float32


class Place:
    def __init__(self):
        self.seq = lax.axis_size("seq")
        self.rows = lax.axis_size("rows")
        self.n = self.seq * self.rows
        self.fast = self.seq == 8 and self.rows == 4
        me = lax.axis_index(BOTH)
        self.c = me % 2
        self.y = (me // 2) % 2
        self.x = (me // 4) % 2
        self.z = me // 8
        self.s = lax.axis_index("seq")

    def flip(self, a, stride):
        return lax.ppermute(a, BOTH, [(d, d ^ stride) for d in range(self.n)])

    def swap_c(self, a):
        return self.flip(a, 1)

    def swap_y(self, a):
        return self.flip(a, 2)

    def swap_x(self, a):
        return self.flip(a, 4)

    def turn_z(self, a, by):
        return lax.ppermute(a, BOTH, [(d, (d + 8 * by) % self.n) for d in range(self.n)])

    def along(self, a, by):
        pairs = [(i, i + by) for i in range(self.seq) if 0 <= i + by < self.seq]
        return lax.ppermute(a, "seq", pairs)


def ordered(first, mine, other, axis):
    return jnp.where(
        first, jnp.stack([mine, other], axis=axis), jnp.stack([other, mine], axis=axis)
    )


def gather_halves(at, left, right):
    r, half = left.shape
    c0 = at.c == 0
    if not at.fast:
        left = lax.all_gather(left, BOTH, axis=0, tiled=True)
        right = lax.all_gather(right, BOTH, axis=0, tiled=True)
        return jnp.where(c0, left, right), jnp.where(c0, right, left)
    got = at.swap_c(jnp.where(c0, right, left))
    piece = ordered(c0, jnp.where(c0, left, right), got, 0).reshape(2 * r, half)
    turned = [at.turn_z(piece, by) for by in (1, 2, 3)]
    rel = jnp.stack([piece, turned[2], turned[1], turned[0]])
    by_z = lax.dynamic_slice_in_dim(jnp.concatenate([rel, rel]), (4 - at.z) % 4, 4)
    low, high = by_z[:2], by_z[2:]
    low_x = ordered(at.x == 0, low, at.swap_x(low), 1)
    high_y = ordered(at.y == 0, high, at.swap_y(high), 1)
    low_xy = ordered(at.y == 0, low_x, at.swap_y(low_x), 2)
    high_xy = ordered(at.x == 0, high_y, at.swap_x(high_y), 1)
    mine = jnp.concatenate([low_xy, high_xy]).reshape(at.n * r, half)
    return mine, at.swap_c(mine)


def half_at(a, index, axis):
    return lax.dynamic_index_in_dim(a, index, axis, keepdims=False)


def plus(kept, got):
    return (kept.astype(F32) + got.astype(F32)).astype(BF)


def scatter_halves(at, keep, send):
    total, half = keep.shape
    r = total // at.n
    c0 = at.c == 0
    if not at.fast:
        left, right = jnp.where(c0, keep, send).astype(F32), jnp.where(c0, send, keep).astype(F32)
        return (
            lax.psum_scatter(left, BOTH, scatter_dimension=0, tiled=True),
            lax.psum_scatter(right, BOTH, scatter_dimension=0, tiled=True),
        )
    mine = plus(keep, at.swap_c(send)).reshape(4, 2, 2, 2 * r, half)
    low, high = mine[:2], mine[2:]
    low = plus(half_at(low, at.y, 2), at.swap_y(half_at(low, 1 - at.y, 2)))
    high = plus(half_at(high, at.x, 1), at.swap_x(half_at(high, 1 - at.x, 1)))
    low = plus(half_at(low, at.x, 1), at.swap_x(half_at(low, 1 - at.x, 1)))
    high = plus(half_at(high, at.y, 1), at.swap_y(half_at(high, 1 - at.y, 1)))
    by_z = jnp.concatenate([low, high])
    got = [at.turn_z(half_at(by_z, (at.z + by) % 4, 0), by).astype(F32) for by in (1, 2, 3)]
    piece = (half_at(by_z, at.z, 0).astype(F32) + got[0] + got[1] + got[2]).reshape(2, r, half)
    stays = half_at(piece, at.c, 0)
    got = at.swap_c(half_at(piece, 1 - at.c, 0))
    return jnp.where(c0, stays, got), jnp.where(c0, got, stays)


def sum_before(at, a, reverse):
    if not at.fast:
        everything = lax.all_gather(a, "seq").astype(F32)
        index = jnp.arange(at.seq).reshape((-1,) + (1,) * a.ndim)
        reached = index > at.s if reverse else index < at.s
        return jnp.sum(jnp.where(reached, everything, 0.0), axis=0)
    beside = at.swap_x(a).astype(F32)
    pair = plus(a, beside)
    before = jnp.where((at.x == 0) if reverse else (at.x == 1), beside, 0.0)
    for by in (1, 2, 3):
        if reverse:
            got = lax.ppermute(pair, BOTH, [(d, d - 8 * by) for d in range(8 * by, at.n)])
        else:
            got = lax.ppermute(pair, BOTH, [(d, d + 8 * by) for d in range(at.n - 8 * by)])
        before = before + got.astype(F32)
    return before


def sum_everywhere(at, a):
    if not at.fast:
        return lax.psum(a, BOTH)
    a = a + at.swap_c(a)
    a = a + at.swap_y(a)
    a = a + at.swap_x(a)
    a = a + at.flip(a, 8)
    return a + at.flip(a, 16)


VMEM = pltpu.VMEM
SCALAR = pl.BlockSpec(memory_space=pltpu.SMEM)
WHOLE = pl.BlockSpec(memory_space=VMEM)


def params(mib):
    return pltpu.CompilerParams(vmem_limit_bytes=mib * 2**20)


def cost(flops, moved):
    return pl.CostEstimate(flops=int(flops), bytes_accessed=int(moved), transcendentals=0)


def tdot(a, b):
    return lax.dot_general(a, b, (((0,), (0,)), ((), ())), preferred_element_type=F32)


def dot_t(a, b):
    return lax.dot_general(a, b, (((1,), (1,)), ((), ())), preferred_element_type=F32)


def dot(a, b):
    return jnp.dot(a, b, preferred_element_type=F32)


def parts(a):
    high = a.astype(BF)
    return high, (a - high.astype(F32)).astype(BF)


def left_lanes(shape):
    return lax.broadcasted_iota(jnp.int32, shape, len(shape) - 1) % 128 < 64


def two_heads(a):
    first = left_lanes(a.shape)
    wide = a.astype(F32)
    return jnp.concatenate(
        [jnp.where(first, wide, 0.0), jnp.where(first, 0.0, wide)], axis=0
    ).astype(BF)


def fold(a):
    half = a.shape[0] // 2
    return jnp.where(left_lanes((half, a.shape[1])), a[:half], a[half:])


def head_ones():
    row = lax.broadcasted_iota(jnp.int32, (128, 128), 0) // 64
    col = lax.broadcasted_iota(jnp.int32, (128, 128), 1) // 64
    return jnp.where(row == col, 1.0, 0.0).astype(BF)


def head_sums(a, ones):
    high, low = parts(a)
    return dot(high, ones) + dot(low, ones)


def features(s, g_high, g_low):
    high, low = parts(jnp.concatenate([s, s * s], axis=1))
    return jnp.exp(dot(high, g_high) + dot(high, g_low) + dot(low, g_high)) * 0.125


def features_back(t, s, g_high, g_low, ones, scale):
    high, low = parts(t)
    f_high, f_low = g_high[:128], g_low[:128]
    back = dot_t(high, f_high) + dot_t(high, f_low) + dot_t(low, f_high)
    return ((back - s * (dot(high, ones) + dot(low, ones))) * scale).astype(BF)


def lanes(p):
    return slice(p * 128, (p + 1) * 128)


def key_kernel(c_ref, tok, mine, other, gh, gl, s_out, phi_out, feat_out, v_out, state_out, vec_out):
    first = c_ref[0] == 0
    pairs, block = gh.shape[0], 128
    hw = pairs * 64
    eye = jnp.where(
        lax.broadcasted_iota(jnp.int32, (128, 128), 0) == lax.broadcasted_iota(jnp.int32, (128, 128), 1), 1.0, 0.0
    ).astype(BF)
    vecs = dot_t(eye, mine[:, 3 * hw :])[:16]
    vec_out[...] = vecs
    a = dot(tok[...], mine[:, hw : 3 * hw])
    b = dot(tok[...], other[:, hw : 3 * hw])
    left, right = jnp.where(first, a, b), jnp.where(first, b, a)
    scale = 64 ** (-0.25)
    for p in range(pairs):
        half, at = (left, p * 128) if p < pairs // 2 else (right, p * 128 - hw)
        s = (half[:, at : at + 128] + vecs[1:2, lanes(p)]) * scale
        v = (half[:, hw + at : hw + at + 128] + vecs[2:3, lanes(p)]).astype(BF)
        phi = features(s, gh[p], gl[p])
        k = phi.astype(BF)
        s_out[:, lanes(p)] = s
        phi_out[:, lanes(p)] = phi
        feat_out[:, lanes(p)] = k
        v_out[:, lanes(p)] = v
        for r in range(tok.shape[0] // block):
            rows = slice(r * block, (r + 1) * block)
            state_out[r, :64, lanes(p)] = fold(tdot(k[rows], v[rows])).astype(BF)
            total = jnp.sum(k[rows].astype(F32), axis=0, keepdims=True)
            state_out[r, 64:, lanes(p)] = jnp.broadcast_to(total, (16, 128)).astype(BF)


def query_kernel(c_ref, tok, halo, mine, other, vec, gh, gl, s_out, phi_out, feat_out, hk_out, hv_out):
    first, inner = c_ref[0] == 0, c_ref[1] > 0
    pairs = gh.shape[0]
    hw = pairs * 64
    scale = 64 ** (-0.25)
    a, b = dot(tok[...], mine[:, :hw]), dot(tok[...], other[:, :hw])
    left, right = jnp.where(first, a, b), jnp.where(first, b, a)
    for p in range(pairs):
        half, at = (left, p * 128) if p < pairs // 2 else (right, p * 128 - hw)
        s = (half[:, at : at + 128] + vec[0:1, lanes(p)]) * scale
        phi = features(s, gh[p], gl[p])
        s_out[:, lanes(p)] = s
        phi_out[:, lanes(p)] = phi
        feat_out[:, lanes(p)] = phi.astype(BF)
    a, b = dot(halo[...], mine[:, hw : 3 * hw]), dot(halo[...], other[:, hw : 3 * hw])
    left, right = jnp.where(first, a, b), jnp.where(first, b, a)
    for p in range(pairs):
        half, at = (left, p * 128) if p < pairs // 2 else (right, p * 128 - hw)
        s = (half[:, at : at + 128] + vec[1:2, lanes(p)]) * scale
        v = half[:, hw + at : hw + at + 128] + vec[2:3, lanes(p)]
        hk_out[:, lanes(p)] = jnp.where(inner, features(s, gh[p], gl[p]), 0.0).astype(BF)
        hv_out[:, lanes(p)] = jnp.where(inner, v, 0.0).astype(BF)


def block_diagonal(packed):
    return two_heads(packed)


def attention_kernel(q, k, v, hk, hv, table, state, far, context_out, ratio_out, denom_out):
    ones = head_ones()
    wmat = table[...].reshape(256, 256)
    far_row = far[0:1]
    for r in range(q.shape[0] // 128):
        rows = slice(r * 128, (r + 1) * 128)
        qr = q[rows]
        kw = jnp.concatenate([hk[rows], k[rows]], axis=0)
        vw = jnp.concatenate([hv[rows], v[rows]], axis=0)
        weighted = dot_t(two_heads(qr), kw) * wmat
        numer = fold(dot(weighted.astype(BF), vw))
        near = jnp.sum(weighted, axis=1, keepdims=True)
        near = fold(jnp.broadcast_to(near, (256, 128)))
        bd = block_diagonal(state[r, :64])
        total = state[r, 64:80].astype(F32)[0:1]
        numer = numer + far_row * dot(qr, bd)
        denom = near + far_row * head_sums(qr.astype(F32) * total, ones)
        ratio = numer / denom
        context_out[rows] = ratio.astype(BF)
        ratio_out[rows] = ratio
        denom_out[rows] = denom


def normed(x):
    centred = x - jnp.mean(x, axis=-1, keepdims=True)
    rstd = lax.rsqrt(jnp.mean(centred * centred, axis=-1, keepdims=True) + EPS)
    return centred * rstd, rstd


def norm_back(dy, xhat, rstd, gain):
    d = dy * gain
    return rstd * (
        d - jnp.mean(d, axis=-1, keepdims=True) - xhat * jnp.mean(d * xhat, axis=-1, keepdims=True)
    )


def col_sums(a):
    return jnp.sum(a, axis=0, keepdims=True)


def forward_kernel(
    c_ref, context, tok, m2, o2, m3, o3, cot, vec, bu,
    out, dlower_out, dlow_out, hlow_out, xhat_out, rstd_out, gp_out, keep_out, send_out, sums_out,
):
    c = c_ref[0]
    first = c == 0
    hw = m3.shape[1]
    hf = bu.shape[1] // 2
    a, b = dot(context[...], m2[:, :hw]), dot(context[...], o2[:, :hw])
    attn = jnp.concatenate([jnp.where(first, a, b), jnp.where(first, b, a)], axis=1)
    xhat, rstd = normed(tok[...].astype(F32) + attn + vec[3:4])
    hidden = xhat * vec[4:5] + vec[5:6]
    xhat_out[...] = xhat
    rstd_out[...] = jnp.broadcast_to(rstd, rstd_out.shape)
    h_low = hidden.astype(BF)
    hlow_out[...] = h_low
    my_rows, its_rows = pl.ds(pl.multiple_of(c * hf, hf), hf), pl.ds(pl.multiple_of((1 - c) * hf, hf), hf)
    actives = []
    for w, at, flip in ((m2, 0, False), (o2, 1, True)):
        b_left, b_right = (bu[:, hf:], bu[:, :hf]) if flip else (bu[:, :hf], bu[:, hf:])
        bias = jnp.where(first, b_left, b_right)
        upper = dot(h_low, w[:, hw:]) + bias
        cdf = 0.5 * (1.0 + lax.erf(upper * 2.0 ** (-0.5)))
        pdf = jnp.exp(-0.5 * upper * upper) * (2.0 * math.pi) ** (-0.5)
        gp_out[at] = (cdf + upper * pdf).astype(BF)
        actives.append((upper * cdf).astype(BF))
    a = dot(actives[0], m3[my_rows]) + dot(actives[1], m3[its_rows])
    b = dot(actives[0], o3[my_rows]) + dot(actives[1], o3[its_rows])
    lower = jnp.concatenate([jnp.where(first, a, b), jnp.where(first, b, a)], axis=1)
    xhat2, rstd2 = normed(hidden + lower + vec[6:7])
    gain2 = vec[7:8]
    out[...] = xhat2 * gain2 + vec[8:9]
    dy = cot[...].astype(F32)
    d_lower = norm_back(dy, xhat2, rstd2, gain2)
    dlower_out[...] = d_lower
    d_low = d_lower.astype(BF)
    dlow_out[...] = d_low
    wide = d_low.astype(F32)
    sums_out[0:1] = col_sums(wide)
    sums_out[1:2] = col_sums(dy * xhat2)
    sums_out[2:3] = col_sums(dy)
    keep = jnp.where(first, wide[:, :hw], wide[:, hw:]).astype(BF)
    send = jnp.where(first, wide[:, hw:], wide[:, :hw]).astype(BF)
    send_out[my_rows] = tdot(actives[0], send).astype(BF)
    send_out[its_rows] = tdot(actives[1], send).astype(BF)
    keep_out[my_rows] = tdot(actives[0], keep).astype(BF)
    keep_out[its_rows] = tdot(actives[1], keep).astype(BF)


def middle_kernel(
    c_ref, dlower, dlow, hlow, xhat, rstd, gp, m2, o2, m3, o3, vec, context, ratio, denom, q, state, far,
    dresid_out, dn_out, later_out, keep_out, send_out, sums_out, du_sums_out, near_out,
):
    c = c_ref[0]
    first = c == 0
    hw = m3.shape[1]
    hf = gp.shape[2]
    my_rows, its_rows = pl.ds(pl.multiple_of(c * hf, hf), hf), pl.ds(pl.multiple_of((1 - c) * hf, hf), hf)
    wide = dlow[...].astype(F32)
    keep = jnp.where(first, wide[:, :hw], wide[:, hw:]).astype(BF)
    send = jnp.where(first, wide[:, hw:], wide[:, :hw]).astype(BF)
    h_low = hlow[...]
    d_hidden = dlower[...]
    for rows, w, at, g_out in ((its_rows, o2, 1, send_out), (my_rows, m2, 0, keep_out)):
        d_active = dot_t(keep, m3[rows]) + dot_t(send, o3[rows])
        d_upper = (d_active * gp[at].astype(F32)).astype(BF)
        du_sums_out[at] = jnp.broadcast_to(col_sums(d_upper.astype(F32)), du_sums_out.shape[1:])
        g_out[:, hw:] = tdot(h_low, d_upper).astype(BF)
        d_hidden = d_hidden + dot_t(d_upper, w[:, hw:])
    xh = xhat[...]
    d_resid = norm_back(d_hidden, xh, rstd[:, 0:1], vec[4:5])
    dresid_out[...] = d_resid
    d_attn = d_resid.astype(BF)
    wide = d_attn.astype(F32)
    sums_out[0:1] = col_sums(wide)
    sums_out[1:2] = col_sums(d_hidden * xh)
    sums_out[2:3] = col_sums(d_hidden)
    keep = jnp.where(first, wide[:, :hw], wide[:, hw:]).astype(BF)
    send = jnp.where(first, wide[:, hw:], wide[:, :hw]).astype(BF)
    send_out[:, :hw] = tdot(context[...], send).astype(BF)
    keep_out[:, :hw] = tdot(context[...], keep).astype(BF)
    d_context = dot_t(keep, m2[:, :hw]) + dot_t(send, o2[:, :hw])
    ones = head_ones()
    width = 2 * hw
    pick = jnp.where(
        lax.broadcasted_iota(jnp.int32, (width, 128), 0) == 64 * lax.broadcasted_iota(jnp.int32, (width, 128), 1), 1.0, 0.0
    ).astype(BF)
    all_denoms = []
    for p in range(width // 128):
        dc = d_context[:, lanes(p)]
        inverse = 1.0 / denom[:, lanes(p)]
        dn = (dc * inverse).astype(BF)
        dd = (-head_sums(dc * ratio[:, lanes(p)], ones) * inverse).astype(BF)
        dn_out[:, lanes(p)] = dn
        all_denoms.append(dd)
        near = jnp.zeros((1, 128), F32)
        for r in range(dlow.shape[0] // 128):
            rows = slice(r * 128, (r + 1) * 128)
            qr = q[rows, lanes(p)]
            packed = fold(tdot(qr, dn[rows]))
            total = col_sums(qr.astype(F32) * dd[rows].astype(F32))
            far_row = far[0:1, lanes(p)]
            later_out[r, :64, lanes(p)] = (far_row * packed).astype(BF)
            later_out[r, 64:, lanes(p)] = jnp.broadcast_to(far_row * total, (16, 128)).astype(BF)
            held = state[r, :, lanes(p)].astype(F32)
            near = near + col_sums(held[:64] * packed) + held[64:65] * total
        near_out[:, lanes(p)] = jnp.broadcast_to(near, (8, 128))
    dn_out[:, width:] = dot(jnp.concatenate(all_denoms, axis=1), pick).astype(BF)


def spread(dn, p):
    lane = lax.broadcasted_iota(jnp.int32, dn.shape, 1)
    wide = dn.astype(F32)
    return [jnp.sum(jnp.where(lane == 2 * p + h, wide, 0.0), axis=1, keepdims=True) for h in (0, 1)]


def query_back_kernel(
    c_ref, tok, q, k, v, hk, hv, dn, dd, table, state, far, phi, s, gh, gl,
    dq_out, g_out, pos_out, sums_out,
):
    p = pl.program_id(0)
    ones = head_ones()
    wmat = table[...].reshape(256, 256)
    far_row = far[0:1]
    first = left_lanes((128, 128))
    pieces = jnp.zeros((256, 256), F32)
    grads = []
    for r in range(q.shape[0] // 128):
        rows = slice(r * 128, (r + 1) * 128)
        kw = jnp.concatenate([hk[rows], k[rows]], axis=0)
        vw = jnp.concatenate([hv[rows], v[rows]], axis=0)
        scores = dot_t(two_heads(q[rows]), kw)
        d0, d1 = spread(dd[rows], p)
        dnr = dn[rows]
        dw = dot_t(two_heads(dnr), vw) + jnp.concatenate([d0, d1], axis=0)
        pieces = pieces + dw * scores
        ds = (dw * wmat).astype(BF)
        bd = block_diagonal(state[r, :64])
        total = state[r, 64:80].astype(F32)[0:1]
        dq = fold(dot(ds, kw)) + far_row * (dot_t(dnr, bd) + jnp.where(first, d0, d1) * total)
        grads.append(
            features_back(dq * phi[rows], s[rows], gh[0], gl[0], ones, 64 ** (-0.25))
        )
    dq = jnp.concatenate(grads, axis=0)
    dq_out[...] = dq
    sums_out[...] = jnp.broadcast_to(col_sums(dq.astype(F32)), sums_out.shape)
    g_out[0] = tdot(tok[...], dq).astype(BF)
    row = lax.broadcasted_iota(jnp.int32, (256, 256), 0)
    col = lax.broadcasted_iota(jnp.int32, (256, 256), 1)
    upside = jnp.where(row + col == 255, 1.0, 0.0).astype(BF)
    high, low = parts(jnp.where(col <= row % 128 + 128, pieces, 0.0))
    turned = dot(upside, high) + dot(upside, low)
    for h in (0, 1):
        pos_out[0, 2 + h : 3 + h] = col_sums(pieces[h * 128 : (h + 1) * 128])
        skewed = pltpu.roll(turned[(1 - h) * 128 : (2 - h) * 128], 0, 1, stride=1, stride_axis=0)
        pos_out[0, h : h + 1] = col_sums(skewed)


def key_back_kernel(
    c_ref, tok, q, k, v, dn, dd, qn, dnn, ddn, table, later, phi, s, gh, gl,
    dk_out, dv_out, gk_out, gv_out, sums_out,
):
    p = pl.program_id(0)
    ones = head_ones()
    tables = jnp.concatenate(
        [table[0, :, 128:], table[1, :, 128:], table[0, :, :128], table[1, :, :128]], axis=0
    )
    dks, dvs = [], []
    for r in range(q.shape[0] // 128):
        rows = slice(r * 128, (r + 1) * 128)
        kr, vr = k[rows], v[rows]
        q4 = jnp.concatenate([two_heads(q[rows]), two_heads(qn[rows])], axis=0)
        dn4 = jnp.concatenate([two_heads(dn[rows]), two_heads(dnn[rows])], axis=0)
        dd4 = jnp.concatenate(spread(dd[rows], p) + spread(ddn[rows], p), axis=0)
        w = (dot_t(q4, kr) * tables).astype(BF)
        ds = ((dot_t(dn4, vr) + dd4) * tables).astype(BF)
        bd = block_diagonal(later[r, :64])
        total = later[r, 64:80].astype(F32)[0:1]
        dk = tdot(ds, q4) + dot_t(vr, bd) + total
        dvs.append((tdot(w, dn4) + dot(kr, bd)).astype(BF))
        dks.append(features_back(dk * phi[rows], s[rows], gh[0], gl[0], ones, 64 ** (-0.25)))
    dk, dv = jnp.concatenate(dks, axis=0), jnp.concatenate(dvs, axis=0)
    dk_out[...] = dk
    dv_out[...] = dv
    sums_out[0:8] = jnp.broadcast_to(col_sums(dk.astype(F32)), (8, 128))
    sums_out[8:16] = jnp.broadcast_to(col_sums(dv.astype(F32)), (8, 128))
    gk_out[0] = tdot(tok[...], dk).astype(BF)
    gv_out[0] = tdot(tok[...], dv).astype(BF)


def tokens_kernel(c_ref, dresid, dq, dk, dv, mine, other, out):
    first = c_ref[0] == 0
    hw = dq.shape[1] // 2
    total = dresid[...]
    for i, d in enumerate((dq, dk, dv)):
        wide = d[...].astype(F32)
        a = jnp.where(first, wide[:, :hw], wide[:, hw:]).astype(BF)
        b = jnp.where(first, wide[:, hw:], wide[:, :hw]).astype(BF)
        cols = slice(i * hw, (i + 1) * hw)
        total = total + dot_t(a, mine[:, cols]) + dot_t(b, other[:, cols])
    out[...] = total


def window_table(exp_bias, window, block_len):
    head_count = exp_bias.shape[0]
    key_span = window + block_len
    period = key_span + block_len
    far_column = exp_bias[:, window : window + 1]
    periodic = jnp.concatenate(
        [
            exp_bias[:, ::-1],
            jnp.zeros((head_count, block_len - 1), F32),
            jnp.broadcast_to(far_column, (head_count, block_len)),
        ],
        axis=1,
    )
    tiled_rows = jnp.tile(periodic, (1, block_len))
    table = tiled_rows[:, : block_len * (period - 1)].reshape(head_count, block_len, period - 1)[
        :, :, :key_span
    ]
    column = lax.broadcasted_iota(jnp.int32, (1, 1, key_span), 2)
    return table - jnp.where(column < window, far_column[:, :, None], 0.0)


def feature_blocks(matrix):
    heads, size, feats = matrix.shape
    zero = jnp.zeros((heads // 2, size, feats), F32)
    even, odd = matrix[0::2], matrix[1::2]
    half = jnp.full(zero.shape, -0.5, F32)
    blocks = jnp.concatenate(
        [
            jnp.concatenate([even, zero], axis=2),
            jnp.concatenate([zero, odd], axis=2),
            jnp.concatenate([half, zero], axis=2),
            jnp.concatenate([zero, half], axis=2),
        ],
        axis=1,
    )
    high = lax.reduce_precision(blocks, 8, 7)
    return high.astype(BF), (blocks - high).astype(BF)


def on_device(
    tokens,
    query_weight,
    query_bias,
    key_weight,
    key_bias,
    value_weight,
    value_bias,
    output_weight,
    output_bias,
    first_gain,
    first_shift,
    up_weight,
    up_bias,
    down_weight,
    down_bias,
    second_gain,
    second_shift,
    position_bias,
    feature_matrix,
    cotangent,
):
    at = Place()
    rows, block, width = tokens.shape
    heads, size, feats = feature_matrix.shape
    window = position_bias.shape[1] - 1
    pairs = heads // 2
    n = rows * block
    hw = width // 2
    ff = up_weight.shape[1]
    hf = ff // 2
    own = query_weight.shape[0]
    up_own = up_bias.shape[0] // own
    tok = tokens.reshape(n, width)
    cot = cotangent.reshape(n, width)
    first = at.c == 0
    flags = jnp.stack([at.c, at.s]).astype(jnp.int32)

    def arr(shape, kind):
        return jax.ShapeDtypeStruct(shape, kind)

    halo_tok = at.along(tok, 1)

    vectors = (
        query_bias, key_bias, value_bias, output_bias, first_gain, first_shift,
        down_bias, second_gain, second_shift,
    )
    count = len(vectors)
    small = jnp.concatenate([v[:, None] for v in vectors] + [up_bias.reshape(own, up_own)], axis=1)
    small = jnp.pad(small, ((0, 0), (0, 128 - small.shape[1])))
    m1, o1 = gather_halves(
        at,
        jnp.concatenate([query_weight[:, :hw], key_weight[:, :hw], value_weight[:, :hw], small], axis=1),
        jnp.concatenate([query_weight[:, hw:], key_weight[:, hw:], value_weight[:, hw:], small], axis=1),
    )
    b_u = m1[:, 3 * hw + count : 3 * hw + count + up_own].reshape(1, ff).astype(F32)
    m2, o2 = gather_halves(
        at,
        jnp.concatenate([output_weight[:, :hw], up_weight[:, :hf]], axis=1),
        jnp.concatenate([output_weight[:, hw:], up_weight[:, hf:]], axis=1),
    )
    m3, o3 = gather_halves(at, down_weight[:, :hw], down_weight[:, hw:])

    exp_bias = jnp.exp(position_bias)
    table = window_table(exp_bias, window, block)
    far = jnp.broadcast_to(jnp.repeat(exp_bias[:, window], size)[None], (8, width))
    gh, gl = feature_blocks(feature_matrix)

    wide32, wide16 = arr((n, width), F32), arr((n, width), BF)
    sums = arr((rows, 80, width), BF)
    sk, k_phi, k, v, local, vec = pl.pallas_call(
        key_kernel,
        out_shape=(wide32, wide32, wide16, wide16, sums, arr((16, width), F32)),
        in_specs=[SCALAR] + [WHOLE] * 5,
        out_specs=(WHOLE,) * 6,
        compiler_params=params(48),
        cost_estimate=cost(2 * n * width * 2 * width, 10e6),
        name="keys",
    )(flags, tok, m1, o1, gh, gl)
    before = sum_before(at, local, False).astype(BF)
    sq, q_phi, q, hk, hv = pl.pallas_call(
        query_kernel,
        out_shape=(wide32, wide32, wide16, wide16, wide16),
        in_specs=[SCALAR] + [WHOLE] * 7,
        out_specs=(WHOLE,) * 5,
        compiler_params=params(48),
        cost_estimate=cost(2 * n * width * 3 * width, 12e6),
        name="queries",
    )(flags, tok, halo_tok, m1, o1, vec, gh, gl)
    q_next = at.along(q, -1)

    def columns(height=n):
        return pl.BlockSpec((height, 128), lambda p, *_: (0, p))

    table_spec = pl.BlockSpec((2, block, window + block), lambda p, *_: (p, 0, 0))
    sums_spec = pl.BlockSpec((rows, 80, 128), lambda p, *_: (0, 0, p))
    g_spec = pl.BlockSpec((1, 256, 128), lambda p, *_: (p, 0, 0))
    tok_spec = pl.BlockSpec((n, width), lambda p, *_: (0, 0))
    dd_spec = pl.BlockSpec((n, 128), lambda p, *_: (0, pairs))
    context, ratio, denom = pl.pallas_call(
        attention_kernel,
        grid=(pairs,),
        out_shape=(wide16, wide32, wide32),
        in_specs=[columns()] * 5 + [table_spec, sums_spec, columns(8)],
        out_specs=(columns(),) * 3,
        compiler_params=params(32),
        cost_estimate=cost(1e9, 8e6),
        name="attention",
    )(q, k, v, hk, hv, table, before, far)

    out, d_lower, d_low, h_low, xhat, rstd, gp, keep3, send3, sums3 = pl.pallas_call(
        forward_kernel,
        out_shape=(
            wide32, wide32, wide16, wide16, wide32, arr((n, 128), F32), arr((2, n, hf), BF),
            arr((ff, hw), BF), arr((ff, hw), BF), arr((8, width), F32),
        ),
        in_specs=[SCALAR] + [WHOLE] * 9,
        out_specs=(WHOLE,) * 10,
        compiler_params=params(56),
        cost_estimate=cost(2 * n * width * (width + 3 * ff), 24e6),
        name="forward",
    )(flags, context, tok, m2, o2, m3, o3, cot, vec, b_u)
    s_d = scatter_halves(at, keep3, send3)
    d_resid, dn, local, keep2, send2, sums2, du_sums, near = pl.pallas_call(
        middle_kernel,
        out_shape=(
            wide32, arr((n, width + 128), BF), sums, arr((width, hw + hf), BF), arr((width, hw + hf), BF),
            arr((8, width), F32), arr((2, 8, hf), F32), arr((8, width), F32),
        ),
        in_specs=[SCALAR] + [WHOLE] * 17,
        out_specs=(WHOLE,) * 8,
        compiler_params=params(56),
        cost_estimate=cost(2 * n * width * (2 * width + 3 * ff), 28e6),
        name="middle",
    )(flags, d_lower, d_low, h_low, xhat, rstd, gp, m2, o2, m3, o3, vec, context, ratio, denom, q, before, far)
    dn_next = at.along(dn, -1)
    after = sum_before(at, local, True).astype(BF)
    s_uo = scatter_halves(at, keep2, send2)

    def half_spec():
        return pl.BlockSpec((1, width, 128), lambda p, c: ((p // (pairs // 2)) ^ c[0], 0, p % (pairs // 2)))

    halves = arr((2, width, hw), BF)
    dq, gq, pos, sums_q = pl.pallas_call(
        query_back_kernel,
        grid_spec=pltpu.PrefetchScalarGridSpec(
            num_scalar_prefetch=1,
            grid=(pairs,),
            in_specs=[tok_spec] + [columns()] * 6 + [dd_spec, table_spec, sums_spec, columns(8)]
            + [columns()] * 2 + [g_spec] * 2,
            out_specs=(
                columns(), half_spec(), pl.BlockSpec((1, 8, 256), lambda p, c: (p, 0, 0)), columns(8),
            ),
        ),
        out_shape=(wide16, halves, arr((pairs, 8, 256), F32), arr((8, width), F32)),
        compiler_params=params(32),
        cost_estimate=cost(2e9, 10e6),
        name="query_back",
    )(flags, tok, q, k, v, hk, hv, dn, dn, table, before, far, q_phi, sq, gh, gl)
    s_q = scatter_halves(at, gq[0], gq[1])
    diag = pos[:, 0:2].reshape(heads, 2 * block)
    plain = pos[:, 2:4].reshape(heads, 2 * block)
    far_grad = (
        jnp.sum(diag[:, : 2 * block - window], axis=1)
        - jnp.sum(plain[:, :window], axis=1)
        + jnp.sum(near[0].reshape(heads, size), axis=1)
    )
    position_grad = sum_everywhere(
        at,
        jnp.concatenate(
            [exp_bias[:, :window] * diag[:, : 2 * block - window - 1 : -1], (exp_bias[:, window] * far_grad)[:, None]], axis=1
        ),
    )
    dk, dv, gk, gv, sums_kv = pl.pallas_call(
        key_back_kernel,
        grid_spec=pltpu.PrefetchScalarGridSpec(
            num_scalar_prefetch=1,
            grid=(pairs,),
            in_specs=[tok_spec] + [columns()] * 4 + [dd_spec] + [columns()] * 2
            + [dd_spec, table_spec, sums_spec] + [columns()] * 2 + [g_spec] * 2,
            out_specs=(columns(), columns(), half_spec(), half_spec(), columns(16)),
        ),
        out_shape=(wide16, wide16, halves, halves, arr((16, width), F32)),
        compiler_params=params(32),
        cost_estimate=cost(3e9, 12e6),
        name="key_back",
    )(flags, tok, q, k, v, dn, dn, q_next, dn_next, dn_next, table, after, k_phi, sk, gh, gl)

    g_small = jnp.stack(
        [sums_q[0], sums_kv[0], sums_kv[8], sums2[0], sums2[1], sums2[2], sums3[0], sums3[1], sums3[2]]
    ).T
    du = jnp.where(first, du_sums[:, 0], du_sums[::-1, 0]).reshape(width, up_own)
    g_small = jnp.concatenate([g_small, du], axis=1)
    g_small = jnp.pad(g_small, ((0, 0), (0, 128 - g_small.shape[1]))).astype(BF)
    s_kv = scatter_halves(
        at,
        jnp.concatenate([gk[0], gv[0], g_small], axis=1),
        jnp.concatenate([gk[1], gv[1], g_small], axis=1),
    )
    d_tokens = pl.pallas_call(
        tokens_kernel,
        out_shape=wide32,
        in_specs=[SCALAR] + [WHOLE] * 6,
        out_specs=WHOLE,
        compiler_params=params(40),
        cost_estimate=cost(2 * n * width * 3 * width, 8e6),
        name="tokens",
    )(flags, d_resid, dq, dk, dv, m1, o1)

    def both(pair, start, size):
        return jnp.concatenate([pair[0][:, start : start + size], pair[1][:, start : start + size]], axis=1)

    s_small = s_kv[0][:, 2 * hw :]
    bq, bk, bv, bo, sg1, ss1, bd, sg2, ss2 = [s_small[:, i] for i in range(count)]
    bu = s_small[:, count : count + up_own].reshape(-1)
    return (
        out.reshape(rows, block, width),
        d_tokens.reshape(rows, block, width),
        both(s_q, 0, hw),
        bq,
        both(s_kv, 0, hw),
        bk,
        both(s_kv, hw, hw),
        bv,
        both(s_uo, 0, hw),
        bo,
        sg1,
        ss1,
        both(s_uo, hw, hf),
        bu,
        both(s_d, 0, hw),
        bd,
        sg2,
        ss2,
        position_grad,
    )


def solution(mesh):
    matrix, vector, split = P(BOTH, None), P(BOTH), P("rows", "seq", None)
    return jax.shard_map(
        on_device,
        mesh=mesh,
        in_specs=(split,)
        + (matrix, vector) * 4
        + (vector, vector)
        + (matrix, vector) * 2
        + (vector, vector)
        + (P(), P(), split),
        out_specs=(split, split)
        + (matrix, vector) * 4
        + (vector, vector)
        + (matrix, vector) * 2
        + (vector, vector)
        + (P(),),
        check_vma=False,
    )
```

```python
import math

import jax
import jax.numpy as jnp
from jax import lax
from jax.experimental import pallas as pl
from jax.experimental.pallas import tpu as pltpu
from jax.sharding import PartitionSpec as P

BOTH = ("seq", "rows")
EPS = 1e-06
BF = jnp.bfloat16
F32 = jnp.float32


class Place:
    def __init__(self):
        self.seq = lax.axis_size("seq")
        self.rows = lax.axis_size("rows")
        self.n = self.seq * self.rows
        self.fast = self.seq == 8 and self.rows == 4
        me = lax.axis_index(BOTH)
        self.c = me % 2
        self.y = (me // 2) % 2
        self.x = (me // 4) % 2
        self.z = me // 8
        self.s = lax.axis_index("seq")

    def flip(self, a, stride):
        return lax.ppermute(a, BOTH, [(d, d ^ stride) for d in range(self.n)])

    def swap_c(self, a):
        return self.flip(a, 1)

    def swap_y(self, a):
        return self.flip(a, 2)

    def swap_x(self, a):
        return self.flip(a, 4)

    def turn_z(self, a, by):
        return lax.ppermute(a, BOTH, [(d, (d + 8 * by) % self.n) for d in range(self.n)])

    def along(self, a, by):
        pairs = [(i, i + by) for i in range(self.seq) if 0 <= i + by < self.seq]
        return lax.ppermute(a, "seq", pairs)


def after(a, *others):
    return lax.optimization_barrier((a, others))[0]


def ordered(first, mine, other, axis):
    return jnp.where(
        first, jnp.stack([mine, other], axis=axis), jnp.stack([other, mine], axis=axis)
    )


class Gather:
    def __init__(self, at, name, left, right, small):
        self.at, self.name = at, name
        self.r, self.half = left.shape
        self.first = at.c == 0
        self.left, self.right, self.small = left, right, small
        self.done = ()

    def step_core(self, *wait):
        if not self.at.fast:
            return
        with jax.named_scope(self.name + "_core"):
            got = self.at.swap_c(after(jnp.where(self.first, self.right, self.left), *wait))
            kept = jnp.where(self.first, self.left, self.right)
            piece = ordered(self.first, kept, got, 0)
            mine = after(self.small, piece)
            small = ordered(self.first, mine, self.at.swap_c(mine), 0)
            self.half += self.small.shape[1]
            self.piece = jnp.concatenate([piece, small], axis=2).reshape(2 * self.r, self.half)
            self.done = (got,)

    def step_z(self, *wait):
        if not self.at.fast:
            return
        at = self.at
        with jax.named_scope(self.name + "_z"):
            piece = after(self.piece, *wait)
            turned = [at.turn_z(piece, by) for by in (1, 2, 3)]
            rel = jnp.stack([piece, turned[2], turned[1], turned[0]])
            by_z = lax.dynamic_slice_in_dim(jnp.concatenate([rel, rel]), (4 - at.z) % 4, 4)
            self.low, self.high = by_z[:2], by_z[2:]
            self.done = tuple(turned)

    def step_one(self, *wait):
        if not self.at.fast:
            return
        at = self.at
        with jax.named_scope(self.name + "_one"):
            low, high = after(self.low, *wait), after(self.high, *wait)
            got = at.swap_x(low), at.swap_y(high)
            self.low = ordered(at.x == 0, low, got[0], 1)
            self.high = ordered(at.y == 0, high, got[1], 1)
            self.done = got

    def step_two(self, *wait):
        if not self.at.fast:
            return
        at = self.at
        with jax.named_scope(self.name + "_two"):
            low, high = after(self.low, *wait), after(self.high, *wait)
            got = at.swap_y(low), at.swap_x(high)
            low = ordered(at.y == 0, low, got[0], 2)
            high = ordered(at.x == 0, high, got[1], 1)
            self.mine = jnp.concatenate([low, high]).reshape(at.n * self.r, self.half)
            self.done = got

    def step_last(self, *wait):
        at = self.at
        with jax.named_scope(self.name + "_last"):
            if not at.fast:
                left = lax.all_gather(jnp.concatenate([self.left, self.small], axis=1), BOTH, axis=0, tiled=True)
                right = lax.all_gather(jnp.concatenate([self.right, self.small], axis=1), BOTH, axis=0, tiled=True)
                return jnp.where(self.first, left, right), jnp.where(self.first, right, left)
            mine = after(self.mine, *wait)
            other = at.swap_c(mine)
            self.done = (other,)
            return mine, other


def half_at(a, index, axis):
    return lax.dynamic_index_in_dim(a, index, axis, keepdims=False)


def plus(kept, got):
    return (kept.astype(F32) + got.astype(F32)).astype(BF)


class Scatter:
    def __init__(self, at, name, keeps, sends):
        self.at, self.name, self.keeps, self.sends = at, name, keeps, sends
        self.total = keeps[0].shape[0]
        self.half = sum(k.shape[1] for k in keeps)
        self.r = self.total // at.n
        self.first = at.c == 0
        self.done = ()

    def step_core(self, *wait):
        if not self.at.fast:
            return
        at = self.at
        with jax.named_scope(self.name + "_core"):
            got = [at.swap_c(after(send, *wait)) for send in self.sends]
            mine = jnp.concatenate([plus(k, g) for k, g in zip(self.keeps, got)], axis=1)
            mine = mine.reshape(4, 2, 2, 2 * self.r, self.half)
            self.low, self.high = mine[:2], mine[2:]
            self.done = tuple(got)

    def step_one(self, *wait):
        if not self.at.fast:
            return
        at = self.at
        with jax.named_scope(self.name + "_one"):
            low, high = after(self.low, *wait), after(self.high, *wait)
            got = at.swap_y(half_at(low, 1 - at.y, 2)), at.swap_x(half_at(high, 1 - at.x, 1))
            self.low = plus(half_at(low, at.y, 2), got[0])
            self.high = plus(half_at(high, at.x, 1), got[1])
            self.done = got

    def step_two(self, *wait):
        if not self.at.fast:
            return
        at = self.at
        with jax.named_scope(self.name + "_two"):
            low, high = after(self.low, *wait), after(self.high, *wait)
            got = at.swap_x(half_at(low, 1 - at.x, 1)), at.swap_y(half_at(high, 1 - at.y, 1))
            low = plus(half_at(low, at.x, 1), got[0])
            high = plus(half_at(high, at.y, 1), got[1])
            self.by_z = jnp.concatenate([low, high])
            self.done = got

    def step_z(self, *wait):
        if not self.at.fast:
            return
        at = self.at
        with jax.named_scope(self.name + "_z"):
            by_z = after(self.by_z, *wait)
            got = [at.turn_z(half_at(by_z, (at.z + by) % 4, 0), by) for by in (1, 2, 3)]
            total = half_at(by_z, at.z, 0).astype(F32) + got[0].astype(F32) + got[1].astype(F32) + got[2].astype(F32)
            self.piece = total.reshape(2, self.r, self.half)
            self.done = tuple(got)

    def step_last(self, *wait):
        at = self.at
        with jax.named_scope(self.name + "_last"):
            if not at.fast:
                keep, send = jnp.concatenate(self.keeps, axis=1), jnp.concatenate(self.sends, axis=1)
                left = jnp.where(self.first, keep, send).astype(F32)
                right = jnp.where(self.first, send, keep).astype(F32)
                return (
                    lax.psum_scatter(left, BOTH, scatter_dimension=0, tiled=True),
                    lax.psum_scatter(right, BOTH, scatter_dimension=0, tiled=True),
                )
            piece = after(self.piece, *wait)
            stays = half_at(piece, at.c, 0)
            got = at.swap_c(half_at(piece, 1 - at.c, 0))
            self.done = (got,)
            return jnp.where(self.first, stays, got), jnp.where(self.first, got, stays)


class Before:
    def __init__(self, at, name, a, reverse):
        self.at, self.name, self.a, self.reverse = at, name, a, reverse
        self.fast = at.fast and a.shape[0] == 2
        self.done = ()

    def step_beside(self):
        if self.fast:
            at = self.at
            with jax.named_scope(self.name + "_beside"):
                self.got = at.swap_x(half_at(self.a, 1 - at.x, 0))
                self.own = half_at(self.a, at.x, 0)
                self.pair = plus(self.own, self.got)
                self.done = (self.got,)

    def step_z(self, *wait):
        if self.fast:
            at = self.at
            with jax.named_scope(self.name + "_z"):
                pair = after(self.pair, *wait)
                got = []
                for by in (1, 2, 3):
                    if self.reverse:
                        pairs = [(d, d - 8 * by) for d in range(8 * by, at.n)]
                    else:
                        pairs = [(d, d + 8 * by) for d in range(at.n - 8 * by)]
                    got.append(lax.ppermute(pair, BOTH, pairs))
                self.done = tuple(got)

    def step_last(self, *wait):
        at, a, reverse = self.at, self.a, self.reverse
        with jax.named_scope(self.name + "_last"):
            if not self.fast:
                everything = lax.all_gather(a, "seq").astype(F32)
                index = jnp.arange(at.seq).reshape((-1,) + (1,) * a.ndim)
                reached = index > at.s if reverse else index < at.s
                return jnp.sum(jnp.where(reached, everything, 0.0), axis=0).astype(BF)
            inner = (at.x == 0) if reverse else (at.x == 1)
            got = [after(g, *wait).astype(F32) for g in self.done]
            self.total = got[0] + got[1] + got[2]
            mine = (self.total + jnp.where(inner, self.got.astype(F32), 0.0)).astype(BF)
            send = (self.total + jnp.where(inner, 0.0, self.own.astype(F32))).astype(BF)
            return ordered(at.x == 0, mine, at.swap_x(send), 0)


class Everywhere:
    def __init__(self, at, a):
        self.at, self.a, self.done = at, a, ()

    def step(self, stride, *wait):
        if self.at.fast:
            with jax.named_scope("everywhere"):
                got = self.at.flip(after(self.a, *wait), stride)
                self.a = self.a + got
                self.done = (got,)

    def step_z(self, *wait):
        at = self.at
        with jax.named_scope("everywhere"):
            if not at.fast:
                return lax.psum(self.a, BOTH)
            a = after(self.a, *wait)
            rel = jnp.stack([a] + [at.turn_z(a, by) for by in (3, 2, 1)])
            by_z = lax.dynamic_slice_in_dim(jnp.concatenate([rel, rel]), (4 - at.z) % 4, 4)
            return (by_z[0] + by_z[1]) + (by_z[2] + by_z[3])


VMEM = pltpu.VMEM
SCALAR = pl.BlockSpec(memory_space=pltpu.SMEM)
WHOLE = pl.BlockSpec(memory_space=VMEM)


def params(mib):
    return pltpu.CompilerParams(vmem_limit_bytes=60 * 2**20)


def cost(micros):
    return pl.CostEstimate(flops=int(micros * 1e9), bytes_accessed=int(micros * 1e6), transcendentals=0)


def tdot(a, b):
    return lax.dot_general(a, b, (((0,), (0,)), ((), ())), preferred_element_type=F32)


def dot_t(a, b):
    return lax.dot_general(a, b, (((1,), (1,)), ((), ())), preferred_element_type=F32)


def dot(a, b):
    return jnp.dot(a, b, preferred_element_type=F32)


def parts(a):
    high = a.astype(BF)
    return high, (a - high.astype(F32)).astype(BF)


def left_lanes(shape):
    return lax.broadcasted_iota(jnp.int32, shape, len(shape) - 1) % 128 < 64


def two_heads(a):
    first = left_lanes(a.shape)
    wide = a.astype(F32)
    return jnp.concatenate(
        [jnp.where(first, wide, 0.0), jnp.where(first, 0.0, wide)], axis=0
    ).astype(BF)


def fold(a):
    half = a.shape[0] // 2
    return jnp.where(left_lanes((half, a.shape[1])), a[:half], a[half:])


def head_ones():
    row = lax.broadcasted_iota(jnp.int32, (128, 128), 0) // 64
    col = lax.broadcasted_iota(jnp.int32, (128, 128), 1) // 64
    return jnp.where(row == col, 1.0, 0.0).astype(BF)


def head_sums(a, ones):
    high, low = parts(a)
    return dot(high, ones) + dot(low, ones)


def features(s, g_high, g_low):
    high, low = parts(jnp.concatenate([s, s * s], axis=1))
    return jnp.exp(dot(high, g_high) + dot(high, g_low) + dot(low, g_high)) * 0.125


def features_back(t, s, g_high, g_low, ones, scale):
    high, low = parts(t)
    f_high, f_low = g_high[:128], g_low[:128]
    back = dot_t(high, f_high) + dot_t(high, f_low) + dot_t(low, f_high)
    return ((back - s * (dot(high, ones) + dot(low, ones))) * scale).astype(BF)


def lanes(p):
    return slice(p * 128, (p + 1) * 128)


def key_kernel(c_ref, tok, mine, other, gh, gl, s_out, phi_out, feat_out, v_out, state_out, vec_out):
    first = c_ref[0] == 0
    pairs, block = gh.shape[0], 128
    hw = pairs * 64
    eye = jnp.where(
        lax.broadcasted_iota(jnp.int32, (128, 128), 0) == lax.broadcasted_iota(jnp.int32, (128, 128), 1), 1.0, 0.0
    ).astype(BF)
    vecs = dot_t(eye, mine[:, 3 * hw :])[:16]
    vec_out[...] = vecs
    a = dot(tok[...], mine[:, hw : 3 * hw])
    b = dot(tok[...], other[:, hw : 3 * hw])
    left, right = jnp.where(first, a, b), jnp.where(first, b, a)
    scale = 64 ** (-0.25)
    for p in range(pairs):
        half, at = (left, p * 128) if p < pairs // 2 else (right, p * 128 - hw)
        s = (half[:, at : at + 128] + vecs[1:2, lanes(p)]) * scale
        v = (half[:, hw + at : hw + at + 128] + vecs[2:3, lanes(p)]).astype(BF)
        phi = features(s, gh[p], gl[p])
        k = phi.astype(BF)
        s_out[:, lanes(p)] = s
        phi_out[:, lanes(p)] = phi
        feat_out[:, lanes(p)] = k
        v_out[:, lanes(p)] = v
        for r in range(tok.shape[0] // block):
            rows = slice(r * block, (r + 1) * block)
            state_out[r, :64, lanes(p)] = fold(tdot(k[rows], v[rows])).astype(BF)
            total = jnp.sum(k[rows].astype(F32), axis=0, keepdims=True)
            state_out[r, 64:, lanes(p)] = jnp.broadcast_to(total, (16, 128)).astype(BF)


def query_kernel(c_ref, tok, mine, other, vec, gh, gl, s_out, phi_out, feat_out):
    first = c_ref[0] == 0
    pairs = gh.shape[0]
    hw = pairs * 64
    a, b = dot(tok[...], mine[:, :hw]), dot(tok[...], other[:, :hw])
    left, right = jnp.where(first, a, b), jnp.where(first, b, a)
    for p in range(pairs):
        half, at = (left, p * 128) if p < pairs // 2 else (right, p * 128 - hw)
        s = (half[:, at : at + 128] + vec[0:1, lanes(p)]) * 64 ** (-0.25)
        phi = features(s, gh[p], gl[p])
        s_out[:, lanes(p)] = s
        phi_out[:, lanes(p)] = phi
        feat_out[:, lanes(p)] = phi.astype(BF)


def halo_kernel(c_ref, halo, mine, other, vec, gh, gl, hk_out, hv_out):
    first, inner = c_ref[0] == 0, c_ref[1] > 0
    pairs = gh.shape[0]
    hw = pairs * 64
    a, b = dot(halo[...], mine[:, hw : 3 * hw]), dot(halo[...], other[:, hw : 3 * hw])
    left, right = jnp.where(first, a, b), jnp.where(first, b, a)
    for p in range(pairs):
        half, at = (left, p * 128) if p < pairs // 2 else (right, p * 128 - hw)
        s = (half[:, at : at + 128] + vec[1:2, lanes(p)]) * 64 ** (-0.25)
        v = half[:, hw + at : hw + at + 128] + vec[2:3, lanes(p)]
        hk_out[:, lanes(p)] = jnp.where(inner, features(s, gh[p], gl[p]), 0.0).astype(BF)
        hv_out[:, lanes(p)] = jnp.where(inner, v, 0.0).astype(BF)


def window_weights(base):
    turned = pltpu.roll(jnp.broadcast_to(base, (128, 256)), 0, 1, stride=1, stride_axis=0)
    row = lax.broadcasted_iota(jnp.int32, (128, 256), 0)
    col = lax.broadcasted_iota(jnp.int32, (128, 256), 1)
    return jnp.where(col > row + 128, 0.0, turned - jnp.where(col < 128, base[:, 255:256], 0.0))


def pair_at(step, c, pairs):
    return (step + (pairs // 2) * (1 - c)) % pairs


def block_diagonal(packed):
    return two_heads(packed)


def attention_kernel(q, k, v, hk, hv, table, state, far, context_out, turned_out, ratio_out, denom_out):
    ones = head_ones()
    wmat = jnp.concatenate([window_weights(table[0, 0:1]), window_weights(table[0, 1:2])], axis=0)
    far_row = far[0:1]
    for r in range(q.shape[0] // 128):
        rows = slice(r * 128, (r + 1) * 128)
        qr = q[rows]
        kw = jnp.concatenate([hk[rows], k[rows]], axis=0)
        vw = jnp.concatenate([hv[rows], v[rows]], axis=0)
        weighted = dot_t(two_heads(qr), kw) * wmat
        numer = fold(dot(weighted.astype(BF), vw))
        near = jnp.sum(weighted, axis=1, keepdims=True)
        near = fold(jnp.broadcast_to(near, (256, 128)))
        bd = block_diagonal(state[r, :64])
        total = state[r, 64:80].astype(F32)[0:1]
        numer = numer + far_row * dot(qr, bd)
        denom = near + far_row * head_sums(qr.astype(F32) * total, ones)
        ratio = numer / denom
        context_out[rows] = ratio.astype(BF)
        turned_out[:, rows] = ratio.T.astype(BF)
        ratio_out[rows] = ratio
        denom_out[rows] = denom


def normed(x):
    centred = x - jnp.mean(x, axis=-1, keepdims=True)
    rstd = lax.rsqrt(jnp.mean(centred * centred, axis=-1, keepdims=True) + EPS)
    return centred * rstd, rstd


def norm_back(dy, xhat, rstd, gain):
    d = dy * gain
    return rstd * (
        d - jnp.mean(d, axis=-1, keepdims=True) - xhat * jnp.mean(d * xhat, axis=-1, keepdims=True)
    )


def col_sums(a):
    return jnp.sum(a, axis=0, keepdims=True)


def forward_kernel(
    context, tok, wu, wo, wd, cot, vec, bu,
    out, dlower_out, dlow_out, hlow_out, xhat_out, rstd_out, gp_out, grad_out, sums_out,
):
    attn = jnp.concatenate([dot(context[...], wo[i]) for i in range(wo.shape[0])], axis=1)
    xhat, rstd = normed(tok[...].astype(F32) + attn + vec[3:4])
    hidden = xhat * vec[4:5] + vec[5:6]
    xhat_out[...] = xhat
    rstd_out[...] = jnp.broadcast_to(rstd, rstd_out.shape)
    h_low = hidden.astype(BF)
    hlow_out[...] = h_low
    step = wu.shape[2]
    lower = hidden + vec[6:7]
    actives = []
    for i in range(wu.shape[0]):
        cols = slice(i * step, (i + 1) * step)
        upper = dot(h_low, wu[i]) + bu[:, cols]
        cdf = 0.5 * (1.0 + lax.erf(upper * 2.0 ** (-0.5)))
        pdf = jnp.exp(-0.5 * upper * upper) * (2.0 * math.pi) ** (-0.5)
        gp_out[:, cols] = (cdf + upper * pdf).astype(BF)
        actives.append((upper * cdf).astype(BF))
        lower = lower + dot(actives[-1], wd[cols])
    xhat2, rstd2 = normed(lower)
    gain2 = vec[7:8]
    out[...] = xhat2 * gain2 + vec[8:9]
    dy = cot[...].astype(F32)
    d_lower = norm_back(dy, xhat2, rstd2, gain2)
    dlower_out[...] = d_lower
    d_low = d_lower.astype(BF)
    dlow_out[...] = d_low
    sums_out[0:1] = col_sums(d_low.astype(F32))
    sums_out[1:2] = col_sums(dy * xhat2)
    sums_out[2:3] = col_sums(dy)
    for i in range(wu.shape[0]):
        grad_out[i * step : (i + 1) * step, : d_low.shape[1]] = tdot(actives[i], d_low).astype(BF)


def upper_back_kernel(dlow, hlow, gp, wd, du_out, grad_out, sums_out):
    d_low, h_low = dlow[...], hlow[...]
    step = grad_out.shape[2]
    for i in range(grad_out.shape[0]):
        cols = slice(i * step, (i + 1) * step)
        d_upper = (dot_t(d_low, wd[cols]) * gp[:, cols].astype(F32)).astype(BF)
        du_out[:, cols] = d_upper
        sums_out[:, cols] = jnp.broadcast_to(col_sums(d_upper.astype(F32)), (8, step))
        grad_out[i] = tdot(h_low, d_upper).astype(BF)


def middle_kernel(
    dlower, du, xhat, rstd, wu, wo, vec, ratio, denom, q, state, far,
    dresid_out, dattn_out, dn_out, later_out, sums_out, near_out,
):
    hw = dlower.shape[1] // 2
    d_hidden = dlower[...]
    step = wu.shape[2]
    for i in range(wu.shape[0]):
        d_hidden = d_hidden + dot_t(du[:, i * step : (i + 1) * step], wu[i])
    xh = xhat[...]
    d_resid = norm_back(d_hidden, xh, rstd[:, 0:1], vec[4:5])
    dresid_out[...] = d_resid
    d_attn = d_resid.astype(BF)
    dattn_out[...] = d_attn
    sums_out[0:1] = col_sums(d_attn.astype(F32))
    sums_out[1:2] = col_sums(d_hidden * xh)
    sums_out[2:3] = col_sums(d_hidden)
    step = wo.shape[2]
    d_context = sum(dot_t(d_resid[:, i * step : (i + 1) * step].astype(BF), wo[i]) for i in range(wo.shape[0]))
    ones = head_ones()
    width = 2 * hw
    pick = jnp.where(
        lax.broadcasted_iota(jnp.int32, (width, 128), 0) == 64 * lax.broadcasted_iota(jnp.int32, (width, 128), 1), 1.0, 0.0
    ).astype(BF)
    all_denoms = []
    for p in range(width // 128):
        dc = d_context[:, lanes(p)]
        inverse = 1.0 / denom[:, lanes(p)]
        dn = (dc * inverse).astype(BF)
        dd = (-head_sums(dc * ratio[:, lanes(p)], ones) * inverse).astype(BF)
        dn_out[:, lanes(p)] = dn
        all_denoms.append(dd)
        near = jnp.zeros((1, 128), F32)
        for r in range(dlower.shape[0] // 128):
            rows = slice(r * 128, (r + 1) * 128)
            qr = q[rows, lanes(p)]
            packed = fold(tdot(qr, dn[rows]))
            total = col_sums(qr.astype(F32) * dd[rows].astype(F32))
            far_row = far[0:1, lanes(p)]
            later_out[r, :64, lanes(p)] = (far_row * packed).astype(BF)
            later_out[r, 64:, lanes(p)] = jnp.broadcast_to(far_row * total, (16, 128)).astype(BF)
            held = state[r, :, lanes(p)].astype(F32)
            near = near + col_sums(held[:64] * packed) + held[64:65] * total
        near_out[:, lanes(p)] = jnp.broadcast_to(near, (8, 128))
    dn_out[:, width:] = dot(jnp.concatenate(all_denoms, axis=1), pick).astype(BF)


def spread(dn, p):
    lane = lax.broadcasted_iota(jnp.int32, dn.shape, 1)
    wide = dn.astype(F32)
    return [jnp.sum(jnp.where(lane == 2 * p + h, wide, 0.0), axis=1, keepdims=True) for h in (0, 1)]


def query_back_kernel(
    c_ref, tok, context, dattn, q, k, v, hk, hv, dn, dd, table, state, far, phi, s, gh, gl, near,
    dq_out, keep_out, send_out, pos_out, sums_out,
):
    steps = pl.num_programs(0)
    p = pair_at(pl.program_id(0), c_ref[0], steps)
    ones = head_ones()
    wmat = jnp.concatenate([window_weights(table[0, 0:1]), window_weights(table[0, 1:2])], axis=0)
    far_row = far[0:1]
    first = left_lanes((128, 128))
    pieces = jnp.zeros((256, 256), F32)
    grads = []
    for r in range(q.shape[0] // 128):
        rows = slice(r * 128, (r + 1) * 128)
        kw = jnp.concatenate([hk[rows], k[rows]], axis=0)
        vw = jnp.concatenate([hv[rows], v[rows]], axis=0)
        scores = dot_t(two_heads(q[rows]), kw)
        d0, d1 = spread(dd[rows], p)
        dnr = dn[rows]
        dw = dot_t(two_heads(dnr), vw) + jnp.concatenate([d0, d1], axis=0)
        pieces = pieces + dw * scores
        ds = (dw * wmat).astype(BF)
        bd = block_diagonal(state[r, :64])
        total = state[r, 64:80].astype(F32)[0:1]
        dq = fold(dot(ds, kw)) + far_row * (dot_t(dnr, bd) + jnp.where(first, d0, d1) * total)
        grads.append(
            features_back(dq * phi[rows], s[rows], gh[0], gl[0], ones, 64 ** (-0.25))
        )
    dq = jnp.concatenate(grads, axis=0)
    dq_out[...] = dq
    sums_out[...] = jnp.broadcast_to(col_sums(dq.astype(F32)), sums_out.shape)
    grad = jnp.concatenate([dot(tok[...], dq), dot(context[...], dattn[...])], axis=1).astype(BF)
    place_half(grad, keep_out, send_out)
    row = lax.broadcasted_iota(jnp.int32, (256, 256), 0)
    col = lax.broadcasted_iota(jnp.int32, (256, 256), 1)
    mirror = jnp.where(row + col == 255, 1.0, 0.0).astype(BF)
    high, low = parts(jnp.where(col <= row % 128 + 128, pieces, 0.0))
    mirrored = dot(high, mirror) + dot(low, mirror)
    lane = lax.broadcasted_iota(jnp.int32, (1, 256), 1)
    for h in (0, 1):
        rows = slice(h * 128, (h + 1) * 128)
        by_distance = col_sums(pltpu.roll(mirrored[rows], 129, 1, stride=1, stride_axis=0))
        plain = col_sums(pieces[rows])
        apart = jnp.where(lane >= 128, by_distance, 0.0) - jnp.where(lane < 128, plain, 0.0)
        state_part = jnp.where(lane[:, :128] // 64 == h, near[0:1], 0.0)
        far_sum = jnp.sum(apart, axis=1, keepdims=True) + jnp.sum(state_part, axis=1, keepdims=True)
        pos_out[0, h : h + 1] = jnp.where(lane < 128, by_distance, far_sum)


def place_half(grad, keep_out, send_out):
    early = pl.program_id(0) < pl.num_programs(0) // 2

    @pl.when(early)
    def _():
        send_out[...] = grad

    @pl.when(jnp.logical_not(early))
    def _():
        keep_out[...] = grad


def key_back_kernel(
    c_ref, tok, q, k, v, dn, dd, qn, dnn, ddn, table, later, phi, s, gh, gl, rows_in,
    dk_out, dv_out, keep_out, send_out, small_out,
):
    p = pair_at(pl.program_id(0), c_ref[0], pl.num_programs(0))
    ones = head_ones()
    first, second = window_weights(table[0, 0:1]), window_weights(table[0, 1:2])
    tables = jnp.concatenate([first[:, 128:], second[:, 128:], first[:, :128], second[:, :128]], axis=0)
    dks, dvs = [], []
    for r in range(q.shape[0] // 128):
        rows = slice(r * 128, (r + 1) * 128)
        kr, vr = k[rows], v[rows]
        q4 = jnp.concatenate([two_heads(q[rows]), two_heads(qn[rows])], axis=0)
        dn4 = jnp.concatenate([two_heads(dn[rows]), two_heads(dnn[rows])], axis=0)
        dd4 = jnp.concatenate(spread(dd[rows], p) + spread(ddn[rows], p), axis=0)
        w = (dot_t(q4, kr) * tables).astype(BF)
        ds = ((dot_t(dn4, vr) + dd4) * tables).astype(BF)
        bd = block_diagonal(later[r, :64])
        total = later[r, 64:80].astype(F32)[0:1]
        dk = tdot(ds, q4) + dot_t(vr, bd) + total
        dvs.append((tdot(w, dn4) + dot(kr, bd)).astype(BF))
        dks.append(features_back(dk * phi[rows], s[rows], gh[0], gl[0], ones, 64 ** (-0.25)))
    dk, dv = jnp.concatenate(dks, axis=0), jnp.concatenate(dvs, axis=0)
    dk_out[...] = dk
    dv_out[...] = dv
    place_half(jnp.concatenate([dot(tok[...], dk), dot(tok[...], dv)], axis=1).astype(BF), keep_out, send_out)
    row = lax.broadcasted_iota(jnp.int32, (16, 128), 0)
    lane = lax.broadcasted_iota(jnp.int32, (16, 128), 1)
    late = jnp.where(row == 1, col_sums(dk.astype(F32)), 0.0) + jnp.where(row == 2, col_sums(dv.astype(F32)), 0.0)
    small_out[...] = tdot((rows_in[...] + late).astype(BF), jnp.where(row == lane, 1.0, 0.0).astype(BF)).astype(BF)


def tokens_kernel(c_ref, dresid, dq, dk, dv, mine, other, out):
    first = c_ref[0] == 0
    hw = dq.shape[1] // 2
    total = dresid[...]
    for i, d in enumerate((dq, dk, dv)):
        wide = d[...].astype(F32)
        a = jnp.where(first, wide[:, :hw], wide[:, hw:]).astype(BF)
        b = jnp.where(first, wide[:, hw:], wide[:, :hw]).astype(BF)
        cols = slice(i * hw, (i + 1) * hw)
        total = total + dot_t(a, mine[:, cols]) + dot_t(b, other[:, cols])
    out[...] = total


def feature_blocks(matrix):
    heads, size, feats = matrix.shape
    zero = jnp.zeros((heads // 2, size, feats), F32)
    even, odd = matrix[0::2], matrix[1::2]
    half = jnp.full(zero.shape, -0.5, F32)
    blocks = jnp.concatenate(
        [
            jnp.concatenate([even, zero], axis=2),
            jnp.concatenate([zero, odd], axis=2),
            jnp.concatenate([half, zero], axis=2),
            jnp.concatenate([zero, half], axis=2),
        ],
        axis=1,
    )
    high = lax.reduce_precision(blocks, 8, 7)
    return high.astype(BF), (blocks - high).astype(BF)


def on_device(
    tokens,
    query_weight,
    query_bias,
    key_weight,
    key_bias,
    value_weight,
    value_bias,
    output_weight,
    output_bias,
    first_gain,
    first_shift,
    up_weight,
    up_bias,
    down_weight,
    down_bias,
    second_gain,
    second_shift,
    position_bias,
    feature_matrix,
    cotangent,
):
    at = Place()
    rows, block, width = tokens.shape
    heads, size, feats = feature_matrix.shape
    window = position_bias.shape[1] - 1
    pairs = heads // 2
    n = rows * block
    hw = width // 2
    ff = up_weight.shape[1]
    hf = ff // 2
    own = query_weight.shape[0]
    up_own = up_bias.shape[0] // own
    tok = tokens.reshape(n, width)
    cot = cotangent.reshape(n, width)
    flags = jnp.stack([at.c, at.s]).astype(jnp.int32)

    def arr(shape, kind):
        return jax.ShapeDtypeStruct(shape, kind)

    halo_tok = at.along(tok, 1)
    tok_t = tok.T

    vectors = (
        query_bias, key_bias, value_bias, output_bias, first_gain, first_shift,
        down_bias, second_gain, second_shift,
    )
    count = len(vectors)
    small = jnp.concatenate(vectors + (up_bias,)).reshape(count + up_own, own).T
    small = jnp.pad(small, ((0, 0), (0, 128 - small.shape[1])))
    slices = down_weight.shape[0] // own
    step, wo_step = ff // slices, width // slices

    def stacked(a):
        return jnp.concatenate(jnp.split(a, slices, axis=1), axis=0)

    rest = lax.all_gather(
        jnp.concatenate([down_weight, stacked(up_weight), stacked(output_weight)], axis=1), BOTH, axis=0, tiled=True
    )
    g1 = Gather(
        at,
        "qkv",
        jnp.concatenate([query_weight[:, :hw], key_weight[:, :hw], value_weight[:, :hw]], axis=1),
        jnp.concatenate([query_weight[:, hw:], key_weight[:, hw:], value_weight[:, hw:]], axis=1),
        small,
    )
    exp_bias = jnp.exp(position_bias)
    table = jnp.concatenate(
        [exp_bias[:, ::-1], jnp.broadcast_to(exp_bias[:, window:], (heads, block - 1))], axis=1
    ).reshape(pairs, 2, window + block)
    table = jnp.pad(table, ((0, 0), (0, 6), (0, 0)))
    far = jnp.broadcast_to(jnp.repeat(exp_bias[:, window], size)[None], (8, width))
    gh, gl = feature_blocks(feature_matrix)

    g1.step_core()
    g1.step_z()
    g1.step_one()
    g1.step_two()
    m1, o1 = g1.step_last(table, far, gh, gl, tok_t)

    wide32, wide16 = arr((n, width), F32), arr((n, width), BF)
    sums = arr((rows, 80, width), BF)
    sk, k_phi, k, v, local, vec = pl.pallas_call(
        key_kernel,
        out_shape=(wide32, wide32, wide16, wide16, sums, arr((16, width), F32)),
        in_specs=[SCALAR] + [WHOLE] * 5,
        out_specs=(WHOLE,) * 6,
        compiler_params=params(48),
        cost_estimate=cost(5),
        name="keys",
    )(flags, tok, m1, o1, gh, gl)
    scan = Before(at, "before", local, False)
    scan.step_beside()
    sq, q_phi, q = pl.pallas_call(
        query_kernel,
        out_shape=(wide32, wide32, wide16),
        in_specs=[SCALAR] + [WHOLE] * 6,
        out_specs=(WHOLE,) * 3,
        compiler_params=params(48),
        cost_estimate=cost(3),
        name="queries",
    )(flags, tok, m1, o1, vec, gh, gl)
    scan.step_z(q)
    hk, hv = pl.pallas_call(
        halo_kernel,
        out_shape=(wide16, wide16),
        in_specs=[SCALAR] + [WHOLE] * 6,
        out_specs=(WHOLE,) * 2,
        compiler_params=params(48),
        cost_estimate=cost(2),
        name="halo",
    )(flags, after(halo_tok, *scan.done), m1, o1, vec, gh, gl)
    before = scan.step_last(hk)
    b_u = m1[:, 3 * hw + count : 3 * hw + count + up_own].reshape(at.n, own, up_own)
    b_u = jnp.swapaxes(after(b_u, hk), 1, 2).reshape(1, ff).astype(F32)
    q_next = at.along(q, -1)

    def columns(height=n):
        return pl.BlockSpec((height, 128), lambda p, *_: (0, p))

    table_spec = pl.BlockSpec((1, 8, window + block), lambda p, *_: (p, 0, 0))
    sums_spec = pl.BlockSpec((rows, 80, 128), lambda p, *_: (0, 0, p))
    g_spec = pl.BlockSpec((1, 256, 128), lambda p, *_: (p, 0, 0))
    tok_spec = pl.BlockSpec((width, n), lambda p, *_: (0, 0))
    dd_spec = pl.BlockSpec((n, 128), lambda p, *_: (0, pairs))
    context, context_t, ratio, denom = pl.pallas_call(
        attention_kernel,
        grid=(pairs,),
        out_shape=(wide16, arr((width, n), BF), wide32, wide32),
        in_specs=[columns()] * 5 + [table_spec, sums_spec, columns(8)],
        out_specs=(columns(), pl.BlockSpec((128, n), lambda p, *_: (p, 0)), columns(), columns()),
        compiler_params=params(32),
        cost_estimate=cost(5),
        name="attention",
    )(q, k, v, hk, hv, table, before, far)

    split = rest.reshape(at.n, slices, own, rest.shape[1])
    wu = jnp.swapaxes(split[..., width : width + step], 0, 1).reshape(slices, width, step)
    wo = jnp.swapaxes(split[..., width + step :], 0, 1).reshape(slices, width, wo_step)
    wd_spec = pl.BlockSpec((ff, width), lambda i: (0, 0), pipeline_mode=pl.Buffered(1))
    out, d_lower, d_low, h_low, xhat, rstd, gp, g_down, sums3 = pl.pallas_call(
        forward_kernel,
        grid=(1,),
        out_shape=(
            wide32, wide32, wide16, wide16, wide32, arr((n, 128), F32), arr((n, ff), BF),
            arr((ff, width + step), BF), arr((8, width), F32),
        ),
        in_specs=[WHOLE] * 4 + [wd_spec] + [WHOLE] * 3,
        out_specs=(WHOLE,) * 9,
        compiler_params=params(56),
        cost_estimate=cost(13),
        name="forward",
    )(context, tok, wu, wo, rest, cot, vec, b_u)
    du, g_up, du_sums = pl.pallas_call(
        upper_back_kernel,
        grid=(1,),
        out_shape=(arr((n, ff), BF), arr((slices, width, step), BF), arr((8, ff), F32)),
        in_specs=[WHOLE] * 3 + [wd_spec],
        out_specs=(WHOLE,) * 3,
        compiler_params=params(48),
        cost_estimate=cost(7),
        name="upper_back",
    )(d_low, h_low, gp, rest)
    g_up = jnp.swapaxes(g_up.reshape(slices, at.n, own, step), 0, 1).reshape(ff, step)
    g_rest = lax.dynamic_update_slice(g_down, g_up, (0, width))
    s_rest = lax.psum_scatter(g_rest, BOTH, scatter_dimension=0, tiled=True).astype(F32)
    s_d = s_rest[:, :width]
    s_u = jnp.concatenate(jnp.split(s_rest[:, width:], slices, axis=0), axis=1)
    d_resid, d_attn, dn, local, sums2, near = pl.pallas_call(
        middle_kernel,
        out_shape=(wide32, wide16, arr((n, width + 128), BF), sums, arr((8, width), F32), arr((8, width), F32)),
        in_specs=[WHOLE] * 12,
        out_specs=(WHOLE,) * 6,
        compiler_params=params(48),
        cost_estimate=cost(7),
        name="middle",
    )(after(d_lower, g_rest), du, xhat, rstd, wu, wo, vec, ratio, denom, q, before, far)
    scan = Before(at, "later", local, True)
    scan.step_beside()
    dn_next = at.along(dn, -1)

    def turned(p, c):
        return pair_at(p, c[0], pairs)

    cols = pl.BlockSpec((n, 128), lambda p, c: (0, turned(p, c)))
    cols8 = pl.BlockSpec((8, 128), lambda p, c: (0, turned(p, c)))
    by_pair = pl.BlockSpec((1, 8, window + block), lambda p, c: (turned(p, c), 0, 0))
    sums_by_pair = pl.BlockSpec((rows, 80, 128), lambda p, c: (0, 0, turned(p, c)))
    g_by_pair = pl.BlockSpec((1, 256, 128), lambda p, c: (turned(p, c), 0, 0))
    kept = pl.BlockSpec((width, 256), lambda p, c: (0, jnp.maximum(p - pairs // 2, 0)))
    sent = pl.BlockSpec((width, 256), lambda p, c: (0, jnp.minimum(p, pairs // 2 - 1)))
    half = arr((width, 2 * hw), BF)
    dq, keep1, send1, pos, sums_q = pl.pallas_call(
        query_back_kernel,
        grid_spec=pltpu.PrefetchScalarGridSpec(
            num_scalar_prefetch=1,
            grid=(pairs,),
            in_specs=[tok_spec] * 2 + [cols] * 7 + [dd_spec, by_pair, sums_by_pair, cols8]
            + [cols] * 2 + [g_by_pair] * 2 + [cols8],
            out_specs=(cols, kept, sent, by_pair, cols8),
        ),
        out_shape=(wide16, half, half, arr((pairs, 8, 256), F32), arr((8, width), F32)),
        compiler_params=params(32),
        cost_estimate=cost(11),
        name="query_back",
    )(flags, after(tok_t, *scan.done), context_t, d_attn, q, k, v, hk, hv, dn, dn, table, before, far, q_phi, sq, gh, gl, near)
    scan.step_z()
    later = scan.step_last(dq, q_next, dn_next)
    everywhere = Everywhere(at, exp_bias * pos[:, :2, : window + 1].reshape(heads, window + 1))
    everywhere.step(1)
    du = du_sums[0].reshape(at.n, up_own, own)
    du = jnp.swapaxes(du, 0, 1).reshape(up_own, width)
    nil = jnp.zeros((2, width), F32)
    early = jnp.concatenate([sums_q[:1], nil, sums2[:3], sums3[:3], du], axis=0)
    early = jnp.pad(early, ((0, 16 - early.shape[0]), (0, 0)))
    dk, dv, keep0, send0, small = pl.pallas_call(
        key_back_kernel,
        grid_spec=pltpu.PrefetchScalarGridSpec(
            num_scalar_prefetch=1,
            grid=(pairs,),
            in_specs=[tok_spec] + [cols] * 4 + [dd_spec] + [cols] * 2
            + [dd_spec, by_pair, sums_by_pair] + [cols] * 2 + [g_by_pair] * 2
            + [pl.BlockSpec((16, 128), lambda p, c: (0, turned(p, c)))],
            out_specs=(cols, cols, kept, sent, pl.BlockSpec((128, 128), lambda p, c: (turned(p, c), 0))),
        ),
        out_shape=(wide16, wide16, half, half, arr((width, 128), BF)),
        compiler_params=params(32),
        cost_estimate=cost(12),
        name="key_back",
    )(flags, after(tok_t, *everywhere.done), q, k, v, dn, dn, q_next, dn_next, dn_next, table, later, k_phi, sk, gh, gl, early)

    r0 = Scatter(at, "d_qkv", (keep1, keep0, small), (send1, send0, small))
    r0.step_core()
    everywhere.step(2, dk)
    r0.step_one(*everywhere.done)
    everywhere.step(4, *r0.done)
    r0.step_two(*everywhere.done)
    two0 = r0.done
    r0.step_z()
    position_grad = everywhere.step_z(*two0)
    s_qkv = r0.step_last()
    d_tokens = pl.pallas_call(
        tokens_kernel,
        out_shape=wide32,
        in_specs=[SCALAR] + [WHOLE] * 6,
        out_specs=WHOLE,
        compiler_params=params(40),
        cost_estimate=cost(3),
        name="tokens",
    )(flags, d_resid, dq, dk, dv, m1, o1)

    def woven(pair, at):
        return jnp.concatenate(
            [half[:, at + p * 256 : at + p * 256 + 128] for half in pair for p in range(pairs // 2)], axis=1
        )

    s_small = s_qkv[0][:, 4 * hw :]
    bq, bk, bv, bo, sg1, ss1, bd, sg2, ss2 = [s_small[:, i] for i in range(count)]
    bu = s_small[:, count : count + up_own].T.reshape(-1)
    return (
        out.reshape(rows, block, width),
        d_tokens.reshape(rows, block, width),
        woven(s_qkv, 0),
        bq,
        woven(s_qkv, 2 * hw),
        bk,
        woven(s_qkv, 2 * hw + 128),
        bv,
        woven(s_qkv, 128),
        bo,
        sg1,
        ss1,
        s_u,
        bu,
        s_d,
        bd,
        sg2,
        ss2,
        position_grad,
    )


def solution(mesh):
    matrix, vector, split = P(BOTH, None), P(BOTH), P("rows", "seq", None)
    return jax.shard_map(
        on_device,
        mesh=mesh,
        in_specs=(split,)
        + (matrix, vector) * 4
        + (vector, vector)
        + (matrix, vector) * 2
        + (vector, vector)
        + (P(), P(), split),
        out_specs=(split, split)
        + (matrix, vector) * 4
        + (vector, vector)
        + (matrix, vector) * 2
        + (vector, vector)
        + (P(),),
        check_vma=False,
    )
```

```python
import functools
import math

import jax
import jax.numpy as jnp
from jax import lax
from jax.experimental import pallas as pl
from jax.experimental.pallas import tpu as pltpu
from jax.sharding import PartitionSpec as P

BOTH = ("seq", "rows")
EPS = 1e-06
BF = jnp.bfloat16
F32 = jnp.float32


class Place:
    def __init__(self):
        self.seq = lax.axis_size("seq")
        self.rows = lax.axis_size("rows")
        self.n = self.seq * self.rows
        self.fast = self.seq == 8 and self.rows == 4
        me = lax.axis_index(BOTH)
        self.c = me % 2
        self.y = (me // 2) % 2
        self.x = (me // 4) % 2
        self.z = me // 8
        self.s = lax.axis_index("seq")

    def flip(self, a, stride):
        return lax.ppermute(a, BOTH, [(d, d ^ stride) for d in range(self.n)])

    def swap_c(self, a):
        return self.flip(a, 1)

    def swap_y(self, a):
        return self.flip(a, 2)

    def swap_x(self, a):
        return self.flip(a, 4)

    def turn_z(self, a, by):
        return lax.ppermute(a, BOTH, [(d, (d + 8 * by) % self.n) for d in range(self.n)])

    def along(self, a, by):
        pairs = [(i, i + by) for i in range(self.seq) if 0 <= i + by < self.seq]
        return lax.ppermute(a, "seq", pairs)


def after(a, *others):
    return lax.optimization_barrier((a, others))[0]


def ordered(first, mine, other, axis):
    return jnp.where(
        first, jnp.stack([mine, other], axis=axis), jnp.stack([other, mine], axis=axis)
    )


class Gather:
    def __init__(self, at, name, left, right, small):
        self.at, self.name = at, name
        self.r, self.half = left.shape
        self.first = at.c == 0
        self.left, self.right, self.small = left, right, small
        self.done = ()

    def step_core(self, *wait):
        if not self.at.fast:
            return
        with jax.named_scope(self.name + "_core"):
            got = self.at.swap_c(after(jnp.where(self.first, self.right, self.left), *wait))
            kept = jnp.where(self.first, self.left, self.right)
            piece = ordered(self.first, kept, got, 0)
            mine = after(self.small, piece)
            small = ordered(self.first, mine, self.at.swap_c(mine), 0)
            self.half += self.small.shape[1]
            self.piece = jnp.concatenate([piece, small], axis=2).reshape(2 * self.r, self.half)
            self.done = (got,)

    def step_z(self, *wait):
        if not self.at.fast:
            return
        at = self.at
        with jax.named_scope(self.name + "_z"):
            piece = after(self.piece, *wait)
            turned = [at.turn_z(piece, by) for by in (1, 2, 3)]
            rel = jnp.stack([piece, turned[2], turned[1], turned[0]])
            by_z = lax.dynamic_slice_in_dim(jnp.concatenate([rel, rel]), (4 - at.z) % 4, 4)
            self.low, self.high = by_z[:2], by_z[2:]
            self.done = tuple(turned)

    def step_one(self, *wait):
        if not self.at.fast:
            return
        at = self.at
        with jax.named_scope(self.name + "_one"):
            low, high = after(self.low, *wait), after(self.high, *wait)
            got = at.swap_x(low), at.swap_y(high)
            self.low = ordered(at.x == 0, low, got[0], 1)
            self.high = ordered(at.y == 0, high, got[1], 1)
            self.done = got

    def step_two(self, *wait):
        if not self.at.fast:
            return
        at = self.at
        with jax.named_scope(self.name + "_two"):
            low, high = after(self.low, *wait), after(self.high, *wait)
            got = at.swap_y(low), at.swap_x(high)
            low = ordered(at.y == 0, low, got[0], 2)
            high = ordered(at.x == 0, high, got[1], 1)
            self.mine = jnp.concatenate([low, high]).reshape(at.n * self.r, self.half)
            self.done = got

    def step_last(self, *wait):
        at = self.at
        with jax.named_scope(self.name + "_last"):
            if not at.fast:
                left = lax.all_gather(jnp.concatenate([self.left, self.small], axis=1), BOTH, axis=0, tiled=True)
                right = lax.all_gather(jnp.concatenate([self.right, self.small], axis=1), BOTH, axis=0, tiled=True)
                return jnp.where(self.first, left, right), jnp.where(self.first, right, left)
            mine = after(self.mine, *wait)
            other = at.swap_c(mine)
            self.done = (other,)
            return mine, other


def half_at(a, index, axis):
    return lax.dynamic_index_in_dim(a, index, axis, keepdims=False)


def plus(kept, got):
    return (kept.astype(F32) + got.astype(F32)).astype(BF)


class Scatter:
    def __init__(self, at, name, keeps, sends):
        self.at, self.name, self.keeps, self.sends = at, name, keeps, sends
        self.total = keeps[0].shape[0]
        self.half = sum(k.shape[1] for k in keeps)
        self.r = self.total // at.n
        self.first = at.c == 0
        self.done = ()

    def step_core(self, *wait):
        if not self.at.fast:
            return
        at = self.at
        with jax.named_scope(self.name + "_core"):
            got = [at.swap_c(after(send, *wait)) for send in self.sends]
            mine = jnp.concatenate([plus(k, g) for k, g in zip(self.keeps, got)], axis=1)
            mine = mine.reshape(4, 2, 2, 2 * self.r, self.half)
            self.low, self.high = mine[:2], mine[2:]
            self.done = tuple(got)

    def step_one(self, *wait):
        if not self.at.fast:
            return
        at = self.at
        with jax.named_scope(self.name + "_one"):
            low, high = after(self.low, *wait), after(self.high, *wait)
            got = at.swap_y(half_at(low, 1 - at.y, 2)), at.swap_x(half_at(high, 1 - at.x, 1))
            self.low = plus(half_at(low, at.y, 2), got[0])
            self.high = plus(half_at(high, at.x, 1), got[1])
            self.done = got

    def step_two(self, *wait):
        if not self.at.fast:
            return
        at = self.at
        with jax.named_scope(self.name + "_two"):
            low, high = after(self.low, *wait), after(self.high, *wait)
            got = at.swap_x(half_at(low, 1 - at.x, 1)), at.swap_y(half_at(high, 1 - at.y, 1))
            low = plus(half_at(low, at.x, 1), got[0])
            high = plus(half_at(high, at.y, 1), got[1])
            self.by_z = jnp.concatenate([low, high])
            self.done = got

    def step_z(self, *wait):
        if not self.at.fast:
            return
        at = self.at
        with jax.named_scope(self.name + "_z"):
            by_z = after(self.by_z, *wait)
            got = [at.turn_z(half_at(by_z, (at.z + by) % 4, 0), by) for by in (1, 2, 3)]
            total = half_at(by_z, at.z, 0).astype(F32) + got[0].astype(F32) + got[1].astype(F32) + got[2].astype(F32)
            self.piece = total.reshape(2, self.r, self.half)
            self.done = tuple(got)

    def step_last(self, *wait):
        at = self.at
        with jax.named_scope(self.name + "_last"):
            if not at.fast:
                keep, send = jnp.concatenate(self.keeps, axis=1), jnp.concatenate(self.sends, axis=1)
                left = jnp.where(self.first, keep, send).astype(F32)
                right = jnp.where(self.first, send, keep).astype(F32)
                return (
                    lax.psum_scatter(left, BOTH, scatter_dimension=0, tiled=True),
                    lax.psum_scatter(right, BOTH, scatter_dimension=0, tiled=True),
                )
            piece = after(self.piece, *wait)
            stays = half_at(piece, at.c, 0)
            got = at.swap_c(half_at(piece, 1 - at.c, 0))
            self.done = (got,)
            return jnp.where(self.first, stays, got), jnp.where(self.first, got, stays)


class Before:
    def __init__(self, at, name, a, reverse):
        self.at, self.name, self.a, self.reverse = at, name, a, reverse
        self.fast = at.fast and a.shape[0] == 2
        self.done = ()

    def step_beside(self):
        if self.fast:
            at = self.at
            with jax.named_scope(self.name + "_beside"):
                self.got = at.swap_x(half_at(self.a, 1 - at.x, 0))
                self.own = half_at(self.a, at.x, 0)
                self.pair = plus(self.own, self.got)
                self.done = (self.got,)

    def step_z(self, *wait):
        if self.fast:
            at = self.at
            with jax.named_scope(self.name + "_z"):
                pair = after(self.pair, *wait)
                got = []
                for by in (1, 2, 3):
                    if self.reverse:
                        pairs = [(d, d - 8 * by) for d in range(8 * by, at.n)]
                    else:
                        pairs = [(d, d + 8 * by) for d in range(at.n - 8 * by)]
                    got.append(lax.ppermute(pair, BOTH, pairs))
                self.done = tuple(got)

    def step_last(self, *wait):
        at, a, reverse = self.at, self.a, self.reverse
        with jax.named_scope(self.name + "_last"):
            if not self.fast:
                everything = lax.all_gather(a, "seq").astype(F32)
                index = jnp.arange(at.seq).reshape((-1,) + (1,) * a.ndim)
                reached = index > at.s if reverse else index < at.s
                return jnp.sum(jnp.where(reached, everything, 0.0), axis=0).astype(BF)
            inner = (at.x == 0) if reverse else (at.x == 1)
            got = [after(g, *wait).astype(F32) for g in self.done]
            self.total = got[0] + got[1] + got[2]
            mine = (self.total + jnp.where(inner, self.got.astype(F32), 0.0)).astype(BF)
            send = (self.total + jnp.where(inner, 0.0, self.own.astype(F32))).astype(BF)
            return ordered(at.x == 0, mine, at.swap_x(send), 0)


class Everywhere:
    def __init__(self, at, a):
        self.at, self.a, self.done = at, a, ()

    def step(self, stride, *wait):
        if self.at.fast:
            with jax.named_scope("everywhere"):
                got = self.at.flip(after(self.a, *wait), stride)
                self.a = self.a + got
                self.done = (got,)

    def step_z(self, *wait):
        at = self.at
        with jax.named_scope("everywhere"):
            if not at.fast:
                return lax.psum(self.a, BOTH)
            a = after(self.a, *wait)
            rel = jnp.stack([a] + [at.turn_z(a, by) for by in (3, 2, 1)])
            by_z = lax.dynamic_slice_in_dim(jnp.concatenate([rel, rel]), (4 - at.z) % 4, 4)
            return (by_z[0] + by_z[1]) + (by_z[2] + by_z[3])


VMEM = pltpu.VMEM
SCALAR = pl.BlockSpec(memory_space=pltpu.SMEM)
WHOLE = pl.BlockSpec(memory_space=VMEM)


def params(mib):
    return pltpu.CompilerParams(vmem_limit_bytes=60 * 2**20)


def cost(micros):
    return pl.CostEstimate(flops=int(micros * 1e9), bytes_accessed=int(micros * 1e6), transcendentals=0)


def tdot(a, b):
    return lax.dot_general(a, b, (((0,), (0,)), ((), ())), preferred_element_type=F32)


def dot_t(a, b):
    return lax.dot_general(a, b, (((1,), (1,)), ((), ())), preferred_element_type=F32)


def dot(a, b):
    return jnp.dot(a, b, preferred_element_type=F32)


def parts(a):
    high = a.astype(BF)
    return high, (a - high.astype(F32)).astype(BF)


def left_lanes(shape):
    return lax.broadcasted_iota(jnp.int32, shape, len(shape) - 1) % 128 < 64


def two_heads(a):
    first = left_lanes(a.shape)
    wide = a.astype(F32)
    return jnp.concatenate(
        [jnp.where(first, wide, 0.0), jnp.where(first, 0.0, wide)], axis=0
    ).astype(BF)


def fold(a):
    half = a.shape[0] // 2
    return jnp.where(left_lanes((half, a.shape[1])), a[:half], a[half:])


def head_ones():
    row = lax.broadcasted_iota(jnp.int32, (128, 128), 0) // 64
    col = lax.broadcasted_iota(jnp.int32, (128, 128), 1) // 64
    return jnp.where(row == col, 1.0, 0.0).astype(BF)


def head_sums(a, ones):
    high, low = parts(a)
    return dot(high, ones) + dot(low, ones)


def features(s, g_high, g_low):
    high, low = parts(jnp.concatenate([s, s * s], axis=1))
    return jnp.exp(dot(high, g_high) + dot(high, g_low) + dot(low, g_high)) * 0.125


def features_back(t, s, g_high, g_low, ones, scale):
    high, low = parts(t)
    f_high, f_low = g_high[:128], g_low[:128]
    back = dot_t(high, f_high) + dot_t(high, f_low) + dot_t(low, f_high)
    return ((back - s * (dot(high, ones) + dot(low, ones))) * scale).astype(BF)


def lanes(p):
    return slice(p * 128, (p + 1) * 128)


def key_kernel(c_ref, tok, mine, other, gh, gl, s_out, phi_out, feat_out, v_out, state_out, vec_out):
    first = c_ref[0] == 0
    pairs, block = gh.shape[0], 128
    hw = pairs * 64
    eye = jnp.where(
        lax.broadcasted_iota(jnp.int32, (128, 128), 0) == lax.broadcasted_iota(jnp.int32, (128, 128), 1), 1.0, 0.0
    ).astype(BF)
    vecs = dot_t(eye, mine[:, 3 * hw :])[:16]
    vec_out[...] = vecs
    a = dot(tok[...], mine[:, hw : 3 * hw])
    b = dot(tok[...], other[:, hw : 3 * hw])
    left, right = jnp.where(first, a, b), jnp.where(first, b, a)
    scale = 64 ** (-0.25)
    for p in range(pairs):
        half, at = (left, p * 128) if p < pairs // 2 else (right, p * 128 - hw)
        s = (half[:, at : at + 128] + vecs[1:2, lanes(p)]) * scale
        v = (half[:, hw + at : hw + at + 128] + vecs[2:3, lanes(p)]).astype(BF)
        phi = features(s, gh[p], gl[p])
        k = phi.astype(BF)
        s_out[:, lanes(p)] = s
        phi_out[:, lanes(p)] = phi
        feat_out[:, lanes(p)] = k
        v_out[:, lanes(p)] = v
        for r in range(tok.shape[0] // block):
            rows = slice(r * block, (r + 1) * block)
            state_out[r, :64, lanes(p)] = fold(tdot(k[rows], v[rows])).astype(BF)
            total = jnp.sum(k[rows].astype(F32), axis=0, keepdims=True)
            state_out[r, 64:, lanes(p)] = jnp.broadcast_to(total, (16, 128)).astype(BF)


def query_kernel(c_ref, tok, mine, other, vec, gh, gl, s_out, phi_out, feat_out):
    first = c_ref[0] == 0
    pairs = gh.shape[0]
    hw = pairs * 64
    a, b = dot(tok[...], mine[:, :hw]), dot(tok[...], other[:, :hw])
    left, right = jnp.where(first, a, b), jnp.where(first, b, a)
    for p in range(pairs):
        half, at = (left, p * 128) if p < pairs // 2 else (right, p * 128 - hw)
        s = (half[:, at : at + 128] + vec[0:1, lanes(p)]) * 64 ** (-0.25)
        phi = features(s, gh[p], gl[p])
        s_out[:, lanes(p)] = s
        phi_out[:, lanes(p)] = phi
        feat_out[:, lanes(p)] = phi.astype(BF)


def halo_kernel(c_ref, halo, mine, other, vec, gh, gl, hk_out, hv_out):
    first, inner = c_ref[0] == 0, c_ref[1] > 0
    pairs = gh.shape[0]
    hw = pairs * 64
    a, b = dot(halo[...], mine[:, hw : 3 * hw]), dot(halo[...], other[:, hw : 3 * hw])
    left, right = jnp.where(first, a, b), jnp.where(first, b, a)
    for p in range(pairs):
        half, at = (left, p * 128) if p < pairs // 2 else (right, p * 128 - hw)
        s = (half[:, at : at + 128] + vec[1:2, lanes(p)]) * 64 ** (-0.25)
        v = half[:, hw + at : hw + at + 128] + vec[2:3, lanes(p)]
        hk_out[:, lanes(p)] = jnp.where(inner, features(s, gh[p], gl[p]), 0.0).astype(BF)
        hv_out[:, lanes(p)] = jnp.where(inner, v, 0.0).astype(BF)


def window_weights(base):
    turned = pltpu.roll(jnp.broadcast_to(base, (128, 256)), 0, 1, stride=1, stride_axis=0)
    row = lax.broadcasted_iota(jnp.int32, (128, 256), 0)
    col = lax.broadcasted_iota(jnp.int32, (128, 256), 1)
    return jnp.where(col > row + 128, 0.0, turned - jnp.where(col < 128, base[:, 255:256], 0.0))


def pair_at(step, c, pairs):
    return (step + (pairs // 2) * (1 - c)) % pairs


def block_diagonal(packed):
    return two_heads(packed)


def attention_kernel(q, k, v, hk, hv, table, state, far, context_out, turned_out, ratio_out, denom_out):
    ones = head_ones()
    wmat = jnp.concatenate([window_weights(table[0, 0:1]), window_weights(table[0, 1:2])], axis=0)
    far_row = far[0:1]
    for r in range(q.shape[0] // 128):
        rows = slice(r * 128, (r + 1) * 128)
        qr = q[rows]
        kw = jnp.concatenate([hk[rows], k[rows]], axis=0)
        vw = jnp.concatenate([hv[rows], v[rows]], axis=0)
        weighted = dot_t(two_heads(qr), kw) * wmat
        numer = fold(dot(weighted.astype(BF), vw))
        near = jnp.sum(weighted, axis=1, keepdims=True)
        near = fold(jnp.broadcast_to(near, (256, 128)))
        bd = block_diagonal(state[r, :64])
        total = state[r, 64:80].astype(F32)[0:1]
        numer = numer + far_row * dot(qr, bd)
        denom = near + far_row * head_sums(qr.astype(F32) * total, ones)
        ratio = numer / denom
        context_out[rows] = ratio.astype(BF)
        turned_out[:, rows] = ratio.T.astype(BF)
        ratio_out[rows] = ratio
        denom_out[rows] = denom


def normed(x):
    centred = x - jnp.mean(x, axis=-1, keepdims=True)
    rstd = lax.rsqrt(jnp.mean(centred * centred, axis=-1, keepdims=True) + EPS)
    return centred * rstd, rstd


def norm_back(dy, xhat, rstd, gain):
    d = dy * gain
    return rstd * (
        d - jnp.mean(d, axis=-1, keepdims=True) - xhat * jnp.mean(d * xhat, axis=-1, keepdims=True)
    )


def col_sums(a):
    return jnp.sum(a, axis=0, keepdims=True)


def forward_kernel(
    context, tok, cot, vec, bu, wu_hbm, wo_hbm, rest_hbm,
    out, dlower_out, du_out, xhat_out, rstd_out, sums_out, du_sums_out, down_hbm, up_hbm,
    wu, wo, wd, gp, grads, in_sems, out_sems,
):
    count, width, step = wu.shape
    loads = [pltpu.make_async_copy(wo_hbm, wo, in_sems.at[2 * count])]
    for i in range(count):
        loads.append(pltpu.make_async_copy(wu_hbm.at[i], wu.at[i], in_sems.at[i]))
        wd_block = rest_hbm.at[pl.ds(i * step, step), pl.ds(0, width)]
        loads.append(pltpu.make_async_copy(wd_block, wd.at[i], in_sems.at[count + i]))
    for load in loads:
        load.start()
    loads[0].wait()
    attn = jnp.concatenate([dot(context[...], wo[i]) for i in range(count)], axis=1)
    xhat, rstd = normed(tok[...].astype(F32) + attn + vec[3:4])
    hidden = xhat * vec[4:5] + vec[5:6]
    xhat_out[...] = xhat
    rstd_out[...] = jnp.broadcast_to(rstd, rstd_out.shape)
    h_low = hidden.astype(BF)
    lower = hidden + vec[6:7]
    actives = []
    for i in range(count):
        cols = slice(i * step, (i + 1) * step)
        loads[1 + 2 * i].wait()
        upper = dot(h_low, wu[i]) + bu[:, cols]
        cdf = 0.5 * (1.0 + lax.erf(upper * 2.0 ** (-0.5)))
        pdf = jnp.exp(-0.5 * upper * upper) * (2.0 * math.pi) ** (-0.5)
        gp[:, cols] = (cdf + upper * pdf).astype(BF)
        actives.append((upper * cdf).astype(BF))
        loads[2 + 2 * i].wait()
        lower = lower + dot(actives[-1], wd[i])
    xhat2, rstd2 = normed(lower)
    gain2 = vec[7:8]
    out[...] = xhat2 * gain2 + vec[8:9]
    dy = cot[...].astype(F32)
    d_lower = norm_back(dy, xhat2, rstd2, gain2)
    dlower_out[...] = d_lower
    d_low = d_lower.astype(BF)
    sums_out[0:1] = col_sums(d_low.astype(F32))
    sums_out[1:2] = col_sums(dy * xhat2)
    sums_out[2:3] = col_sums(dy)
    stores = []
    for i in range(count):
        cols = slice(i * step, (i + 1) * step)
        d_upper = (dot_t(d_low, wd[i]) * gp[:, cols].astype(F32)).astype(BF)
        du_out[:, cols] = d_upper
        du_sums_out[:, cols] = jnp.broadcast_to(col_sums(d_upper.astype(F32)), (8, step))
        grads[2 * i] = tdot(h_low, d_upper).astype(BF)
        stores.append(pltpu.make_async_copy(grads.at[2 * i], up_hbm.at[i], out_sems.at[2 * i]))
        stores[-1].start()
        grads[2 * i + 1] = tdot(actives[i], d_low).astype(BF)
        block = down_hbm.at[pl.ds(i * step, step), pl.ds(0, width)]
        stores.append(pltpu.make_async_copy(grads.at[2 * i + 1], block, out_sems.at[2 * i + 1]))
        stores[-1].start()
    for store in stores:
        store.wait()


def middle_kernel(
    dlower, du, xhat, rstd, wu_hbm, wo, vec, ratio, denom, q, state, far,
    dresid_out, dattn_out, dn_out, later_out, sums_out, near_out,
    wu, sems,
):
    hw = dlower.shape[1] // 2
    d_hidden = dlower[...]
    step = wu.shape[2]
    loads = [pltpu.make_async_copy(wu_hbm.at[i], wu.at[i], sems.at[i]) for i in range(wu.shape[0])]
    for load in loads:
        load.start()
    for i in range(wu.shape[0]):
        loads[i].wait()
        d_hidden = d_hidden + dot_t(du[:, i * step : (i + 1) * step], wu[i])
    xh = xhat[...]
    d_resid = norm_back(d_hidden, xh, rstd[:, 0:1], vec[4:5])
    dresid_out[...] = d_resid
    d_attn = d_resid.astype(BF)
    dattn_out[...] = d_attn
    sums_out[0:1] = col_sums(d_attn.astype(F32))
    sums_out[1:2] = col_sums(d_hidden * xh)
    sums_out[2:3] = col_sums(d_hidden)
    step = wo.shape[2]
    d_context = sum(dot_t(d_resid[:, i * step : (i + 1) * step].astype(BF), wo[i]) for i in range(wo.shape[0]))
    ones = head_ones()
    width = 2 * hw
    pick = jnp.where(
        lax.broadcasted_iota(jnp.int32, (width, 128), 0) == 64 * lax.broadcasted_iota(jnp.int32, (width, 128), 1), 1.0, 0.0
    ).astype(BF)
    all_denoms = []
    for p in range(width // 128):
        dc = d_context[:, lanes(p)]
        inverse = 1.0 / denom[:, lanes(p)]
        dn = (dc * inverse).astype(BF)
        dd = (-head_sums(dc * ratio[:, lanes(p)], ones) * inverse).astype(BF)
        dn_out[:, lanes(p)] = dn
        all_denoms.append(dd)
        near = jnp.zeros((1, 128), F32)
        for r in range(dlower.shape[0] // 128):
            rows = slice(r * 128, (r + 1) * 128)
            qr = q[rows, lanes(p)]
            packed = fold(tdot(qr, dn[rows]))
            total = col_sums(qr.astype(F32) * dd[rows].astype(F32))
            far_row = far[0:1, lanes(p)]
            later_out[r, :64, lanes(p)] = (far_row * packed).astype(BF)
            later_out[r, 64:, lanes(p)] = jnp.broadcast_to(far_row * total, (16, 128)).astype(BF)
            held = state[r, :, lanes(p)].astype(F32)
            near = near + col_sums(held[:64] * packed) + held[64:65] * total
        near_out[:, lanes(p)] = jnp.broadcast_to(near, (8, 128))
    dn_out[:, width:] = dot(jnp.concatenate(all_denoms, axis=1), pick).astype(BF)


def spread(dn, p):
    lane = lax.broadcasted_iota(jnp.int32, dn.shape, 1)
    wide = dn.astype(F32)
    return [jnp.sum(jnp.where(lane == 2 * p + h, wide, 0.0), axis=1, keepdims=True) for h in (0, 1)]


def query_back_kernel(
    c_ref, tok, context, dattn, q, k, v, hk, hv, dn, dd, table, state, far, phi, s, gh, gl, near,
    dq_out, keep_out, send_out, pos_out, sums_out,
):
    steps = pl.num_programs(0)
    p = pair_at(pl.program_id(0), c_ref[0], steps)
    ones = head_ones()
    wmat = jnp.concatenate([window_weights(table[0, 0:1]), window_weights(table[0, 1:2])], axis=0)
    far_row = far[0:1]
    first = left_lanes((128, 128))
    pieces = jnp.zeros((256, 256), F32)
    grads = []
    for r in range(q.shape[0] // 128):
        rows = slice(r * 128, (r + 1) * 128)
        kw = jnp.concatenate([hk[rows], k[rows]], axis=0)
        vw = jnp.concatenate([hv[rows], v[rows]], axis=0)
        scores = dot_t(two_heads(q[rows]), kw)
        d0, d1 = spread(dd[rows], p)
        dnr = dn[rows]
        dw = dot_t(two_heads(dnr), vw) + jnp.concatenate([d0, d1], axis=0)
        pieces = pieces + dw * scores
        ds = (dw * wmat).astype(BF)
        bd = block_diagonal(state[r, :64])
        total = state[r, 64:80].astype(F32)[0:1]
        dq = fold(dot(ds, kw)) + far_row * (dot_t(dnr, bd) + jnp.where(first, d0, d1) * total)
        grads.append(
            features_back(dq * phi[rows], s[rows], gh[0], gl[0], ones, 64 ** (-0.25))
        )
    dq = jnp.concatenate(grads, axis=0)
    dq_out[...] = dq
    sums_out[...] = jnp.broadcast_to(col_sums(dq.astype(F32)), sums_out.shape)
    grad = jnp.concatenate([dot(tok[...], dq), dot(context[...], dattn[...])], axis=1).astype(BF)
    place_half(grad, keep_out, send_out)
    row = lax.broadcasted_iota(jnp.int32, (256, 256), 0)
    col = lax.broadcasted_iota(jnp.int32, (256, 256), 1)
    mirror = jnp.where(row + col == 255, 1.0, 0.0).astype(BF)
    high, low = parts(jnp.where(col <= row % 128 + 128, pieces, 0.0))
    mirrored = dot(high, mirror) + dot(low, mirror)
    lane = lax.broadcasted_iota(jnp.int32, (1, 256), 1)
    for h in (0, 1):
        rows = slice(h * 128, (h + 1) * 128)
        by_distance = col_sums(pltpu.roll(mirrored[rows], 129, 1, stride=1, stride_axis=0))
        plain = col_sums(pieces[rows])
        apart = jnp.where(lane >= 128, by_distance, 0.0) - jnp.where(lane < 128, plain, 0.0)
        state_part = jnp.where(lane[:, :128] // 64 == h, near[0:1], 0.0)
        far_sum = jnp.sum(apart, axis=1, keepdims=True) + jnp.sum(state_part, axis=1, keepdims=True)
        pos_out[0, h : h + 1] = jnp.where(lane < 128, by_distance, far_sum)


def place_half(grad, keep_out, send_out):
    early = pl.program_id(0) < pl.num_programs(0) // 2

    @pl.when(early)
    def _():
        send_out[...] = grad

    @pl.when(jnp.logical_not(early))
    def _():
        keep_out[...] = grad


def key_back_kernel(
    c_ref, tok, q, k, v, dn, dd, qn, dnn, ddn, table, later, phi, s, gh, gl, rows_in,
    dk_out, dv_out, keep_out, send_out, small_out,
):
    p = pair_at(pl.program_id(0), c_ref[0], pl.num_programs(0))
    ones = head_ones()
    first, second = window_weights(table[0, 0:1]), window_weights(table[0, 1:2])
    tables = jnp.concatenate([first[:, 128:], second[:, 128:], first[:, :128], second[:, :128]], axis=0)
    dks, dvs = [], []
    for r in range(q.shape[0] // 128):
        rows = slice(r * 128, (r + 1) * 128)
        kr, vr = k[rows], v[rows]
        q4 = jnp.concatenate([two_heads(q[rows]), two_heads(qn[rows])], axis=0)
        dn4 = jnp.concatenate([two_heads(dn[rows]), two_heads(dnn[rows])], axis=0)
        dd4 = jnp.concatenate(spread(dd[rows], p) + spread(ddn[rows], p), axis=0)
        w = (dot_t(q4, kr) * tables).astype(BF)
        ds = ((dot_t(dn4, vr) + dd4) * tables).astype(BF)
        bd = block_diagonal(later[r, :64])
        total = later[r, 64:80].astype(F32)[0:1]
        dk = tdot(ds, q4) + dot_t(vr, bd) + total
        dvs.append((tdot(w, dn4) + dot(kr, bd)).astype(BF))
        dks.append(features_back(dk * phi[rows], s[rows], gh[0], gl[0], ones, 64 ** (-0.25)))
    dk, dv = jnp.concatenate(dks, axis=0), jnp.concatenate(dvs, axis=0)
    dk_out[...] = dk
    dv_out[...] = dv
    place_half(jnp.concatenate([dot(tok[...], dk), dot(tok[...], dv)], axis=1).astype(BF), keep_out, send_out)
    row = lax.broadcasted_iota(jnp.int32, (16, 128), 0)
    lane = lax.broadcasted_iota(jnp.int32, (16, 128), 1)
    late = jnp.where(row == 1, col_sums(dk.astype(F32)), 0.0) + jnp.where(row == 2, col_sums(dv.astype(F32)), 0.0)
    small_out[...] = tdot((rows_in[...] + late).astype(BF), jnp.where(row == lane, 1.0, 0.0).astype(BF)).astype(BF)


def tokens_kernel(c_ref, dresid, dq, dk, dv, mine, other, out):
    first = c_ref[0] == 0
    hw = dq.shape[1] // 2
    total = dresid[...]
    for i, d in enumerate((dq, dk, dv)):
        wide = d[...].astype(F32)
        a = jnp.where(first, wide[:, :hw], wide[:, hw:]).astype(BF)
        b = jnp.where(first, wide[:, hw:], wide[:, :hw]).astype(BF)
        cols = slice(i * hw, (i + 1) * hw)
        total = total + dot_t(a, mine[:, cols]) + dot_t(b, other[:, cols])
    out[...] = total


def unpack_kernel(packed, down_out, up_out):
    own, width = up_out.shape[0], down_out.shape[1]
    step = packed.shape[1] - width
    wide = packed[...].astype(F32)
    down_out[...] = wide[:, :width]
    for i in range(packed.shape[0] // own):
        up_out[:, i * step : (i + 1) * step] = wide[i * own : (i + 1) * own, width:]


def feature_blocks(matrix):
    heads, size, feats = matrix.shape
    zero = jnp.zeros((heads // 2, size, feats), F32)
    even, odd = matrix[0::2], matrix[1::2]
    half = jnp.full(zero.shape, -0.5, F32)
    blocks = jnp.concatenate(
        [
            jnp.concatenate([even, zero], axis=2),
            jnp.concatenate([zero, odd], axis=2),
            jnp.concatenate([half, zero], axis=2),
            jnp.concatenate([zero, half], axis=2),
        ],
        axis=1,
    )
    high = lax.reduce_precision(blocks, 8, 7)
    return high.astype(BF), (blocks - high).astype(BF)


def on_device(
    tokens,
    query_weight,
    query_bias,
    key_weight,
    key_bias,
    value_weight,
    value_bias,
    output_weight,
    output_bias,
    first_gain,
    first_shift,
    up_weight,
    up_bias,
    down_weight,
    down_bias,
    second_gain,
    second_shift,
    position_bias,
    feature_matrix,
    cotangent,
):
    at = Place()
    rows, block, width = tokens.shape
    heads, size, feats = feature_matrix.shape
    window = position_bias.shape[1] - 1
    pairs = heads // 2
    n = rows * block
    hw = width // 2
    ff = up_weight.shape[1]
    hf = ff // 2
    own = query_weight.shape[0]
    up_own = up_bias.shape[0] // own
    tok = tokens.reshape(n, width)
    cot = cotangent.reshape(n, width)
    flags = jnp.stack([at.c, at.s]).astype(jnp.int32)

    def arr(shape, kind):
        return jax.ShapeDtypeStruct(shape, kind)

    halo_tok = at.along(tok, 1)
    tok_t = tok.T

    vectors = (
        query_bias, key_bias, value_bias, output_bias, first_gain, first_shift,
        down_bias, second_gain, second_shift,
    )
    count = len(vectors)
    small = jnp.concatenate(vectors + (up_bias,)).reshape(count + up_own, own).T
    small = jnp.pad(small, ((0, 0), (0, 128 - small.shape[1])))
    slices = down_weight.shape[0] // own
    step, wo_step = ff // slices, width // slices

    def stacked(a):
        return jnp.concatenate(jnp.split(a, slices, axis=1), axis=0)

    rest = lax.all_gather(
        jnp.concatenate([down_weight, stacked(up_weight), stacked(output_weight)], axis=1), BOTH, axis=0, tiled=True
    )
    g1 = Gather(
        at,
        "qkv",
        jnp.concatenate([query_weight[:, :hw], key_weight[:, :hw], value_weight[:, :hw]], axis=1),
        jnp.concatenate([query_weight[:, hw:], key_weight[:, hw:], value_weight[:, hw:]], axis=1),
        small,
    )
    exp_bias = jnp.exp(position_bias)
    table = jnp.concatenate(
        [exp_bias[:, ::-1], jnp.broadcast_to(exp_bias[:, window:], (heads, block - 1))], axis=1
    ).reshape(pairs, 2, window + block)
    table = jnp.pad(table, ((0, 0), (0, 6), (0, 0)))
    far = jnp.broadcast_to(jnp.repeat(exp_bias[:, window], size)[None], (8, width))
    gh, gl = feature_blocks(feature_matrix)

    g1.step_core()
    g1.step_z()
    g1.step_one()
    g1.step_two()
    m1, o1 = g1.step_last(table, far, gh, gl, tok_t)

    wide32, wide16 = arr((n, width), F32), arr((n, width), BF)
    sums = arr((rows, 80, width), BF)
    sk, k_phi, k, v, local, vec = pl.pallas_call(
        key_kernel,
        out_shape=(wide32, wide32, wide16, wide16, sums, arr((16, width), F32)),
        in_specs=[SCALAR] + [WHOLE] * 5,
        out_specs=(WHOLE,) * 6,
        compiler_params=params(48),
        cost_estimate=cost(5),
        name="keys",
    )(flags, tok, m1, o1, gh, gl)
    scan = Before(at, "before", local, False)
    scan.step_beside()
    sq, q_phi, q = pl.pallas_call(
        query_kernel,
        out_shape=(wide32, wide32, wide16),
        in_specs=[SCALAR] + [WHOLE] * 6,
        out_specs=(WHOLE,) * 3,
        compiler_params=params(48),
        cost_estimate=cost(3),
        name="queries",
    )(flags, tok, m1, o1, vec, gh, gl)
    scan.step_z(q)
    hk, hv = pl.pallas_call(
        halo_kernel,
        out_shape=(wide16, wide16),
        in_specs=[SCALAR] + [WHOLE] * 6,
        out_specs=(WHOLE,) * 2,
        compiler_params=params(48),
        cost_estimate=cost(2),
        name="halo",
    )(flags, after(halo_tok, *scan.done), m1, o1, vec, gh, gl)
    q_next = at.along(q, -1)
    before = scan.step_last(hk, q_next)
    b_u = m1[:, 3 * hw + count : 3 * hw + count + up_own].reshape(at.n, own, up_own)
    b_u = jnp.swapaxes(after(b_u, hk), 1, 2).reshape(1, ff).astype(F32)

    def columns(height=n):
        return pl.BlockSpec((height, 128), lambda p, *_: (0, p))

    table_spec = pl.BlockSpec((1, 8, window + block), lambda p, *_: (p, 0, 0))
    sums_spec = pl.BlockSpec((rows, 80, 128), lambda p, *_: (0, 0, p))
    g_spec = pl.BlockSpec((1, 256, 128), lambda p, *_: (p, 0, 0))
    tok_spec = pl.BlockSpec((width, n), lambda p, *_: (0, 0))
    dd_spec = pl.BlockSpec((n, 128), lambda p, *_: (0, pairs))
    context, context_t, ratio, denom = pl.pallas_call(
        attention_kernel,
        grid=(pairs,),
        out_shape=(wide16, arr((width, n), BF), wide32, wide32),
        in_specs=[columns()] * 5 + [table_spec, sums_spec, columns(8)],
        out_specs=(columns(), pl.BlockSpec((128, n), lambda p, *_: (p, 0)), columns(), columns()),
        compiler_params=params(32),
        cost_estimate=cost(5),
        name="attention",
    )(q, k, v, hk, hv, table, before, far)

    split = rest.reshape(at.n, slices, own, rest.shape[1])
    wu = jnp.swapaxes(split[..., width : width + step], 0, 1).reshape(slices, width, step)
    wo = jnp.swapaxes(split[..., width + step :], 0, 1).reshape(slices, width, wo_step)
    away = pl.BlockSpec(memory_space=pl.ANY)
    out, d_lower, du, xhat, rstd, sums3, du_sums, g_down, g_up = pl.pallas_call(
        forward_kernel,
        out_shape=(
            wide32, wide32, arr((n, ff), BF), wide32, arr((n, 128), F32), arr((8, width), F32), arr((8, ff), F32),
            arr((ff, width + step), BF), arr((slices, width, step), BF),
        ),
        in_specs=[WHOLE] * 5 + [away] * 3,
        out_specs=(WHOLE,) * 7 + (away,) * 2,
        scratch_shapes=[
            VMEM((slices, width, step), BF),
            VMEM((slices, width, wo_step), BF),
            VMEM((slices, step, width), BF),
            VMEM((n, ff), BF),
            VMEM((2 * slices, width, step), BF),
            pltpu.SemaphoreType.DMA((2 * slices + 1,)),
            pltpu.SemaphoreType.DMA((2 * slices,)),
        ],
        compiler_params=params(56),
        cost_estimate=cost(18),
        name="forward",
    )(context, tok, cot, vec, b_u, wu, wo, rest)
    g_up = jnp.swapaxes(g_up.reshape(slices, at.n, own, step), 0, 1).reshape(ff, step)
    g_rest = lax.dynamic_update_slice(g_down, g_up, (0, width))
    s_rest = lax.psum_scatter(g_rest, BOTH, scatter_dimension=0, tiled=True)
    if own % 8 == 0:
        s_d, s_u = pl.pallas_call(
            unpack_kernel,
            out_shape=(arr((slices * own, width), F32), arr((own, ff), F32)),
            in_specs=[WHOLE],
            out_specs=(WHOLE,) * 2,
            compiler_params=params(48),
            cost_estimate=cost(1),
            name="unpack",
        )(s_rest)
    else:
        s_d = s_rest[:, :width].astype(F32)
        s_u = jnp.concatenate(jnp.split(s_rest[:, width:].astype(F32), slices, axis=0), axis=1)
    d_resid, d_attn, dn, local, sums2, near = pl.pallas_call(
        middle_kernel,
        out_shape=(wide32, wide16, arr((n, width + 128), BF), sums, arr((8, width), F32), arr((8, width), F32)),
        in_specs=[WHOLE] * 4 + [away] + [WHOLE] * 7,
        out_specs=(WHOLE,) * 6,
        scratch_shapes=[VMEM((slices, width, step), BF), pltpu.SemaphoreType.DMA((slices,))],
        compiler_params=params(48),
        cost_estimate=cost(7),
        name="middle",
    )(after(d_lower, g_rest), du, xhat, rstd, wu, wo, vec, ratio, denom, q, before, far)
    scan = Before(at, "later", local, True)
    scan.step_beside()
    dn_next = at.along(dn, -1)

    def turned(p, c):
        return pair_at(p, c[0], pairs)

    cols = pl.BlockSpec((n, 128), lambda p, c: (0, turned(p, c)))
    cols8 = pl.BlockSpec((8, 128), lambda p, c: (0, turned(p, c)))
    by_pair = pl.BlockSpec((1, 8, window + block), lambda p, c: (turned(p, c), 0, 0))
    sums_by_pair = pl.BlockSpec((rows, 80, 128), lambda p, c: (0, 0, turned(p, c)))
    g_by_pair = pl.BlockSpec((1, 256, 128), lambda p, c: (turned(p, c), 0, 0))
    kept = pl.BlockSpec((width, 256), lambda p, c: (0, jnp.maximum(p - pairs // 2, 0)))
    sent = pl.BlockSpec((width, 256), lambda p, c: (0, jnp.minimum(p, pairs // 2 - 1)))
    half = arr((width, 2 * hw), BF)
    dq, keep1, send1, pos, sums_q = pl.pallas_call(
        query_back_kernel,
        grid_spec=pltpu.PrefetchScalarGridSpec(
            num_scalar_prefetch=1,
            grid=(pairs,),
            in_specs=[tok_spec] * 2 + [cols] * 7 + [dd_spec, by_pair, sums_by_pair, cols8]
            + [cols] * 2 + [g_by_pair] * 2 + [cols8],
            out_specs=(cols, kept, sent, by_pair, cols8),
        ),
        out_shape=(wide16, half, half, arr((pairs, 8, 256), F32), arr((8, width), F32)),
        compiler_params=params(32),
        cost_estimate=cost(11),
        name="query_back",
    )(flags, after(tok_t, *scan.done), context_t, d_attn, q, k, v, hk, hv, dn, dn, table, before, far, q_phi, sq, gh, gl, near)
    scan.step_z()
    later = scan.step_last(dq, dn_next)
    everywhere = Everywhere(at, exp_bias * pos[:, :2, : window + 1].reshape(heads, window + 1))
    everywhere.step(1)
    du = du_sums[0].reshape(at.n, up_own, own)
    du = jnp.swapaxes(du, 0, 1).reshape(up_own, width)
    nil = jnp.zeros((2, width), F32)
    early = jnp.concatenate([sums_q[:1], nil, sums2[:3], sums3[:3], du], axis=0)
    early = jnp.pad(early, ((0, 16 - early.shape[0]), (0, 0)))
    dk, dv, keep0, send0, small = pl.pallas_call(
        key_back_kernel,
        grid_spec=pltpu.PrefetchScalarGridSpec(
            num_scalar_prefetch=1,
            grid=(pairs,),
            in_specs=[tok_spec] + [cols] * 4 + [dd_spec] + [cols] * 2
            + [dd_spec, by_pair, sums_by_pair] + [cols] * 2 + [g_by_pair] * 2
            + [pl.BlockSpec((16, 128), lambda p, c: (0, turned(p, c)))],
            out_specs=(cols, cols, kept, sent, pl.BlockSpec((128, 128), lambda p, c: (turned(p, c), 0))),
        ),
        out_shape=(wide16, wide16, half, half, arr((width, 128), BF)),
        compiler_params=params(32),
        cost_estimate=cost(12),
        name="key_back",
    )(flags, after(tok_t, *everywhere.done), q, k, v, dn, dn, q_next, dn_next, dn_next, table, later, k_phi, sk, gh, gl, early)

    r0 = Scatter(at, "d_qkv", (keep1, keep0, small), (send1, send0, small))
    r0.step_core()
    everywhere.step(2, dk)
    r0.step_one(*everywhere.done)
    everywhere.step(4, *r0.done)
    r0.step_two(*everywhere.done)
    two0 = r0.done
    r0.step_z()
    position_grad = everywhere.step_z(*two0)
    s_qkv = r0.step_last()
    d_tokens = pl.pallas_call(
        tokens_kernel,
        out_shape=wide32,
        in_specs=[SCALAR] + [WHOLE] * 6,
        out_specs=WHOLE,
        compiler_params=params(40),
        cost_estimate=cost(3),
        name="tokens",
    )(flags, d_resid, dq, dk, dv, m1, o1)

    def woven(pair, at):
        return jnp.concatenate(
            [half[:, at + p * 256 : at + p * 256 + 128] for half in pair for p in range(pairs // 2)], axis=1
        )

    s_small = s_qkv[0][:, 4 * hw :]
    bq, bk, bv, bo, sg1, ss1, bd, sg2, ss2 = [s_small[:, i] for i in range(count)]
    bu = s_small[:, count : count + up_own].T.reshape(-1)
    return (
        out.reshape(rows, block, width),
        d_tokens.reshape(rows, block, width),
        woven(s_qkv, 0),
        bq,
        woven(s_qkv, 2 * hw),
        bk,
        woven(s_qkv, 2 * hw + 128),
        bv,
        woven(s_qkv, 128),
        bo,
        sg1,
        ss1,
        s_u,
        bu,
        s_d,
        bd,
        sg2,
        ss2,
        position_grad,
    )


def solution(mesh):
    matrix, vector, split = P(BOTH, None), P(BOTH), P("rows", "seq", None)
    return jax.shard_map(
        on_device,
        mesh=mesh,
        in_specs=(split,)
        + (matrix, vector) * 4
        + (vector, vector)
        + (matrix, vector) * 2
        + (vector, vector)
        + (P(), P(), split),
        out_specs=(split, split)
        + (matrix, vector) * 4
        + (vector, vector)
        + (matrix, vector) * 2
        + (vector, vector)
        + (P(),),
        check_vma=False,
    )
```

```python
import functools
import math

import jax
import jax.numpy as jnp
from jax import lax
from jax.experimental import pallas as pl
from jax.experimental.pallas import tpu as pltpu
from jax.sharding import PartitionSpec as P

BOTH = ("seq", "rows")
EPS = 1e-06
BF = jnp.bfloat16
F32 = jnp.float32


class Place:
    def __init__(self):
        self.seq = lax.axis_size("seq")
        self.rows = lax.axis_size("rows")
        self.n = self.seq * self.rows
        self.fast = self.seq == 8 and self.rows == 4
        me = lax.axis_index(BOTH)
        self.c = me % 2
        self.y = (me // 2) % 2
        self.x = (me // 4) % 2
        self.z = me // 8
        self.s = lax.axis_index("seq")

    def flip(self, a, stride):
        return lax.ppermute(a, BOTH, [(d, d ^ stride) for d in range(self.n)])

    def swap_c(self, a):
        return self.flip(a, 1)

    def swap_y(self, a):
        return self.flip(a, 2)

    def swap_x(self, a):
        return self.flip(a, 4)

    def turn_z(self, a, by):
        return lax.ppermute(a, BOTH, [(d, (d + 8 * by) % self.n) for d in range(self.n)])

    def along(self, a, by):
        pairs = [(i, i + by) for i in range(self.seq) if 0 <= i + by < self.seq]
        return lax.ppermute(a, "seq", pairs)


def after(a, *others):
    return lax.optimization_barrier((a, others))[0]


def ordered(first, mine, other, axis):
    return jnp.where(
        first, jnp.stack([mine, other], axis=axis), jnp.stack([other, mine], axis=axis)
    )


class Gather:
    def __init__(self, at, name, left, right, small):
        self.at, self.name = at, name
        self.r, self.half = left.shape
        self.first = at.c == 0
        self.left, self.right, self.small = left, right, small
        self.done = ()

    def step_core(self, *wait):
        if not self.at.fast:
            return
        with jax.named_scope(self.name + "_core"):
            got = self.at.swap_c(after(jnp.where(self.first, self.right, self.left), *wait))
            kept = jnp.where(self.first, self.left, self.right)
            piece = ordered(self.first, kept, got, 0)
            mine = after(self.small, piece)
            small = ordered(self.first, mine, self.at.swap_c(mine), 0)
            self.half += self.small.shape[1]
            self.piece = jnp.concatenate([piece, small], axis=2).reshape(2 * self.r, self.half)
            self.done = (got,)

    def step_z(self, *wait):
        if not self.at.fast:
            return
        at = self.at
        with jax.named_scope(self.name + "_z"):
            piece = after(self.piece, *wait)
            turned = [at.turn_z(piece, by) for by in (1, 2, 3)]
            rel = jnp.stack([piece, turned[2], turned[1], turned[0]])
            by_z = lax.dynamic_slice_in_dim(jnp.concatenate([rel, rel]), (4 - at.z) % 4, 4)
            self.low, self.high = by_z[:2], by_z[2:]
            self.done = tuple(turned)

    def step_one(self, *wait):
        if not self.at.fast:
            return
        at = self.at
        with jax.named_scope(self.name + "_one"):
            low, high = after(self.low, *wait), after(self.high, *wait)
            got = at.swap_x(low), at.swap_y(high)
            self.low = ordered(at.x == 0, low, got[0], 1)
            self.high = ordered(at.y == 0, high, got[1], 1)
            self.done = got

    def step_two(self, *wait):
        if not self.at.fast:
            return
        at = self.at
        with jax.named_scope(self.name + "_two"):
            low, high = after(self.low, *wait), after(self.high, *wait)
            got = at.swap_y(low), at.swap_x(high)
            low = ordered(at.y == 0, low, got[0], 2)
            high = ordered(at.x == 0, high, got[1], 1)
            self.mine = jnp.concatenate([low, high]).reshape(at.n * self.r, self.half)
            self.done = got

    def step_last(self, *wait):
        at = self.at
        with jax.named_scope(self.name + "_last"):
            if not at.fast:
                left = lax.all_gather(jnp.concatenate([self.left, self.small], axis=1), BOTH, axis=0, tiled=True)
                right = lax.all_gather(jnp.concatenate([self.right, self.small], axis=1), BOTH, axis=0, tiled=True)
                return jnp.where(self.first, left, right), jnp.where(self.first, right, left)
            mine = after(self.mine, *wait)
            other = at.swap_c(mine)
            self.done = (other,)
            return mine, other


def half_at(a, index, axis):
    return lax.dynamic_index_in_dim(a, index, axis, keepdims=False)


def plus(kept, got):
    return (kept.astype(F32) + got.astype(F32)).astype(BF)


class Scatter:
    def __init__(self, at, name, keeps, sends):
        self.at, self.name, self.keeps, self.sends = at, name, keeps, sends
        self.total = keeps[0].shape[0]
        self.half = sum(k.shape[1] for k in keeps)
        self.r = self.total // at.n
        self.first = at.c == 0
        self.done = ()

    def step_core(self, *wait):
        if not self.at.fast:
            return
        at = self.at
        with jax.named_scope(self.name + "_core"):
            got = [at.swap_c(after(send, *wait)) for send in self.sends]
            mine = jnp.concatenate([plus(k, g) for k, g in zip(self.keeps, got)], axis=1)
            mine = mine.reshape(4, 2, 2, 2 * self.r, self.half)
            self.low, self.high = mine[:2], mine[2:]
            self.done = tuple(got)

    def step_one(self, *wait):
        if not self.at.fast:
            return
        at = self.at
        with jax.named_scope(self.name + "_one"):
            low, high = after(self.low, *wait), after(self.high, *wait)
            got = at.swap_y(half_at(low, 1 - at.y, 2)), at.swap_x(half_at(high, 1 - at.x, 1))
            self.low = plus(half_at(low, at.y, 2), got[0])
            self.high = plus(half_at(high, at.x, 1), got[1])
            self.done = got

    def step_two(self, *wait):
        if not self.at.fast:
            return
        at = self.at
        with jax.named_scope(self.name + "_two"):
            low, high = after(self.low, *wait), after(self.high, *wait)
            got = at.swap_x(half_at(low, 1 - at.x, 1)), at.swap_y(half_at(high, 1 - at.y, 1))
            low = plus(half_at(low, at.x, 1), got[0])
            high = plus(half_at(high, at.y, 1), got[1])
            self.by_z = jnp.concatenate([low, high])
            self.done = got

    def step_z(self, *wait):
        if not self.at.fast:
            return
        at = self.at
        with jax.named_scope(self.name + "_z"):
            by_z = after(self.by_z, *wait)
            got = [at.turn_z(half_at(by_z, (at.z + by) % 4, 0), by) for by in (1, 2, 3)]
            total = half_at(by_z, at.z, 0).astype(F32) + got[0].astype(F32) + got[1].astype(F32) + got[2].astype(F32)
            self.piece = total.reshape(2, self.r, self.half)
            self.done = tuple(got)

    def step_last(self, *wait):
        at = self.at
        with jax.named_scope(self.name + "_last"):
            if not at.fast:
                keep, send = jnp.concatenate(self.keeps, axis=1), jnp.concatenate(self.sends, axis=1)
                left = jnp.where(self.first, keep, send).astype(F32)
                right = jnp.where(self.first, send, keep).astype(F32)
                return (
                    lax.psum_scatter(left, BOTH, scatter_dimension=0, tiled=True),
                    lax.psum_scatter(right, BOTH, scatter_dimension=0, tiled=True),
                )
            piece = after(self.piece, *wait)
            stays = half_at(piece, at.c, 0)
            got = at.swap_c(half_at(piece, 1 - at.c, 0))
            self.done = (got,)
            return jnp.where(self.first, stays, got), jnp.where(self.first, got, stays)


class Before:
    def __init__(self, at, name, a, reverse):
        self.at, self.name, self.a, self.reverse = at, name, a, reverse
        self.fast = at.fast and a.shape[0] == 2
        self.done = ()

    def step_beside(self):
        if self.fast:
            at = self.at
            with jax.named_scope(self.name + "_beside"):
                self.got = at.swap_x(half_at(self.a, 1 - at.x, 0))
                self.own = half_at(self.a, at.x, 0)
                self.pair = plus(self.own, self.got)
                self.done = (self.got,)

    def step_z(self, *wait):
        if self.fast:
            at = self.at
            with jax.named_scope(self.name + "_z"):
                pair = after(self.pair, *wait)
                got = []
                for by in (1, 2, 3):
                    if self.reverse:
                        pairs = [(d, d - 8 * by) for d in range(8 * by, at.n)]
                    else:
                        pairs = [(d, d + 8 * by) for d in range(at.n - 8 * by)]
                    got.append(lax.ppermute(pair, BOTH, pairs))
                self.done = tuple(got)

    def step_last(self, *wait):
        at, a, reverse = self.at, self.a, self.reverse
        with jax.named_scope(self.name + "_last"):
            if not self.fast:
                everything = lax.all_gather(a, "seq").astype(F32)
                index = jnp.arange(at.seq).reshape((-1,) + (1,) * a.ndim)
                reached = index > at.s if reverse else index < at.s
                return jnp.sum(jnp.where(reached, everything, 0.0), axis=0).astype(BF)
            inner = (at.x == 0) if reverse else (at.x == 1)
            got = [after(g, *wait).astype(F32) for g in self.done]
            self.total = got[0] + got[1] + got[2]
            mine = (self.total + jnp.where(inner, self.got.astype(F32), 0.0)).astype(BF)
            send = (self.total + jnp.where(inner, 0.0, self.own.astype(F32))).astype(BF)
            return ordered(at.x == 0, mine, at.swap_x(send), 0)


class Everywhere:
    def __init__(self, at, a):
        self.at, self.a, self.done = at, a, ()

    def step(self, stride, *wait):
        if self.at.fast:
            with jax.named_scope("everywhere"):
                got = self.at.flip(after(self.a, *wait), stride)
                self.a = self.a + got
                self.done = (got,)

    def step_z(self, *wait):
        at = self.at
        with jax.named_scope("everywhere"):
            if not at.fast:
                return lax.psum(self.a, BOTH)
            a = after(self.a, *wait)
            rel = jnp.stack([a] + [at.turn_z(a, by) for by in (3, 2, 1)])
            by_z = lax.dynamic_slice_in_dim(jnp.concatenate([rel, rel]), (4 - at.z) % 4, 4)
            return (by_z[0] + by_z[1]) + (by_z[2] + by_z[3])


VMEM = pltpu.VMEM
SCALAR = pl.BlockSpec(memory_space=pltpu.SMEM)
WHOLE = pl.BlockSpec(memory_space=VMEM)


def params(mib):
    return pltpu.CompilerParams(vmem_limit_bytes=60 * 2**20)


def cost(micros):
    return pl.CostEstimate(flops=int(micros * 1e9), bytes_accessed=int(micros * 1e6), transcendentals=0)


def tdot(a, b):
    return lax.dot_general(a, b, (((0,), (0,)), ((), ())), preferred_element_type=F32)


def dot_t(a, b):
    return lax.dot_general(a, b, (((1,), (1,)), ((), ())), preferred_element_type=F32)


def dot(a, b):
    return jnp.dot(a, b, preferred_element_type=F32)


def parts(a):
    high = a.astype(BF)
    return high, (a - high.astype(F32)).astype(BF)


def left_lanes(shape):
    return lax.broadcasted_iota(jnp.int32, shape, len(shape) - 1) % 128 < 64


def two_heads(a):
    first = left_lanes(a.shape)
    wide = a.astype(F32)
    return jnp.concatenate(
        [jnp.where(first, wide, 0.0), jnp.where(first, 0.0, wide)], axis=0
    ).astype(BF)


def fold(a):
    half = a.shape[0] // 2
    return jnp.where(left_lanes((half, a.shape[1])), a[:half], a[half:])


def head_ones():
    row = lax.broadcasted_iota(jnp.int32, (128, 128), 0) // 64
    col = lax.broadcasted_iota(jnp.int32, (128, 128), 1) // 64
    return jnp.where(row == col, 1.0, 0.0).astype(BF)


def head_sums(a, ones):
    high, low = parts(a)
    return dot(high, ones) + dot(low, ones)


def features(s, g_high, g_low):
    high, low = parts(jnp.concatenate([s, s * s], axis=1))
    return jnp.exp(dot(high, g_high) + dot(high, g_low) + dot(low, g_high)) * 0.125


def features_back(t, s, g_high, g_low, ones, scale):
    high, low = parts(t)
    f_high, f_low = g_high[:128], g_low[:128]
    back = dot_t(high, f_high) + dot_t(high, f_low) + dot_t(low, f_high)
    return ((back - s * (dot(high, ones) + dot(low, ones))) * scale).astype(BF)


def lanes(p):
    return slice(p * 128, (p + 1) * 128)


def key_kernel(c_ref, tok, mine, other, gh, gl, s_out, phi_out, feat_out, v_out, state_out, vec_out):
    first = c_ref[0] == 0
    pairs, block = gh.shape[0], 128
    hw = pairs * 64
    eye = jnp.where(
        lax.broadcasted_iota(jnp.int32, (128, 128), 0) == lax.broadcasted_iota(jnp.int32, (128, 128), 1), 1.0, 0.0
    ).astype(BF)
    vecs = dot_t(eye, mine[:, 3 * hw :])[:16]
    vec_out[...] = vecs
    a = dot(tok[...], mine[:, hw : 3 * hw])
    b = dot(tok[...], other[:, hw : 3 * hw])
    left, right = jnp.where(first, a, b), jnp.where(first, b, a)
    scale = 64 ** (-0.25)
    for p in range(pairs):
        half, at = (left, p * 128) if p < pairs // 2 else (right, p * 128 - hw)
        s = (half[:, at : at + 128] + vecs[1:2, lanes(p)]) * scale
        v = (half[:, hw + at : hw + at + 128] + vecs[2:3, lanes(p)]).astype(BF)
        phi = features(s, gh[p], gl[p])
        k = phi.astype(BF)
        s_out[:, lanes(p)] = s
        phi_out[:, lanes(p)] = phi
        feat_out[:, lanes(p)] = k
        v_out[:, lanes(p)] = v
        for r in range(tok.shape[0] // block):
            rows = slice(r * block, (r + 1) * block)
            state_out[r, :64, lanes(p)] = fold(tdot(k[rows], v[rows])).astype(BF)
            total = jnp.sum(k[rows].astype(F32), axis=0, keepdims=True)
            state_out[r, 64:, lanes(p)] = jnp.broadcast_to(total, (16, 128)).astype(BF)


def query_kernel(c_ref, tok, mine, other, vec, gh, gl, s_out, phi_out, feat_out):
    first = c_ref[0] == 0
    pairs = gh.shape[0]
    hw = pairs * 64
    a, b = dot(tok[...], mine[:, :hw]), dot(tok[...], other[:, :hw])
    left, right = jnp.where(first, a, b), jnp.where(first, b, a)
    for p in range(pairs):
        half, at = (left, p * 128) if p < pairs // 2 else (right, p * 128 - hw)
        s = (half[:, at : at + 128] + vec[0:1, lanes(p)]) * 64 ** (-0.25)
        phi = features(s, gh[p], gl[p])
        s_out[:, lanes(p)] = s
        phi_out[:, lanes(p)] = phi
        feat_out[:, lanes(p)] = phi.astype(BF)


def halo_kernel(c_ref, halo, mine, other, vec, gh, gl, hk_out, hv_out):
    first, inner = c_ref[0] == 0, c_ref[1] > 0
    pairs = gh.shape[0]
    hw = pairs * 64
    a, b = dot(halo[...], mine[:, hw : 3 * hw]), dot(halo[...], other[:, hw : 3 * hw])
    left, right = jnp.where(first, a, b), jnp.where(first, b, a)
    for p in range(pairs):
        half, at = (left, p * 128) if p < pairs // 2 else (right, p * 128 - hw)
        s = (half[:, at : at + 128] + vec[1:2, lanes(p)]) * 64 ** (-0.25)
        v = half[:, hw + at : hw + at + 128] + vec[2:3, lanes(p)]
        hk_out[:, lanes(p)] = jnp.where(inner, features(s, gh[p], gl[p]), 0.0).astype(BF)
        hv_out[:, lanes(p)] = jnp.where(inner, v, 0.0).astype(BF)


def window_weights(base):
    turned = pltpu.roll(jnp.broadcast_to(base, (128, 256)), 0, 1, stride=1, stride_axis=0)
    row = lax.broadcasted_iota(jnp.int32, (128, 256), 0)
    col = lax.broadcasted_iota(jnp.int32, (128, 256), 1)
    return jnp.where(col > row + 128, 0.0, turned - jnp.where(col < 128, base[:, 255:256], 0.0))


def pair_at(step, c, pairs):
    return (step + (pairs // 2) * (1 - c)) % pairs


def block_diagonal(packed):
    return two_heads(packed)


def attention_kernel(q, k, v, hk, hv, table, state, far, context_out, turned_out, ratio_out, denom_out):
    ones = head_ones()
    wmat = jnp.concatenate([window_weights(table[0, 0:1]), window_weights(table[0, 1:2])], axis=0)
    far_row = far[0:1]
    for r in range(q.shape[0] // 128):
        rows = slice(r * 128, (r + 1) * 128)
        qr = q[rows]
        kw = jnp.concatenate([hk[rows], k[rows]], axis=0)
        vw = jnp.concatenate([hv[rows], v[rows]], axis=0)
        weighted = dot_t(two_heads(qr), kw) * wmat
        numer = fold(dot(weighted.astype(BF), vw))
        near = jnp.sum(weighted, axis=1, keepdims=True)
        near = fold(jnp.broadcast_to(near, (256, 128)))
        bd = block_diagonal(state[r, :64])
        total = state[r, 64:80].astype(F32)[0:1]
        numer = numer + far_row * dot(qr, bd)
        denom = near + far_row * head_sums(qr.astype(F32) * total, ones)
        ratio = numer / denom
        context_out[rows] = ratio.astype(BF)
        turned_out[:, rows] = ratio.T.astype(BF)
        ratio_out[rows] = ratio
        denom_out[rows] = denom


def normed(x):
    centred = x - jnp.mean(x, axis=-1, keepdims=True)
    rstd = lax.rsqrt(jnp.mean(centred * centred, axis=-1, keepdims=True) + EPS)
    return centred * rstd, rstd


def norm_back(dy, xhat, rstd, gain):
    d = dy * gain
    return rstd * (
        d - jnp.mean(d, axis=-1, keepdims=True) - xhat * jnp.mean(d * xhat, axis=-1, keepdims=True)
    )


def col_sums(a):
    return jnp.sum(a, axis=0, keepdims=True)


def middle_kernel(
    count, context, tok, cot, vec, bu, ratio, denom, q, state, far, rest_hbm, *more,
):
    blocks_hbm, more = more[:count], more[count:]
    (
        out, dresid_out, dattn_out, dn_out, later_out, sums_out, near_out, du_sums_out, down_hbm, up_hbm,
        w, wd, gp, grads, in_sems, out_sems,
    ) = more
    width, step = tok.shape[1], wd.shape[1]
    hw = width // 2
    loads = []
    for i in range(count):
        loads.append(pltpu.make_async_copy(blocks_hbm[i], w.at[i], in_sems.at[i]))
    for i in range(count):
        wd_block = rest_hbm.at[pl.ds(i * step, step), pl.ds(0, width)]
        loads.append(pltpu.make_async_copy(wd_block, wd.at[i], in_sems.at[count + i]))
    for load in loads:
        load.start()
    for load in loads[:count]:
        load.wait()
    attn = jnp.concatenate([dot(context[...], w[i, :, step:]) for i in range(count)], axis=1)
    xhat, rstd = normed(tok[...].astype(F32) + attn + vec[3:4])
    hidden = xhat * vec[4:5] + vec[5:6]
    h_low = hidden.astype(BF)
    lower = hidden + vec[6:7]
    actives = []
    for i in range(count):
        cols = slice(i * step, (i + 1) * step)
        upper = dot(h_low, w[i, :, :step]) + bu[:, cols]
        cdf = 0.5 * (1.0 + lax.erf(upper * 2.0 ** (-0.5)))
        pdf = jnp.exp(-0.5 * upper * upper) * (2.0 * math.pi) ** (-0.5)
        gp[:, cols] = (cdf + upper * pdf).astype(BF)
        actives.append((upper * cdf).astype(BF))
        loads[count + i].wait()
        lower = lower + dot(actives[-1], wd[i])
    xhat2, rstd2 = normed(lower)
    gain2 = vec[7:8]
    out[...] = xhat2 * gain2 + vec[8:9]
    dy = cot[...].astype(F32)
    d_hidden = norm_back(dy, xhat2, rstd2, gain2)
    d_low = d_hidden.astype(BF)
    sums_out[0:1] = col_sums(d_low.astype(F32))
    sums_out[1:2] = col_sums(dy * xhat2)
    sums_out[2:3] = col_sums(dy)
    stores = []
    for i in range(count):
        cols = slice(i * step, (i + 1) * step)
        d_upper = (dot_t(d_low, wd[i]) * gp[:, cols].astype(F32)).astype(BF)
        du_sums_out[:, cols] = jnp.broadcast_to(col_sums(d_upper.astype(F32)), (8, step))
        d_hidden = d_hidden + dot_t(d_upper, w[i, :, :step])
        grads[2 * i] = tdot(h_low, d_upper).astype(BF)
        stores.append(pltpu.make_async_copy(grads.at[2 * i], up_hbm.at[i], out_sems.at[2 * i]))
        stores[-1].start()
        grads[2 * i + 1] = tdot(actives[i], d_low).astype(BF)
        block = down_hbm.at[pl.ds(i * step, step), pl.ds(0, width)]
        stores.append(pltpu.make_async_copy(grads.at[2 * i + 1], block, out_sems.at[2 * i + 1]))
        stores[-1].start()
    d_resid = norm_back(d_hidden, xhat, rstd, vec[4:5])
    dresid_out[...] = d_resid
    d_attn = d_resid.astype(BF)
    dattn_out[...] = d_attn
    sums_out[3:4] = col_sums(d_attn.astype(F32))
    sums_out[4:5] = col_sums(d_hidden * xhat)
    sums_out[5:6] = col_sums(d_hidden)
    part = width // count
    d_context = sum(dot_t(d_resid[:, i * part : (i + 1) * part].astype(BF), w[i, :, step:]) for i in range(count))
    ones = head_ones()
    pick = jnp.where(
        lax.broadcasted_iota(jnp.int32, (width, 128), 0) == 64 * lax.broadcasted_iota(jnp.int32, (width, 128), 1), 1.0, 0.0
    ).astype(BF)
    all_denoms = []
    for p in range(width // 128):
        dc = d_context[:, lanes(p)]
        inverse = 1.0 / denom[:, lanes(p)]
        dn = (dc * inverse).astype(BF)
        dd = (-head_sums(dc * ratio[:, lanes(p)], ones) * inverse).astype(BF)
        dn_out[:, lanes(p)] = dn
        all_denoms.append(dd)
        near = jnp.zeros((1, 128), F32)
        for r in range(tok.shape[0] // 128):
            rows = slice(r * 128, (r + 1) * 128)
            qr = q[rows, lanes(p)]
            packed = fold(tdot(qr, dn[rows]))
            total = col_sums(qr.astype(F32) * dd[rows].astype(F32))
            far_row = far[0:1, lanes(p)]
            later_out[r, :64, lanes(p)] = (far_row * packed).astype(BF)
            later_out[r, 64:, lanes(p)] = jnp.broadcast_to(far_row * total, (16, 128)).astype(BF)
            held = state[r, :, lanes(p)].astype(F32)
            near = near + col_sums(held[:64] * packed) + held[64:65] * total
        near_out[:, lanes(p)] = jnp.broadcast_to(near, (8, 128))
    dn_out[:, width:] = dot(jnp.concatenate(all_denoms, axis=1), pick).astype(BF)
    for store in stores:
        store.wait()


def spread(dn, p):
    lane = lax.broadcasted_iota(jnp.int32, dn.shape, 1)
    wide = dn.astype(F32)
    return [jnp.sum(jnp.where(lane == 2 * p + h, wide, 0.0), axis=1, keepdims=True) for h in (0, 1)]


def query_back_kernel(
    c_ref, tok, context, dattn, q, k, v, hk, hv, dn, dd, table, state, far, phi, s, gh, gl, near,
    dq_out, keep_out, send_out, pos_out, sums_out,
):
    steps = pl.num_programs(0)
    p = pair_at(pl.program_id(0), c_ref[0], steps)
    ones = head_ones()
    wmat = jnp.concatenate([window_weights(table[0, 0:1]), window_weights(table[0, 1:2])], axis=0)
    far_row = far[0:1]
    first = left_lanes((128, 128))
    pieces = jnp.zeros((256, 256), F32)
    grads = []
    for r in range(q.shape[0] // 128):
        rows = slice(r * 128, (r + 1) * 128)
        kw = jnp.concatenate([hk[rows], k[rows]], axis=0)
        vw = jnp.concatenate([hv[rows], v[rows]], axis=0)
        scores = dot_t(two_heads(q[rows]), kw)
        d0, d1 = spread(dd[rows], p)
        dnr = dn[rows]
        dw = dot_t(two_heads(dnr), vw) + jnp.concatenate([d0, d1], axis=0)
        pieces = pieces + dw * scores
        ds = (dw * wmat).astype(BF)
        bd = block_diagonal(state[r, :64])
        total = state[r, 64:80].astype(F32)[0:1]
        dq = fold(dot(ds, kw)) + far_row * (dot_t(dnr, bd) + jnp.where(first, d0, d1) * total)
        grads.append(
            features_back(dq * phi[rows], s[rows], gh[0], gl[0], ones, 64 ** (-0.25))
        )
    dq = jnp.concatenate(grads, axis=0)
    dq_out[...] = dq
    sums_out[...] = jnp.broadcast_to(col_sums(dq.astype(F32)), sums_out.shape)
    grad = jnp.concatenate([dot(tok[...], dq), dot(context[...], dattn[...])], axis=1).astype(BF)
    place_half(grad, keep_out, send_out)
    row = lax.broadcasted_iota(jnp.int32, (256, 256), 0)
    col = lax.broadcasted_iota(jnp.int32, (256, 256), 1)
    mirror = jnp.where(row + col == 255, 1.0, 0.0).astype(BF)
    high, low = parts(jnp.where(col <= row % 128 + 128, pieces, 0.0))
    mirrored = dot(high, mirror) + dot(low, mirror)
    lane = lax.broadcasted_iota(jnp.int32, (1, 256), 1)
    for h in (0, 1):
        rows = slice(h * 128, (h + 1) * 128)
        by_distance = col_sums(pltpu.roll(mirrored[rows], 129, 1, stride=1, stride_axis=0))
        plain = col_sums(pieces[rows])
        apart = jnp.where(lane >= 128, by_distance, 0.0) - jnp.where(lane < 128, plain, 0.0)
        state_part = jnp.where(lane[:, :128] // 64 == h, near[0:1], 0.0)
        far_sum = jnp.sum(apart, axis=1, keepdims=True) + jnp.sum(state_part, axis=1, keepdims=True)
        pos_out[0, h : h + 1] = jnp.where(lane < 128, by_distance, far_sum)


def place_half(grad, keep_out, send_out):
    early = pl.program_id(0) < pl.num_programs(0) // 2

    @pl.when(early)
    def _():
        send_out[...] = grad

    @pl.when(jnp.logical_not(early))
    def _():
        keep_out[...] = grad


def key_back_kernel(
    c_ref, tok, q, k, v, dn, dd, qn, dnn, ddn, table, later, phi, s, gh, gl, rows_in,
    dk_out, dv_out, keep_out, send_out, small_out,
):
    p = pair_at(pl.program_id(0), c_ref[0], pl.num_programs(0))
    ones = head_ones()
    first, second = window_weights(table[0, 0:1]), window_weights(table[0, 1:2])
    tables = jnp.concatenate([first[:, 128:], second[:, 128:], first[:, :128], second[:, :128]], axis=0)
    dks, dvs = [], []
    for r in range(q.shape[0] // 128):
        rows = slice(r * 128, (r + 1) * 128)
        kr, vr = k[rows], v[rows]
        q4 = jnp.concatenate([two_heads(q[rows]), two_heads(qn[rows])], axis=0)
        dn4 = jnp.concatenate([two_heads(dn[rows]), two_heads(dnn[rows])], axis=0)
        dd4 = jnp.concatenate(spread(dd[rows], p) + spread(ddn[rows], p), axis=0)
        w = (dot_t(q4, kr) * tables).astype(BF)
        ds = ((dot_t(dn4, vr) + dd4) * tables).astype(BF)
        bd = block_diagonal(later[r, :64])
        total = later[r, 64:80].astype(F32)[0:1]
        dk = tdot(ds, q4) + dot_t(vr, bd) + total
        dvs.append((tdot(w, dn4) + dot(kr, bd)).astype(BF))
        dks.append(features_back(dk * phi[rows], s[rows], gh[0], gl[0], ones, 64 ** (-0.25)))
    dk, dv = jnp.concatenate(dks, axis=0), jnp.concatenate(dvs, axis=0)
    dk_out[...] = dk
    dv_out[...] = dv
    place_half(jnp.concatenate([dot(tok[...], dk), dot(tok[...], dv)], axis=1).astype(BF), keep_out, send_out)
    row = lax.broadcasted_iota(jnp.int32, (16, 128), 0)
    lane = lax.broadcasted_iota(jnp.int32, (16, 128), 1)
    late = jnp.where(row == 1, col_sums(dk.astype(F32)), 0.0) + jnp.where(row == 2, col_sums(dv.astype(F32)), 0.0)
    small_out[...] = tdot((rows_in[...] + late).astype(BF), jnp.where(row == lane, 1.0, 0.0).astype(BF)).astype(BF)


def tokens_kernel(c_ref, dresid, dq, dk, dv, mine, other, out):
    first = c_ref[0] == 0
    hw = dq.shape[1] // 2
    total = dresid[...]
    for i, d in enumerate((dq, dk, dv)):
        wide = d[...].astype(F32)
        a = jnp.where(first, wide[:, :hw], wide[:, hw:]).astype(BF)
        b = jnp.where(first, wide[:, hw:], wide[:, :hw]).astype(BF)
        cols = slice(i * hw, (i + 1) * hw)
        total = total + dot_t(a, mine[:, cols]) + dot_t(b, other[:, cols])
    out[...] = total


def unpack_kernel(packed, down_out, up_out):
    own, width = up_out.shape[0], down_out.shape[1]
    step = packed.shape[1] - width
    wide = packed[...].astype(F32)
    down_out[...] = wide[:, :width]
    for i in range(packed.shape[0] // own):
        up_out[:, i * step : (i + 1) * step] = wide[i * own : (i + 1) * own, width:]


def feature_blocks(matrix):
    heads, size, feats = matrix.shape
    zero = jnp.zeros((heads // 2, size, feats), F32)
    even, odd = matrix[0::2], matrix[1::2]
    half = jnp.full(zero.shape, -0.5, F32)
    blocks = jnp.concatenate(
        [
            jnp.concatenate([even, zero], axis=2),
            jnp.concatenate([zero, odd], axis=2),
            jnp.concatenate([half, zero], axis=2),
            jnp.concatenate([zero, half], axis=2),
        ],
        axis=1,
    )
    high = lax.reduce_precision(blocks, 8, 7)
    return high.astype(BF), (blocks - high).astype(BF)


def on_device(
    tokens,
    query_weight,
    query_bias,
    key_weight,
    key_bias,
    value_weight,
    value_bias,
    output_weight,
    output_bias,
    first_gain,
    first_shift,
    up_weight,
    up_bias,
    down_weight,
    down_bias,
    second_gain,
    second_shift,
    position_bias,
    feature_matrix,
    cotangent,
):
    at = Place()
    rows, block, width = tokens.shape
    heads, size, feats = feature_matrix.shape
    window = position_bias.shape[1] - 1
    pairs = heads // 2
    n = rows * block
    hw = width // 2
    ff = up_weight.shape[1]
    hf = ff // 2
    own = query_weight.shape[0]
    up_own = up_bias.shape[0] // own
    tok = tokens.reshape(n, width)
    cot = cotangent.reshape(n, width)
    flags = jnp.stack([at.c, at.s]).astype(jnp.int32)

    def arr(shape, kind):
        return jax.ShapeDtypeStruct(shape, kind)

    halo_tok = at.along(tok, 1)
    tok_t = tok.T

    vectors = (
        query_bias, key_bias, value_bias, output_bias, first_gain, first_shift,
        down_bias, second_gain, second_shift,
    )
    count = len(vectors)
    small = jnp.concatenate(vectors + (up_bias,)).reshape(count + up_own, own).T
    small = jnp.pad(small, ((0, 0), (0, 128 - small.shape[1])))
    slices = down_weight.shape[0] // own
    step, wo_step = ff // slices, width // slices

    def stacked(a):
        return jnp.concatenate(jnp.split(a, slices, axis=1), axis=0)

    rest = lax.all_gather(
        jnp.concatenate([down_weight, stacked(up_weight), stacked(output_weight)], axis=1), BOTH, axis=0, tiled=True
    )
    g1 = Gather(
        at,
        "qkv",
        jnp.concatenate([query_weight[:, :hw], key_weight[:, :hw], value_weight[:, :hw]], axis=1),
        jnp.concatenate([query_weight[:, hw:], key_weight[:, hw:], value_weight[:, hw:]], axis=1),
        small,
    )
    exp_bias = jnp.exp(position_bias)
    table = jnp.concatenate(
        [exp_bias[:, ::-1], jnp.broadcast_to(exp_bias[:, window:], (heads, block - 1))], axis=1
    ).reshape(pairs, 2, window + block)
    table = jnp.pad(table, ((0, 0), (0, 6), (0, 0)))
    far = jnp.broadcast_to(jnp.repeat(exp_bias[:, window], size)[None], (8, width))
    gh, gl = feature_blocks(feature_matrix)

    g1.step_core()
    g1.step_z()
    g1.step_one()
    g1.step_two()
    m1, o1 = g1.step_last(table, far, gh, gl, tok_t)

    wide32, wide16 = arr((n, width), F32), arr((n, width), BF)
    sums = arr((rows, 80, width), BF)
    sk, k_phi, k, v, local, vec = pl.pallas_call(
        key_kernel,
        out_shape=(wide32, wide32, wide16, wide16, sums, arr((16, width), F32)),
        in_specs=[SCALAR] + [WHOLE] * 5,
        out_specs=(WHOLE,) * 6,
        compiler_params=params(48),
        cost_estimate=cost(5),
        name="keys",
    )(flags, tok, m1, o1, gh, gl)
    scan = Before(at, "before", local, False)
    scan.step_beside()
    sq, q_phi, q = pl.pallas_call(
        query_kernel,
        out_shape=(wide32, wide32, wide16),
        in_specs=[SCALAR] + [WHOLE] * 6,
        out_specs=(WHOLE,) * 3,
        compiler_params=params(48),
        cost_estimate=cost(3),
        name="queries",
    )(flags, tok, m1, o1, vec, gh, gl)
    scan.step_z(q)
    hk, hv = pl.pallas_call(
        halo_kernel,
        out_shape=(wide16, wide16),
        in_specs=[SCALAR] + [WHOLE] * 6,
        out_specs=(WHOLE,) * 2,
        compiler_params=params(48),
        cost_estimate=cost(2),
        name="halo",
    )(flags, after(halo_tok, *scan.done), m1, o1, vec, gh, gl)
    q_next = at.along(q, -1)
    before = scan.step_last(hk, q_next)
    b_u = m1[:, 3 * hw + count : 3 * hw + count + up_own].reshape(at.n, own, up_own)
    b_u = jnp.swapaxes(after(b_u, hk), 1, 2).reshape(1, ff).astype(F32)

    def columns(height=n):
        return pl.BlockSpec((height, 128), lambda p, *_: (0, p))

    table_spec = pl.BlockSpec((1, 8, window + block), lambda p, *_: (p, 0, 0))
    sums_spec = pl.BlockSpec((rows, 80, 128), lambda p, *_: (0, 0, p))
    g_spec = pl.BlockSpec((1, 256, 128), lambda p, *_: (p, 0, 0))
    tok_spec = pl.BlockSpec((width, n), lambda p, *_: (0, 0))
    dd_spec = pl.BlockSpec((n, 128), lambda p, *_: (0, pairs))
    context, context_t, ratio, denom = pl.pallas_call(
        attention_kernel,
        grid=(pairs,),
        out_shape=(wide16, arr((width, n), BF), wide32, wide32),
        in_specs=[columns()] * 5 + [table_spec, sums_spec, columns(8)],
        out_specs=(columns(), pl.BlockSpec((128, n), lambda p, *_: (p, 0)), columns(), columns()),
        compiler_params=params(32),
        cost_estimate=cost(5),
        name="attention",
    )(q, k, v, hk, hv, table, before, far)

    split = rest.reshape(at.n, slices, own, rest.shape[1])
    blocks = [split[:, i, :, width:].reshape(width, step + wo_step) for i in range(slices)]
    away = pl.BlockSpec(memory_space=pl.ANY)
    out, d_resid, d_attn, dn, local, sums2, near, du_sums, g_down, g_up = pl.pallas_call(
        functools.partial(middle_kernel, slices),
        out_shape=(
            wide32, wide32, wide16, arr((n, width + 128), BF), sums, arr((8, width), F32), arr((8, width), F32),
            arr((8, ff), F32), arr((ff, width + step), BF), arr((slices, width, step), BF),
        ),
        in_specs=[WHOLE] * 10 + [away] * (1 + slices),
        out_specs=(WHOLE,) * 8 + (away,) * 2,
        scratch_shapes=[
            VMEM((slices, width, step + wo_step), BF),
            VMEM((slices, step, width), BF),
            VMEM((n, ff), BF),
            VMEM((2 * slices, width, step), BF),
            pltpu.SemaphoreType.DMA((2 * slices,)),
            pltpu.SemaphoreType.DMA((2 * slices,)),
        ],
        compiler_params=params(56),
        cost_estimate=cost(20),
        name="middle",
    )(context, tok, cot, vec, b_u, ratio, denom, q, before, far, rest, *blocks)
    g_up = jnp.swapaxes(g_up.reshape(slices, at.n, own, step), 0, 1).reshape(ff, step)
    g_rest = lax.dynamic_update_slice(g_down, g_up, (0, width))
    s_rest = lax.psum_scatter(g_rest, BOTH, scatter_dimension=0, tiled=True)
    if own % 8 == 0:
        s_d, s_u = pl.pallas_call(
            unpack_kernel,
            out_shape=(arr((slices * own, width), F32), arr((own, ff), F32)),
            in_specs=[WHOLE],
            out_specs=(WHOLE,) * 2,
            compiler_params=params(48),
            cost_estimate=cost(1),
            name="unpack",
        )(s_rest)
    else:
        s_d = s_rest[:, :width].astype(F32)
        s_u = jnp.concatenate(jnp.split(s_rest[:, width:].astype(F32), slices, axis=0), axis=1)
    scan = Before(at, "later", local, True)
    scan.step_beside()
    dn_next = at.along(dn, -1)

    def turned(p, c):
        return pair_at(p, c[0], pairs)

    cols = pl.BlockSpec((n, 128), lambda p, c: (0, turned(p, c)))
    cols8 = pl.BlockSpec((8, 128), lambda p, c: (0, turned(p, c)))
    by_pair = pl.BlockSpec((1, 8, window + block), lambda p, c: (turned(p, c), 0, 0))
    sums_by_pair = pl.BlockSpec((rows, 80, 128), lambda p, c: (0, 0, turned(p, c)))
    g_by_pair = pl.BlockSpec((1, 256, 128), lambda p, c: (turned(p, c), 0, 0))
    kept = pl.BlockSpec((width, 256), lambda p, c: (0, jnp.maximum(p - pairs // 2, 0)))
    sent = pl.BlockSpec((width, 256), lambda p, c: (0, jnp.minimum(p, pairs // 2 - 1)))
    half = arr((width, 2 * hw), BF)
    dq, keep1, send1, pos, sums_q = pl.pallas_call(
        query_back_kernel,
        grid_spec=pltpu.PrefetchScalarGridSpec(
            num_scalar_prefetch=1,
            grid=(pairs,),
            in_specs=[tok_spec] * 2 + [cols] * 7 + [dd_spec, by_pair, sums_by_pair, cols8]
            + [cols] * 2 + [g_by_pair] * 2 + [cols8],
            out_specs=(cols, kept, sent, by_pair, cols8),
        ),
        out_shape=(wide16, half, half, arr((pairs, 8, 256), F32), arr((8, width), F32)),
        compiler_params=params(32),
        cost_estimate=cost(0.001),
        name="query_back",
    )(flags, after(tok_t, *scan.done, g_rest), context_t, d_attn, q, k, v, hk, hv, dn, dn, table, before, far, q_phi, sq, gh, gl, near)
    scan.step_z()
    later = scan.step_last(dq, dn_next)
    everywhere = Everywhere(at, exp_bias * pos[:, :2, : window + 1].reshape(heads, window + 1))
    everywhere.step(1)
    du = du_sums[0].reshape(at.n, up_own, own)
    du = jnp.swapaxes(du, 0, 1).reshape(up_own, width)
    nil = jnp.zeros((2, width), F32)
    early = jnp.concatenate([sums_q[:1], nil, sums2[3:6], sums2[:3], du], axis=0)
    early = jnp.pad(early, ((0, 16 - early.shape[0]), (0, 0)))
    dk, dv, keep0, send0, small = pl.pallas_call(
        key_back_kernel,
        grid_spec=pltpu.PrefetchScalarGridSpec(
            num_scalar_prefetch=1,
            grid=(pairs,),
            in_specs=[tok_spec] + [cols] * 4 + [dd_spec] + [cols] * 2
            + [dd_spec, by_pair, sums_by_pair] + [cols] * 2 + [g_by_pair] * 2
            + [pl.BlockSpec((16, 128), lambda p, c: (0, turned(p, c)))],
            out_specs=(cols, cols, kept, sent, pl.BlockSpec((128, 128), lambda p, c: (turned(p, c), 0))),
        ),
        out_shape=(wide16, wide16, half, half, arr((width, 128), BF)),
        compiler_params=params(32),
        cost_estimate=cost(0.001),
        name="key_back",
    )(flags, after(tok_t, *everywhere.done), q, k, v, dn, dn, q_next, dn_next, dn_next, table, later, k_phi, sk, gh, gl, early)

    r0 = Scatter(at, "d_qkv", (keep1, keep0, small), (send1, send0, small))
    r0.step_core()
    everywhere.step(2, dk)
    r0.step_one(*everywhere.done)
    everywhere.step(4, *r0.done)
    r0.step_two(*everywhere.done)
    two0 = r0.done
    r0.step_z()
    position_grad = everywhere.step_z(*two0)
    s_qkv = r0.step_last()
    d_tokens = pl.pallas_call(
        tokens_kernel,
        out_shape=wide32,
        in_specs=[SCALAR] + [WHOLE] * 6,
        out_specs=WHOLE,
        compiler_params=params(40),
        cost_estimate=cost(0.001),
        name="tokens",
    )(flags, d_resid, dq, dk, dv, m1, o1)

    def woven(pair, at):
        return jnp.concatenate(
            [half[:, at + p * 256 : at + p * 256 + 128] for half in pair for p in range(pairs // 2)], axis=1
        )

    s_small = s_qkv[0][:, 4 * hw :]
    bq, bk, bv, bo, sg1, ss1, bd, sg2, ss2 = [s_small[:, i] for i in range(count)]
    bu = s_small[:, count : count + up_own].T.reshape(-1)
    return (
        out.reshape(rows, block, width),
        d_tokens.reshape(rows, block, width),
        woven(s_qkv, 0),
        bq,
        woven(s_qkv, 2 * hw),
        bk,
        woven(s_qkv, 2 * hw + 128),
        bv,
        woven(s_qkv, 128),
        bo,
        sg1,
        ss1,
        s_u,
        bu,
        s_d,
        bd,
        sg2,
        ss2,
        position_grad,
    )


def solution(mesh):
    matrix, vector, split = P(BOTH, None), P(BOTH), P("rows", "seq", None)
    return jax.shard_map(
        on_device,
        mesh=mesh,
        in_specs=(split,)
        + (matrix, vector) * 4
        + (vector, vector)
        + (matrix, vector) * 2
        + (vector, vector)
        + (P(), P(), split),
        out_specs=(split, split)
        + (matrix, vector) * 4
        + (vector, vector)
        + (matrix, vector) * 2
        + (vector, vector)
        + (P(),),
        check_vma=False,
    )
```

```python
import functools
import math

import jax
import jax.numpy as jnp
from jax import lax
from jax.experimental import pallas as pl
from jax.experimental.pallas import tpu as pltpu
from jax.sharding import PartitionSpec as P

BOTH = ("seq", "rows")
EPS = 1e-06
BF = jnp.bfloat16
F32 = jnp.float32


class Place:
    def __init__(self):
        self.seq = lax.axis_size("seq")
        self.rows = lax.axis_size("rows")
        self.n = self.seq * self.rows
        self.fast = self.seq == 8 and self.rows == 4
        me = lax.axis_index(BOTH)
        self.c = me % 2
        self.y = (me // 2) % 2
        self.x = (me // 4) % 2
        self.z = me // 8
        self.s = lax.axis_index("seq")

    def flip(self, a, stride):
        return lax.ppermute(a, BOTH, [(d, d ^ stride) for d in range(self.n)])

    def swap_c(self, a):
        return self.flip(a, 1)

    def swap_y(self, a):
        return self.flip(a, 2)

    def swap_x(self, a):
        return self.flip(a, 4)

    def turn_z(self, a, by):
        return lax.ppermute(a, BOTH, [(d, (d + 8 * by) % self.n) for d in range(self.n)])

    def along(self, a, by):
        pairs = [(i, i + by) for i in range(self.seq) if 0 <= i + by < self.seq]
        return lax.ppermute(a, "seq", pairs)


def after(a, *others):
    return lax.optimization_barrier((a, others))[0]


def ordered(first, mine, other, axis):
    return jnp.where(
        first, jnp.stack([mine, other], axis=axis), jnp.stack([other, mine], axis=axis)
    )


class Gather:
    def __init__(self, at, name, left, right, small):
        self.at, self.name = at, name
        self.r, self.half = left.shape
        self.first = at.c == 0
        self.left, self.right, self.small = left, right, small
        self.done = ()

    def step_core(self, *wait):
        if not self.at.fast:
            return
        with jax.named_scope(self.name + "_core"):
            got = self.at.swap_c(after(jnp.where(self.first, self.right, self.left), *wait))
            kept = jnp.where(self.first, self.left, self.right)
            piece = ordered(self.first, kept, got, 0)
            mine = after(self.small, piece)
            small = ordered(self.first, mine, self.at.swap_c(mine), 0)
            self.half += self.small.shape[1]
            self.piece = jnp.concatenate([piece, small], axis=2).reshape(2 * self.r, self.half)
            self.done = (got,)

    def step_z(self, *wait):
        if not self.at.fast:
            return
        at = self.at
        with jax.named_scope(self.name + "_z"):
            piece = after(self.piece, *wait)
            turned = [at.turn_z(piece, by) for by in (1, 2, 3)]
            rel = jnp.stack([piece, turned[2], turned[1], turned[0]])
            by_z = lax.dynamic_slice_in_dim(jnp.concatenate([rel, rel]), (4 - at.z) % 4, 4)
            self.low, self.high = by_z[:2], by_z[2:]
            self.done = tuple(turned)

    def step_one(self, *wait):
        if not self.at.fast:
            return
        at = self.at
        with jax.named_scope(self.name + "_one"):
            low, high = after(self.low, *wait), after(self.high, *wait)
            got = at.swap_x(low), at.swap_y(high)
            self.low = ordered(at.x == 0, low, got[0], 1)
            self.high = ordered(at.y == 0, high, got[1], 1)
            self.done = got

    def step_two(self, *wait):
        if not self.at.fast:
            return
        at = self.at
        with jax.named_scope(self.name + "_two"):
            low, high = after(self.low, *wait), after(self.high, *wait)
            got = at.swap_y(low), at.swap_x(high)
            low = ordered(at.y == 0, low, got[0], 2)
            high = ordered(at.x == 0, high, got[1], 1)
            self.mine = jnp.concatenate([low, high]).reshape(at.n * self.r, self.half)
            self.done = got

    def step_last(self, *wait):
        at = self.at
        with jax.named_scope(self.name + "_last"):
            if not at.fast:
                left = lax.all_gather(jnp.concatenate([self.left, self.small], axis=1), BOTH, axis=0, tiled=True)
                right = lax.all_gather(jnp.concatenate([self.right, self.small], axis=1), BOTH, axis=0, tiled=True)
                return jnp.where(self.first, left, right), jnp.where(self.first, right, left)
            mine = after(self.mine, *wait)
            other = at.swap_c(mine)
            self.done = (other,)
            return mine, other


def half_at(a, index, axis):
    return lax.dynamic_index_in_dim(a, index, axis, keepdims=False)


def plus(kept, got):
    return (kept.astype(F32) + got.astype(F32)).astype(BF)


class Scatter:
    def __init__(self, at, name, keeps, sends):
        self.at, self.name, self.keeps, self.sends = at, name, keeps, sends
        self.total = keeps[0].shape[0]
        self.half = sum(k.shape[1] for k in keeps)
        self.r = self.total // at.n
        self.first = at.c == 0
        self.done = ()

    def step_core(self, *wait):
        if not self.at.fast:
            return
        at = self.at
        with jax.named_scope(self.name + "_core"):
            got = [at.swap_c(after(send, *wait)) for send in self.sends]
            mine = jnp.concatenate([plus(k, g) for k, g in zip(self.keeps, got)], axis=1)
            mine = mine.reshape(4, 2, 2, 2 * self.r, self.half)
            self.low, self.high = mine[:2], mine[2:]
            self.done = tuple(got)

    def step_one(self, *wait):
        if not self.at.fast:
            return
        at = self.at
        with jax.named_scope(self.name + "_one"):
            low, high = after(self.low, *wait), after(self.high, *wait)
            got = at.swap_y(half_at(low, 1 - at.y, 2)), at.swap_x(half_at(high, 1 - at.x, 1))
            self.low = plus(half_at(low, at.y, 2), got[0])
            self.high = plus(half_at(high, at.x, 1), got[1])
            self.done = got

    def step_two(self, *wait):
        if not self.at.fast:
            return
        at = self.at
        with jax.named_scope(self.name + "_two"):
            low, high = after(self.low, *wait), after(self.high, *wait)
            got = at.swap_x(half_at(low, 1 - at.x, 1)), at.swap_y(half_at(high, 1 - at.y, 1))
            low = plus(half_at(low, at.x, 1), got[0])
            high = plus(half_at(high, at.y, 1), got[1])
            self.by_z = jnp.concatenate([low, high])
            self.done = got

    def step_z(self, *wait):
        if not self.at.fast:
            return
        at = self.at
        with jax.named_scope(self.name + "_z"):
            by_z = after(self.by_z, *wait)
            got = [at.turn_z(half_at(by_z, (at.z + by) % 4, 0), by) for by in (1, 2, 3)]
            total = half_at(by_z, at.z, 0).astype(F32) + got[0].astype(F32) + got[1].astype(F32) + got[2].astype(F32)
            self.piece = total.reshape(2, self.r, self.half)
            self.done = tuple(got)

    def step_last(self, *wait):
        at = self.at
        with jax.named_scope(self.name + "_last"):
            if not at.fast:
                keep, send = jnp.concatenate(self.keeps, axis=1), jnp.concatenate(self.sends, axis=1)
                left = jnp.where(self.first, keep, send).astype(F32)
                right = jnp.where(self.first, send, keep).astype(F32)
                return (
                    lax.psum_scatter(left, BOTH, scatter_dimension=0, tiled=True),
                    lax.psum_scatter(right, BOTH, scatter_dimension=0, tiled=True),
                )
            piece = after(self.piece, *wait)
            stays = half_at(piece, at.c, 0)
            got = at.swap_c(half_at(piece, 1 - at.c, 0))
            self.done = (got,)
            return jnp.where(self.first, stays, got), jnp.where(self.first, got, stays)


class Before:
    def __init__(self, at, name, a, reverse):
        self.at, self.name, self.a, self.reverse = at, name, a, reverse
        self.fast = at.fast and a.shape[0] == 2
        self.done = ()

    def step_beside(self):
        if self.fast:
            at = self.at
            with jax.named_scope(self.name + "_beside"):
                self.got = at.swap_x(half_at(self.a, 1 - at.x, 0))
                self.own = half_at(self.a, at.x, 0)
                self.pair = plus(self.own, self.got)
                self.done = (self.got,)

    def step_z(self, *wait):
        if self.fast:
            at = self.at
            with jax.named_scope(self.name + "_z"):
                pair = after(self.pair, *wait)
                got = []
                for by in (1, 2, 3):
                    if self.reverse:
                        pairs = [(d, d - 8 * by) for d in range(8 * by, at.n)]
                    else:
                        pairs = [(d, d + 8 * by) for d in range(at.n - 8 * by)]
                    got.append(lax.ppermute(pair, BOTH, pairs))
                self.done = tuple(got)

    def step_last(self, *wait):
        at, a, reverse = self.at, self.a, self.reverse
        with jax.named_scope(self.name + "_last"):
            if not self.fast:
                everything = lax.all_gather(a, "seq").astype(F32)
                index = jnp.arange(at.seq).reshape((-1,) + (1,) * a.ndim)
                reached = index > at.s if reverse else index < at.s
                return jnp.sum(jnp.where(reached, everything, 0.0), axis=0).astype(BF)
            inner = (at.x == 0) if reverse else (at.x == 1)
            got = [after(g, *wait).astype(F32) for g in self.done]
            self.total = got[0] + got[1] + got[2]
            mine = (self.total + jnp.where(inner, self.got.astype(F32), 0.0)).astype(BF)
            send = (self.total + jnp.where(inner, 0.0, self.own.astype(F32))).astype(BF)
            return ordered(at.x == 0, mine, at.swap_x(send), 0)


class Everywhere:
    def __init__(self, at, a):
        self.at, self.a, self.done = at, a, ()

    def step(self, stride, *wait):
        if self.at.fast:
            with jax.named_scope("everywhere"):
                got = self.at.flip(after(self.a, *wait), stride)
                self.a = self.a + got
                self.done = (got,)

    def step_z(self, *wait):
        at = self.at
        with jax.named_scope("everywhere"):
            if not at.fast:
                return lax.psum(self.a, BOTH)
            a = after(self.a, *wait)
            rel = jnp.stack([a] + [at.turn_z(a, by) for by in (3, 2, 1)])
            by_z = lax.dynamic_slice_in_dim(jnp.concatenate([rel, rel]), (4 - at.z) % 4, 4)
            return (by_z[0] + by_z[1]) + (by_z[2] + by_z[3])


VMEM = pltpu.VMEM
SCALAR = pl.BlockSpec(memory_space=pltpu.SMEM)
WHOLE = pl.BlockSpec(memory_space=VMEM)


def params(mib):
    return pltpu.CompilerParams(vmem_limit_bytes=60 * 2**20)


def cost(micros):
    return pl.CostEstimate(flops=int(micros * 1e9), bytes_accessed=int(micros * 1e6), transcendentals=0)


def tdot(a, b):
    return lax.dot_general(a, b, (((0,), (0,)), ((), ())), preferred_element_type=F32)


def dot_t(a, b):
    return lax.dot_general(a, b, (((1,), (1,)), ((), ())), preferred_element_type=F32)


def dot(a, b):
    return jnp.dot(a, b, preferred_element_type=F32)


def parts(a):
    high = a.astype(BF)
    return high, (a - high.astype(F32)).astype(BF)


def left_lanes(shape):
    return lax.broadcasted_iota(jnp.int32, shape, len(shape) - 1) % 128 < 64


def two_heads(a):
    first = left_lanes(a.shape)
    wide = a.astype(F32)
    return jnp.concatenate(
        [jnp.where(first, wide, 0.0), jnp.where(first, 0.0, wide)], axis=0
    ).astype(BF)


def fold(a):
    half = a.shape[0] // 2
    return jnp.where(left_lanes((half, a.shape[1])), a[:half], a[half:])


def head_ones():
    row = lax.broadcasted_iota(jnp.int32, (128, 128), 0) // 64
    col = lax.broadcasted_iota(jnp.int32, (128, 128), 1) // 64
    return jnp.where(row == col, 1.0, 0.0).astype(BF)


def head_sums(a, ones):
    high, low = parts(a)
    return dot(high, ones) + dot(low, ones)


def features(s, g_high, g_low):
    high, low = parts(jnp.concatenate([s, s * s], axis=1))
    return jnp.exp(dot(high, g_high) + dot(high, g_low) + dot(low, g_high)) * 0.125


def features_back(t, s, g_high, g_low, ones, scale):
    high, low = parts(t)
    f_high, f_low = g_high[:128], g_low[:128]
    back = dot_t(high, f_high) + dot_t(high, f_low) + dot_t(low, f_high)
    return ((back - s * (dot(high, ones) + dot(low, ones))) * scale).astype(BF)


def lanes(p):
    return slice(p * 128, (p + 1) * 128)


def key_kernel(c_ref, tok, mine, other, gh, gl, s_out, phi_out, feat_out, v_out, state_out, vec_out):
    first = c_ref[0] == 0
    pairs, block = gh.shape[0], 128
    hw = pairs * 64
    eye = jnp.where(
        lax.broadcasted_iota(jnp.int32, (128, 128), 0) == lax.broadcasted_iota(jnp.int32, (128, 128), 1), 1.0, 0.0
    ).astype(BF)
    vecs = dot_t(eye, mine[:, 3 * hw :])[:16]
    vec_out[...] = vecs
    a = dot(tok[...], mine[:, hw : 3 * hw])
    b = dot(tok[...], other[:, hw : 3 * hw])
    left, right = jnp.where(first, a, b), jnp.where(first, b, a)
    scale = 64 ** (-0.25)
    for p in range(pairs):
        half, at = (left, p * 128) if p < pairs // 2 else (right, p * 128 - hw)
        s = (half[:, at : at + 128] + vecs[1:2, lanes(p)]) * scale
        v = (half[:, hw + at : hw + at + 128] + vecs[2:3, lanes(p)]).astype(BF)
        phi = features(s, gh[p], gl[p])
        k = phi.astype(BF)
        s_out[:, lanes(p)] = s
        phi_out[:, lanes(p)] = phi
        feat_out[:, lanes(p)] = k
        v_out[:, lanes(p)] = v
        for r in range(tok.shape[0] // block):
            rows = slice(r * block, (r + 1) * block)
            state_out[r, :64, lanes(p)] = fold(tdot(k[rows], v[rows])).astype(BF)
            total = jnp.sum(k[rows].astype(F32), axis=0, keepdims=True)
            state_out[r, 64:, lanes(p)] = jnp.broadcast_to(total, (16, 128)).astype(BF)


def query_kernel(c_ref, tok, mine, other, vec, gh, gl, s_out, phi_out, feat_out):
    first = c_ref[0] == 0
    pairs = gh.shape[0]
    hw = pairs * 64
    a, b = dot(tok[...], mine[:, :hw]), dot(tok[...], other[:, :hw])
    left, right = jnp.where(first, a, b), jnp.where(first, b, a)
    for p in range(pairs):
        half, at = (left, p * 128) if p < pairs // 2 else (right, p * 128 - hw)
        s = (half[:, at : at + 128] + vec[0:1, lanes(p)]) * 64 ** (-0.25)
        phi = features(s, gh[p], gl[p])
        s_out[:, lanes(p)] = s
        phi_out[:, lanes(p)] = phi
        feat_out[:, lanes(p)] = phi.astype(BF)


def halo_kernel(c_ref, halo, mine, other, vec, gh, gl, hk_out, hv_out):
    first, inner = c_ref[0] == 0, c_ref[1] > 0
    pairs = gh.shape[0]
    hw = pairs * 64
    a, b = dot(halo[...], mine[:, hw : 3 * hw]), dot(halo[...], other[:, hw : 3 * hw])
    left, right = jnp.where(first, a, b), jnp.where(first, b, a)
    for p in range(pairs):
        half, at = (left, p * 128) if p < pairs // 2 else (right, p * 128 - hw)
        s = (half[:, at : at + 128] + vec[1:2, lanes(p)]) * 64 ** (-0.25)
        v = half[:, hw + at : hw + at + 128] + vec[2:3, lanes(p)]
        hk_out[:, lanes(p)] = jnp.where(inner, features(s, gh[p], gl[p]), 0.0).astype(BF)
        hv_out[:, lanes(p)] = jnp.where(inner, v, 0.0).astype(BF)


def window_weights(base):
    turned = pltpu.roll(jnp.broadcast_to(base, (128, 256)), 0, 1, stride=1, stride_axis=0)
    row = lax.broadcasted_iota(jnp.int32, (128, 256), 0)
    col = lax.broadcasted_iota(jnp.int32, (128, 256), 1)
    return jnp.where(col > row + 128, 0.0, turned - jnp.where(col < 128, base[:, 255:256], 0.0))


def pair_at(step, c, pairs):
    return (step + (pairs // 2) * (1 - c)) % pairs


def block_diagonal(packed):
    return two_heads(packed)


def attention_kernel(q, k, v, hk, hv, table, state, far, context_out, turned_out, ratio_out, denom_out):
    ones = head_ones()
    wmat = jnp.concatenate([window_weights(table[0, 0:1]), window_weights(table[0, 1:2])], axis=0)
    far_row = far[0:1]
    for r in range(q.shape[0] // 128):
        rows = slice(r * 128, (r + 1) * 128)
        qr = q[rows]
        kw = jnp.concatenate([hk[rows], k[rows]], axis=0)
        vw = jnp.concatenate([hv[rows], v[rows]], axis=0)
        weighted = dot_t(two_heads(qr), kw) * wmat
        numer = fold(dot(weighted.astype(BF), vw))
        near = jnp.sum(weighted, axis=1, keepdims=True)
        near = fold(jnp.broadcast_to(near, (256, 128)))
        bd = block_diagonal(state[r, :64])
        total = state[r, 64:80].astype(F32)[0:1]
        numer = numer + far_row * dot(qr, bd)
        denom = near + far_row * head_sums(qr.astype(F32) * total, ones)
        ratio = numer / denom
        context_out[rows] = ratio.astype(BF)
        turned_out[:, rows] = ratio.T.astype(BF)
        ratio_out[rows] = ratio
        denom_out[rows] = denom


def normed(x):
    centred = x - jnp.mean(x, axis=-1, keepdims=True)
    rstd = lax.rsqrt(jnp.mean(centred * centred, axis=-1, keepdims=True) + EPS)
    return centred * rstd, rstd


def norm_back(dy, xhat, rstd, gain):
    d = dy * gain
    return rstd * (
        d - jnp.mean(d, axis=-1, keepdims=True) - xhat * jnp.mean(d * xhat, axis=-1, keepdims=True)
    )


def col_sums(a):
    return jnp.sum(a, axis=0, keepdims=True)


def middle_kernel(
    count, context, tok, cot, vec, bu, ratio, denom, q, state, far, rest_hbm, *more,
):
    blocks_hbm, more = more[:count], more[count:]
    (
        out, dresid_out, dattn_out, dn_out, later_out, sums_out, near_out, du_sums_out, down_hbm, up_hbm,
        w, wd, gp, grads, in_sems, out_sems,
    ) = more
    width, step = tok.shape[1], wd.shape[1]
    hw = width // 2
    loads = []
    for i in range(count):
        loads.append(pltpu.make_async_copy(blocks_hbm[i], w.at[i], in_sems.at[i]))
    for i in range(count):
        wd_block = rest_hbm.at[pl.ds(i * step, step), pl.ds(0, width)]
        loads.append(pltpu.make_async_copy(wd_block, wd.at[i], in_sems.at[count + i]))
    for load in loads:
        load.start()
    for load in loads[:count]:
        load.wait()
    attn = jnp.concatenate([dot(context[...], w[i, :, step:]) for i in range(count)], axis=1)
    xhat, rstd = normed(tok[...].astype(F32) + attn + vec[3:4])
    hidden = xhat * vec[4:5] + vec[5:6]
    h_low = hidden.astype(BF)
    lower = hidden + vec[6:7]
    actives = []
    for i in range(count):
        cols = slice(i * step, (i + 1) * step)
        upper = dot(h_low, w[i, :, :step]) + bu[:, cols]
        cdf = 0.5 * (1.0 + lax.erf(upper * 2.0 ** (-0.5)))
        pdf = jnp.exp(-0.5 * upper * upper) * (2.0 * math.pi) ** (-0.5)
        gp[:, cols] = (cdf + upper * pdf).astype(BF)
        actives.append((upper * cdf).astype(BF))
        loads[count + i].wait()
        lower = lower + dot(actives[-1], wd[i])
    xhat2, rstd2 = normed(lower)
    gain2 = vec[7:8]
    out[...] = xhat2 * gain2 + vec[8:9]
    dy = cot[...].astype(F32)
    d_hidden = norm_back(dy, xhat2, rstd2, gain2)
    d_low = d_hidden.astype(BF)
    sums_out[0:1] = col_sums(d_low.astype(F32))
    sums_out[1:2] = col_sums(dy * xhat2)
    sums_out[2:3] = col_sums(dy)
    stores = []
    for i in range(count):
        cols = slice(i * step, (i + 1) * step)
        d_upper = (dot_t(d_low, wd[i]) * gp[:, cols].astype(F32)).astype(BF)
        du_sums_out[:, cols] = jnp.broadcast_to(col_sums(d_upper.astype(F32)), (8, step))
        d_hidden = d_hidden + dot_t(d_upper, w[i, :, :step])
        grads[2 * i] = tdot(h_low, d_upper).astype(BF)
        stores.append(pltpu.make_async_copy(grads.at[2 * i], up_hbm.at[i], out_sems.at[2 * i]))
        stores[-1].start()
        grads[2 * i + 1] = tdot(actives[i], d_low).astype(BF)
        block = down_hbm.at[pl.ds(i * step, step), pl.ds(0, width)]
        stores.append(pltpu.make_async_copy(grads.at[2 * i + 1], block, out_sems.at[2 * i + 1]))
        stores[-1].start()
    d_resid = norm_back(d_hidden, xhat, rstd, vec[4:5])
    dresid_out[...] = d_resid
    d_attn = d_resid.astype(BF)
    dattn_out[...] = d_attn
    sums_out[3:4] = col_sums(d_attn.astype(F32))
    sums_out[4:5] = col_sums(d_hidden * xhat)
    sums_out[5:6] = col_sums(d_hidden)
    part = width // count
    d_context = sum(dot_t(d_resid[:, i * part : (i + 1) * part].astype(BF), w[i, :, step:]) for i in range(count))
    ones = head_ones()
    pick = jnp.where(
        lax.broadcasted_iota(jnp.int32, (width, 128), 0) == 64 * lax.broadcasted_iota(jnp.int32, (width, 128), 1), 1.0, 0.0
    ).astype(BF)
    all_denoms = []
    for p in range(width // 128):
        dc = d_context[:, lanes(p)]
        inverse = 1.0 / denom[:, lanes(p)]
        dn = (dc * inverse).astype(BF)
        dd = (-head_sums(dc * ratio[:, lanes(p)], ones) * inverse).astype(BF)
        dn_out[:, lanes(p)] = dn
        all_denoms.append(dd)
        near = jnp.zeros((1, 128), F32)
        for r in range(tok.shape[0] // 128):
            rows = slice(r * 128, (r + 1) * 128)
            qr = q[rows, lanes(p)]
            packed = fold(tdot(qr, dn[rows]))
            total = col_sums(qr.astype(F32) * dd[rows].astype(F32))
            far_row = far[0:1, lanes(p)]
            later_out[r, :64, lanes(p)] = (far_row * packed).astype(BF)
            later_out[r, 64:, lanes(p)] = jnp.broadcast_to(far_row * total, (16, 128)).astype(BF)
            held = state[r, :, lanes(p)].astype(F32)
            near = near + col_sums(held[:64] * packed) + held[64:65] * total
        near_out[:, lanes(p)] = jnp.broadcast_to(near, (8, 128))
    dn_out[:, width:] = dot(jnp.concatenate(all_denoms, axis=1), pick).astype(BF)
    for store in stores:
        store.wait()


def spread(dn, p):
    lane = lax.broadcasted_iota(jnp.int32, dn.shape, 1)
    wide = dn.astype(F32)
    return [jnp.sum(jnp.where(lane == 2 * p + h, wide, 0.0), axis=1, keepdims=True) for h in (0, 1)]


def query_back_kernel(
    c_ref, tok, context, dattn, q, k, v, hk, hv, dn, dd, table, state, far, phi, s, gh, gl, near,
    dq_out, keep_out, send_out, pos_out, sums_out,
):
    steps = pl.num_programs(0)
    p = pair_at(pl.program_id(0), c_ref[0], steps)
    ones = head_ones()
    wmat = jnp.concatenate([window_weights(table[0, 0:1]), window_weights(table[0, 1:2])], axis=0)
    far_row = far[0:1]
    first = left_lanes((128, 128))
    pieces = jnp.zeros((256, 256), F32)
    grads = []
    for r in range(q.shape[0] // 128):
        rows = slice(r * 128, (r + 1) * 128)
        kw = jnp.concatenate([hk[rows], k[rows]], axis=0)
        vw = jnp.concatenate([hv[rows], v[rows]], axis=0)
        scores = dot_t(two_heads(q[rows]), kw)
        d0, d1 = spread(dd[rows], p)
        dnr = dn[rows]
        dw = dot_t(two_heads(dnr), vw) + jnp.concatenate([d0, d1], axis=0)
        pieces = pieces + dw * scores
        ds = (dw * wmat).astype(BF)
        bd = block_diagonal(state[r, :64])
        total = state[r, 64:80].astype(F32)[0:1]
        dq = fold(dot(ds, kw)) + far_row * (dot_t(dnr, bd) + jnp.where(first, d0, d1) * total)
        grads.append(
            features_back(dq * phi[rows], s[rows], gh[0], gl[0], ones, 64 ** (-0.25))
        )
    dq = jnp.concatenate(grads, axis=0)
    dq_out[...] = dq
    sums_out[...] = jnp.broadcast_to(col_sums(dq.astype(F32)), sums_out.shape)
    grad = jnp.concatenate([dot(tok[...], dq), dot(context[...], dattn[...])], axis=1).astype(BF)
    place_half(grad, keep_out, send_out)
    row = lax.broadcasted_iota(jnp.int32, (256, 256), 0)
    col = lax.broadcasted_iota(jnp.int32, (256, 256), 1)
    mirror = jnp.where(row + col == 255, 1.0, 0.0).astype(BF)
    high, low = parts(jnp.where(col <= row % 128 + 128, pieces, 0.0))
    mirrored = dot(high, mirror) + dot(low, mirror)
    lane = lax.broadcasted_iota(jnp.int32, (1, 256), 1)
    for h in (0, 1):
        rows = slice(h * 128, (h + 1) * 128)
        by_distance = col_sums(pltpu.roll(mirrored[rows], 129, 1, stride=1, stride_axis=0))
        plain = col_sums(pieces[rows])
        apart = jnp.where(lane >= 128, by_distance, 0.0) - jnp.where(lane < 128, plain, 0.0)
        state_part = jnp.where(lane[:, :128] // 64 == h, near[0:1], 0.0)
        far_sum = jnp.sum(apart, axis=1, keepdims=True) + jnp.sum(state_part, axis=1, keepdims=True)
        pos_out[0, h : h + 1] = jnp.where(lane < 128, by_distance, far_sum)


def place_half(grad, keep_out, send_out):
    early = pl.program_id(0) < pl.num_programs(0) // 2

    @pl.when(early)
    def _():
        send_out[...] = grad

    @pl.when(jnp.logical_not(early))
    def _():
        keep_out[...] = grad


def key_back_kernel(
    c_ref, tok, q, k, v, dn, dd, qn, dnn, ddn, table, later, phi, s, gh, gl, rows_in,
    dk_out, dv_out, keep_out, send_out, small_out,
):
    p = pair_at(pl.program_id(0), c_ref[0], pl.num_programs(0))
    ones = head_ones()
    first, second = window_weights(table[0, 0:1]), window_weights(table[0, 1:2])
    tables = jnp.concatenate([first[:, 128:], second[:, 128:], first[:, :128], second[:, :128]], axis=0)
    dks, dvs = [], []
    for r in range(q.shape[0] // 128):
        rows = slice(r * 128, (r + 1) * 128)
        kr, vr = k[rows], v[rows]
        q4 = jnp.concatenate([two_heads(q[rows]), two_heads(qn[rows])], axis=0)
        dn4 = jnp.concatenate([two_heads(dn[rows]), two_heads(dnn[rows])], axis=0)
        dd4 = jnp.concatenate(spread(dd[rows], p) + spread(ddn[rows], p), axis=0)
        w = (dot_t(q4, kr) * tables).astype(BF)
        ds = ((dot_t(dn4, vr) + dd4) * tables).astype(BF)
        bd = block_diagonal(later[r, :64])
        total = later[r, 64:80].astype(F32)[0:1]
        dk = tdot(ds, q4) + dot_t(vr, bd) + total
        dvs.append((tdot(w, dn4) + dot(kr, bd)).astype(BF))
        dks.append(features_back(dk * phi[rows], s[rows], gh[0], gl[0], ones, 64 ** (-0.25)))
    dk, dv = jnp.concatenate(dks, axis=0), jnp.concatenate(dvs, axis=0)
    dk_out[...] = dk
    dv_out[...] = dv
    place_half(jnp.concatenate([dot(tok[...], dk), dot(tok[...], dv)], axis=1).astype(BF), keep_out, send_out)
    row = lax.broadcasted_iota(jnp.int32, (16, 128), 0)
    lane = lax.broadcasted_iota(jnp.int32, (16, 128), 1)
    late = jnp.where(row == 1, col_sums(dk.astype(F32)), 0.0) + jnp.where(row == 2, col_sums(dv.astype(F32)), 0.0)
    small_out[...] = tdot((rows_in[...] + late).astype(BF), jnp.where(row == lane, 1.0, 0.0).astype(BF)).astype(BF)


def tokens_kernel(c_ref, dresid, dq, dk, dv, mine, other, out):
    first = c_ref[0] == 0
    hw = dq.shape[1] // 2
    total = dresid[...]
    for i, d in enumerate((dq, dk, dv)):
        wide = d[...].astype(F32)
        a = jnp.where(first, wide[:, :hw], wide[:, hw:]).astype(BF)
        b = jnp.where(first, wide[:, hw:], wide[:, :hw]).astype(BF)
        cols = slice(i * hw, (i + 1) * hw)
        total = total + dot_t(a, mine[:, cols]) + dot_t(b, other[:, cols])
    out[...] = total


def unpack_kernel(packed, down_out, up_out):
    own, width = up_out.shape[0], down_out.shape[1]
    step = packed.shape[1] - width
    wide = packed[...].astype(F32)
    down_out[...] = wide[:, :width]
    for i in range(packed.shape[0] // own):
        up_out[:, i * step : (i + 1) * step] = wide[i * own : (i + 1) * own, width:]


def feature_blocks(matrix):
    heads, size, feats = matrix.shape
    zero = jnp.zeros((heads // 2, size, feats), F32)
    even, odd = matrix[0::2], matrix[1::2]
    half = jnp.full(zero.shape, -0.5, F32)
    blocks = jnp.concatenate(
        [
            jnp.concatenate([even, zero], axis=2),
            jnp.concatenate([zero, odd], axis=2),
            jnp.concatenate([half, zero], axis=2),
            jnp.concatenate([zero, half], axis=2),
        ],
        axis=1,
    )
    high = lax.reduce_precision(blocks, 8, 7)
    return high.astype(BF), (blocks - high).astype(BF)


def on_device(
    tokens,
    query_weight,
    query_bias,
    key_weight,
    key_bias,
    value_weight,
    value_bias,
    output_weight,
    output_bias,
    first_gain,
    first_shift,
    up_weight,
    up_bias,
    down_weight,
    down_bias,
    second_gain,
    second_shift,
    position_bias,
    feature_matrix,
    cotangent,
):
    at = Place()
    rows, block, width = tokens.shape
    heads, size, feats = feature_matrix.shape
    window = position_bias.shape[1] - 1
    pairs = heads // 2
    n = rows * block
    hw = width // 2
    ff = up_weight.shape[1]
    hf = ff // 2
    own = query_weight.shape[0]
    up_own = up_bias.shape[0] // own
    tok = tokens.reshape(n, width)
    cot = cotangent.reshape(n, width)
    flags = jnp.stack([at.c, at.s]).astype(jnp.int32)

    def arr(shape, kind):
        return jax.ShapeDtypeStruct(shape, kind)

    halo_tok = at.along(tok, 1)
    tok_t = tok.T

    vectors = (
        query_bias, key_bias, value_bias, output_bias, first_gain, first_shift,
        down_bias, second_gain, second_shift,
    )
    count = len(vectors)
    small = jnp.concatenate(vectors + (up_bias,)).reshape(count + up_own, own).T
    small = jnp.pad(small, ((0, 0), (0, 128 - small.shape[1])))
    slices = down_weight.shape[0] // own
    step, wo_step = ff // slices, width // slices

    def stacked(a):
        return jnp.concatenate(jnp.split(a, slices, axis=1), axis=0)

    rest = lax.all_gather(
        jnp.concatenate([down_weight, stacked(up_weight), stacked(output_weight)], axis=1), BOTH, axis=0, tiled=True
    )
    g1 = Gather(
        at,
        "qkv",
        jnp.concatenate([query_weight[:, :hw], key_weight[:, :hw], value_weight[:, :hw]], axis=1),
        jnp.concatenate([query_weight[:, hw:], key_weight[:, hw:], value_weight[:, hw:]], axis=1),
        small,
    )
    exp_bias = jnp.exp(position_bias)
    table = jnp.concatenate(
        [exp_bias[:, ::-1], jnp.broadcast_to(exp_bias[:, window:], (heads, block - 1))], axis=1
    ).reshape(pairs, 2, window + block)
    table = jnp.pad(table, ((0, 0), (0, 6), (0, 0)))
    far = jnp.broadcast_to(jnp.repeat(exp_bias[:, window], size)[None], (8, width))
    gh, gl = feature_blocks(feature_matrix)

    g1.step_core()
    g1.step_z()
    g1.step_one()
    g1.step_two()
    m1, o1 = g1.step_last(table, far, gh, gl, tok_t)

    wide32, wide16 = arr((n, width), F32), arr((n, width), BF)
    sums = arr((rows, 80, width), BF)
    sk, k_phi, k, v, local, vec = pl.pallas_call(
        key_kernel,
        out_shape=(wide32, wide32, wide16, wide16, sums, arr((16, width), F32)),
        in_specs=[SCALAR] + [WHOLE] * 5,
        out_specs=(WHOLE,) * 6,
        compiler_params=params(48),
        cost_estimate=cost(5),
        name="keys",
    )(flags, tok, m1, o1, gh, gl)
    scan = Before(at, "before", local, False)
    scan.step_beside()
    sq, q_phi, q = pl.pallas_call(
        query_kernel,
        out_shape=(wide32, wide32, wide16),
        in_specs=[SCALAR] + [WHOLE] * 6,
        out_specs=(WHOLE,) * 3,
        compiler_params=params(48),
        cost_estimate=cost(3),
        name="queries",
    )(flags, tok, m1, o1, vec, gh, gl)
    scan.step_z(q)
    hk, hv = pl.pallas_call(
        halo_kernel,
        out_shape=(wide16, wide16),
        in_specs=[SCALAR] + [WHOLE] * 6,
        out_specs=(WHOLE,) * 2,
        compiler_params=params(48),
        cost_estimate=cost(2),
        name="halo",
    )(flags, after(halo_tok, *scan.done), m1, o1, vec, gh, gl)
    q_next = at.along(q, -1)
    before = scan.step_last(hk, q_next)
    b_u = m1[:, 3 * hw + count : 3 * hw + count + up_own].reshape(at.n, own, up_own)
    b_u = jnp.swapaxes(after(b_u, hk), 1, 2).reshape(1, ff).astype(F32)

    def columns(height=n):
        return pl.BlockSpec((height, 128), lambda p, *_: (0, p))

    table_spec = pl.BlockSpec((1, 8, window + block), lambda p, *_: (p, 0, 0))
    sums_spec = pl.BlockSpec((rows, 80, 128), lambda p, *_: (0, 0, p))
    g_spec = pl.BlockSpec((1, 256, 128), lambda p, *_: (p, 0, 0))
    tok_spec = pl.BlockSpec((width, n), lambda p, *_: (0, 0))
    dd_spec = pl.BlockSpec((n, 128), lambda p, *_: (0, pairs))
    context, context_t, ratio, denom = pl.pallas_call(
        attention_kernel,
        grid=(pairs,),
        out_shape=(wide16, arr((width, n), BF), wide32, wide32),
        in_specs=[columns()] * 5 + [table_spec, sums_spec, columns(8)],
        out_specs=(columns(), pl.BlockSpec((128, n), lambda p, *_: (p, 0)), columns(), columns()),
        compiler_params=params(32),
        cost_estimate=cost(5),
        name="attention",
    )(q, k, v, hk, hv, table, before, far)

    split = rest.reshape(at.n, slices, own, rest.shape[1])
    blocks = [split[:, i, :, width:].reshape(width, step + wo_step) for i in range(slices)]
    away = pl.BlockSpec(memory_space=pl.ANY)
    out, d_resid, d_attn, dn, local, sums2, near, du_sums, g_down, g_up = pl.pallas_call(
        functools.partial(middle_kernel, slices),
        out_shape=(
            wide32, wide32, wide16, arr((n, width + 128), BF), sums, arr((8, width), F32), arr((8, width), F32),
            arr((8, ff), F32), arr((ff, width + step), BF), arr((slices, width, step), BF),
        ),
        in_specs=[WHOLE] * 10 + [away] * (1 + slices),
        out_specs=(WHOLE,) * 8 + (away,) * 2,
        scratch_shapes=[
            VMEM((slices, width, step + wo_step), BF),
            VMEM((slices, step, width), BF),
            VMEM((n, ff), BF),
            VMEM((2 * slices, width, step), BF),
            pltpu.SemaphoreType.DMA((2 * slices,)),
            pltpu.SemaphoreType.DMA((2 * slices,)),
        ],
        compiler_params=pltpu.CompilerParams(vmem_limit_bytes=44 * 2**20),
        cost_estimate=cost(20),
        name="middle",
    )(context, tok, cot, vec, b_u, ratio, denom, q, before, far, rest, *blocks)
    g_up = jnp.swapaxes(g_up.reshape(slices, at.n, own, step), 0, 1).reshape(ff, step)
    g_rest = lax.dynamic_update_slice(g_down, g_up, (0, width))
    s_rest = lax.psum_scatter(g_rest, BOTH, scatter_dimension=0, tiled=True)
    if own % 8 == 0:
        s_d, s_u = pl.pallas_call(
            unpack_kernel,
            out_shape=(arr((slices * own, width), F32), arr((own, ff), F32)),
            in_specs=[WHOLE],
            out_specs=(WHOLE,) * 2,
            compiler_params=params(48),
            cost_estimate=cost(1),
            name="unpack",
        )(s_rest)
    else:
        s_d = s_rest[:, :width].astype(F32)
        s_u = jnp.concatenate(jnp.split(s_rest[:, width:].astype(F32), slices, axis=0), axis=1)
    scan = Before(at, "later", local, True)
    scan.step_beside()
    dn_next = at.along(dn, -1)

    def turned(p, c):
        return pair_at(p, c[0], pairs)

    cols = pl.BlockSpec((n, 128), lambda p, c: (0, turned(p, c)))
    cols8 = pl.BlockSpec((8, 128), lambda p, c: (0, turned(p, c)))
    by_pair = pl.BlockSpec((1, 8, window + block), lambda p, c: (turned(p, c), 0, 0))
    sums_by_pair = pl.BlockSpec((rows, 80, 128), lambda p, c: (0, 0, turned(p, c)))
    g_by_pair = pl.BlockSpec((1, 256, 128), lambda p, c: (turned(p, c), 0, 0))
    kept = pl.BlockSpec((width, 256), lambda p, c: (0, jnp.maximum(p - pairs // 2, 0)))
    sent = pl.BlockSpec((width, 256), lambda p, c: (0, jnp.minimum(p, pairs // 2 - 1)))
    half = arr((width, 2 * hw), BF)
    dq, keep1, send1, pos, sums_q = pl.pallas_call(
        query_back_kernel,
        grid_spec=pltpu.PrefetchScalarGridSpec(
            num_scalar_prefetch=1,
            grid=(pairs,),
            in_specs=[tok_spec] * 2 + [cols] * 7 + [dd_spec, by_pair, sums_by_pair, cols8]
            + [cols] * 2 + [g_by_pair] * 2 + [cols8],
            out_specs=(cols, kept, sent, by_pair, cols8),
        ),
        out_shape=(wide16, half, half, arr((pairs, 8, 256), F32), arr((8, width), F32)),
        compiler_params=params(32),
        cost_estimate=cost(0.001),
        name="query_back",
    )(flags, after(tok_t, *scan.done, g_rest), context_t, d_attn, q, k, v, hk, hv, dn, dn, table, before, far, q_phi, sq, gh, gl, near)
    scan.step_z()
    later = scan.step_last(dq, dn_next)
    everywhere = Everywhere(at, exp_bias * pos[:, :2, : window + 1].reshape(heads, window + 1))
    everywhere.step(1)
    du = du_sums[0].reshape(at.n, up_own, own)
    du = jnp.swapaxes(du, 0, 1).reshape(up_own, width)
    nil = jnp.zeros((2, width), F32)
    early = jnp.concatenate([sums_q[:1], nil, sums2[3:6], sums2[:3], du], axis=0)
    early = jnp.pad(early, ((0, 16 - early.shape[0]), (0, 0)))
    dk, dv, keep0, send0, small = pl.pallas_call(
        key_back_kernel,
        grid_spec=pltpu.PrefetchScalarGridSpec(
            num_scalar_prefetch=1,
            grid=(pairs,),
            in_specs=[tok_spec] + [cols] * 4 + [dd_spec] + [cols] * 2
            + [dd_spec, by_pair, sums_by_pair] + [cols] * 2 + [g_by_pair] * 2
            + [pl.BlockSpec((16, 128), lambda p, c: (0, turned(p, c)))],
            out_specs=(cols, cols, kept, sent, pl.BlockSpec((128, 128), lambda p, c: (turned(p, c), 0))),
        ),
        out_shape=(wide16, wide16, half, half, arr((width, 128), BF)),
        compiler_params=params(32),
        cost_estimate=cost(0.001),
        name="key_back",
    )(flags, after(tok_t, *everywhere.done), q, k, v, dn, dn, q_next, dn_next, dn_next, table, later, k_phi, sk, gh, gl, early)

    r0 = Scatter(at, "d_qkv", (keep1, keep0, small), (send1, send0, small))
    r0.step_core()
    everywhere.step(2, dk)
    r0.step_one(*everywhere.done)
    everywhere.step(4, *r0.done)
    r0.step_two(*everywhere.done)
    two0 = r0.done
    r0.step_z()
    position_grad = everywhere.step_z(*two0)
    s_qkv = r0.step_last()
    d_tokens = pl.pallas_call(
        tokens_kernel,
        out_shape=wide32,
        in_specs=[SCALAR] + [WHOLE] * 6,
        out_specs=WHOLE,
        compiler_params=params(40),
        cost_estimate=cost(0.001),
        name="tokens",
    )(flags, d_resid, dq, dk, dv, m1, o1)

    def woven(pair, at):
        return jnp.concatenate(
            [half[:, at + p * 256 : at + p * 256 + 128] for half in pair for p in range(pairs // 2)], axis=1
        )

    s_small = s_qkv[0][:, 4 * hw :]
    bq, bk, bv, bo, sg1, ss1, bd, sg2, ss2 = [s_small[:, i] for i in range(count)]
    bu = s_small[:, count : count + up_own].T.reshape(-1)
    return (
        out.reshape(rows, block, width),
        d_tokens.reshape(rows, block, width),
        woven(s_qkv, 0),
        bq,
        woven(s_qkv, 2 * hw),
        bk,
        woven(s_qkv, 2 * hw + 128),
        bv,
        woven(s_qkv, 128),
        bo,
        sg1,
        ss1,
        s_u,
        bu,
        s_d,
        bd,
        sg2,
        ss2,
        position_grad,
    )


def solution(mesh):
    matrix, vector, split = P(BOTH, None), P(BOTH), P("rows", "seq", None)
    return jax.shard_map(
        on_device,
        mesh=mesh,
        in_specs=(split,)
        + (matrix, vector) * 4
        + (vector, vector)
        + (matrix, vector) * 2
        + (vector, vector)
        + (P(), P(), split),
        out_specs=(split, split)
        + (matrix, vector) * 4
        + (vector, vector)
        + (matrix, vector) * 2
        + (vector, vector)
        + (P(),),
        check_vma=False,
    )
```

```python
import functools
import math

import jax
import jax.numpy as jnp
from jax import lax
from jax.experimental import pallas as pl
from jax.experimental.pallas import tpu as pltpu
from jax.sharding import PartitionSpec as P

BOTH = ("seq", "rows")
EPS = 1e-06
BF = jnp.bfloat16
F32 = jnp.float32


class Place:
    def __init__(self):
        self.seq = lax.axis_size("seq")
        self.rows = lax.axis_size("rows")
        self.n = self.seq * self.rows
        self.fast = self.seq == 8 and self.rows == 4
        me = lax.axis_index(BOTH)
        self.c = me % 2
        self.y = (me // 2) % 2
        self.x = (me // 4) % 2
        self.z = me // 8
        self.s = lax.axis_index("seq")

    def flip(self, a, stride):
        return lax.ppermute(a, BOTH, [(d, d ^ stride) for d in range(self.n)])

    def swap_c(self, a):
        return self.flip(a, 1)

    def swap_y(self, a):
        return self.flip(a, 2)

    def swap_x(self, a):
        return self.flip(a, 4)

    def turn_z(self, a, by):
        return lax.ppermute(a, BOTH, [(d, (d + 8 * by) % self.n) for d in range(self.n)])

    def along(self, a, by):
        pairs = [(i, i + by) for i in range(self.seq) if 0 <= i + by < self.seq]
        return lax.ppermute(a, "seq", pairs)


def after(a, *others):
    return lax.optimization_barrier((a, others))[0]


def ordered(first, mine, other, axis):
    return jnp.where(
        first, jnp.stack([mine, other], axis=axis), jnp.stack([other, mine], axis=axis)
    )


class Gather:
    def __init__(self, at, name, left, right, small):
        self.at, self.name = at, name
        self.r, self.half = left.shape
        self.first = at.c == 0
        self.left, self.right, self.small = left, right, small
        self.done = ()

    def step_core(self, *wait):
        if not self.at.fast:
            return
        with jax.named_scope(self.name + "_core"):
            got = self.at.swap_c(after(jnp.where(self.first, self.right, self.left), *wait))
            kept = jnp.where(self.first, self.left, self.right)
            piece = ordered(self.first, kept, got, 0)
            mine = after(self.small, piece)
            small = ordered(self.first, mine, self.at.swap_c(mine), 0)
            self.half += self.small.shape[1]
            self.piece = jnp.concatenate([piece, small], axis=2).reshape(2 * self.r, self.half)
            self.done = (got,)

    def step_z(self, *wait):
        if not self.at.fast:
            return
        at = self.at
        with jax.named_scope(self.name + "_z"):
            piece = after(self.piece, *wait)
            turned = [at.turn_z(piece, by) for by in (1, 2, 3)]
            rel = jnp.stack([piece, turned[2], turned[1], turned[0]])
            by_z = lax.dynamic_slice_in_dim(jnp.concatenate([rel, rel]), (4 - at.z) % 4, 4)
            self.low, self.high = by_z[:2], by_z[2:]
            self.done = tuple(turned)

    def step_one(self, *wait):
        if not self.at.fast:
            return
        at = self.at
        with jax.named_scope(self.name + "_one"):
            low, high = after(self.low, *wait), after(self.high, *wait)
            got = at.swap_x(low), at.swap_y(high)
            self.low = ordered(at.x == 0, low, got[0], 1)
            self.high = ordered(at.y == 0, high, got[1], 1)
            self.done = got

    def step_two(self, *wait):
        if not self.at.fast:
            return
        at = self.at
        with jax.named_scope(self.name + "_two"):
            low, high = after(self.low, *wait), after(self.high, *wait)
            got = at.swap_y(low), at.swap_x(high)
            low = ordered(at.y == 0, low, got[0], 2)
            high = ordered(at.x == 0, high, got[1], 1)
            self.mine = jnp.concatenate([low, high]).reshape(at.n * self.r, self.half)
            self.done = got

    def step_last(self, *wait):
        at = self.at
        with jax.named_scope(self.name + "_last"):
            if not at.fast:
                left = lax.all_gather(jnp.concatenate([self.left, self.small], axis=1), BOTH, axis=0, tiled=True)
                right = lax.all_gather(jnp.concatenate([self.right, self.small], axis=1), BOTH, axis=0, tiled=True)
                return jnp.where(self.first, left, right), jnp.where(self.first, right, left)
            mine = after(self.mine, *wait)
            other = at.swap_c(mine)
            self.done = (other,)
            return mine, other


def half_at(a, index, axis):
    return lax.dynamic_index_in_dim(a, index, axis, keepdims=False)


def plus(kept, got):
    return (kept.astype(F32) + got.astype(F32)).astype(BF)


class Scatter:
    def __init__(self, at, name, keeps, sends):
        self.at, self.name, self.keeps, self.sends = at, name, keeps, sends
        self.total = keeps[0].shape[0]
        self.half = sum(k.shape[1] for k in keeps)
        self.r = self.total // at.n
        self.first = at.c == 0
        self.done = ()

    def step_core(self, *wait):
        if not self.at.fast:
            return
        at = self.at
        with jax.named_scope(self.name + "_core"):
            got = [at.swap_c(after(send, *wait)) for send in self.sends]
            mine = jnp.concatenate([plus(k, g) for k, g in zip(self.keeps, got)], axis=1)
            mine = mine.reshape(4, 2, 2, 2 * self.r, self.half)
            self.low, self.high = mine[:2], mine[2:]
            self.done = tuple(got)

    def step_one(self, *wait):
        if not self.at.fast:
            return
        at = self.at
        with jax.named_scope(self.name + "_one"):
            low, high = after(self.low, *wait), after(self.high, *wait)
            got = at.swap_y(half_at(low, 1 - at.y, 2)), at.swap_x(half_at(high, 1 - at.x, 1))
            self.low = plus(half_at(low, at.y, 2), got[0])
            self.high = plus(half_at(high, at.x, 1), got[1])
            self.done = got

    def step_two(self, *wait):
        if not self.at.fast:
            return
        at = self.at
        with jax.named_scope(self.name + "_two"):
            low, high = after(self.low, *wait), after(self.high, *wait)
            got = at.swap_x(half_at(low, 1 - at.x, 1)), at.swap_y(half_at(high, 1 - at.y, 1))
            low = plus(half_at(low, at.x, 1), got[0])
            high = plus(half_at(high, at.y, 1), got[1])
            self.by_z = jnp.concatenate([low, high])
            self.done = got

    def step_z(self, *wait):
        if not self.at.fast:
            return
        at = self.at
        with jax.named_scope(self.name + "_z"):
            by_z = after(self.by_z, *wait)
            got = [at.turn_z(half_at(by_z, (at.z + by) % 4, 0), by) for by in (1, 2, 3)]
            total = half_at(by_z, at.z, 0).astype(F32) + got[0].astype(F32) + got[1].astype(F32) + got[2].astype(F32)
            self.piece = total.reshape(2, self.r, self.half)
            self.done = tuple(got)

    def step_last(self, *wait):
        at = self.at
        with jax.named_scope(self.name + "_last"):
            if not at.fast:
                keep, send = jnp.concatenate(self.keeps, axis=1), jnp.concatenate(self.sends, axis=1)
                left = jnp.where(self.first, keep, send).astype(F32)
                right = jnp.where(self.first, send, keep).astype(F32)
                return (
                    lax.psum_scatter(left, BOTH, scatter_dimension=0, tiled=True),
                    lax.psum_scatter(right, BOTH, scatter_dimension=0, tiled=True),
                )
            piece = after(self.piece, *wait)
            stays = half_at(piece, at.c, 0)
            got = at.swap_c(half_at(piece, 1 - at.c, 0))
            self.done = (got,)
            return jnp.where(self.first, stays, got), jnp.where(self.first, got, stays)


class Before:
    def __init__(self, at, name, a, reverse):
        self.at, self.name, self.a, self.reverse = at, name, a, reverse
        self.fast = at.fast and a.shape[0] == 2
        self.done = ()

    def step_beside(self):
        if self.fast:
            at = self.at
            with jax.named_scope(self.name + "_beside"):
                self.got = at.swap_x(half_at(self.a, 1 - at.x, 0))
                self.own = half_at(self.a, at.x, 0)
                self.pair = plus(self.own, self.got)
                self.done = (self.got,)

    def step_z(self, *wait):
        if self.fast:
            at = self.at
            with jax.named_scope(self.name + "_z"):
                pair = after(self.pair, *wait)
                got = []
                for by in (1, 2, 3):
                    if self.reverse:
                        pairs = [(d, d - 8 * by) for d in range(8 * by, at.n)]
                    else:
                        pairs = [(d, d + 8 * by) for d in range(at.n - 8 * by)]
                    got.append(lax.ppermute(pair, BOTH, pairs))
                self.done = tuple(got)

    def step_last(self, *wait):
        at, a, reverse = self.at, self.a, self.reverse
        with jax.named_scope(self.name + "_last"):
            if not self.fast:
                everything = lax.all_gather(a, "seq").astype(F32)
                index = jnp.arange(at.seq).reshape((-1,) + (1,) * a.ndim)
                reached = index > at.s if reverse else index < at.s
                return jnp.sum(jnp.where(reached, everything, 0.0), axis=0).astype(BF)
            inner = (at.x == 0) if reverse else (at.x == 1)
            got = [after(g, *wait).astype(F32) for g in self.done]
            self.total = got[0] + got[1] + got[2]
            mine = (self.total + jnp.where(inner, self.got.astype(F32), 0.0)).astype(BF)
            send = (self.total + jnp.where(inner, 0.0, self.own.astype(F32))).astype(BF)
            return ordered(at.x == 0, mine, at.swap_x(send), 0)


class Everywhere:
    def __init__(self, at, a):
        self.at, self.a, self.done = at, a, ()

    def step(self, stride, *wait):
        if self.at.fast:
            with jax.named_scope("everywhere"):
                got = self.at.flip(after(self.a, *wait), stride)
                self.a = self.a + got
                self.done = (got,)

    def step_z(self, *wait):
        at = self.at
        with jax.named_scope("everywhere"):
            if not at.fast:
                return lax.psum(self.a, BOTH)
            a = after(self.a, *wait)
            rel = jnp.stack([a] + [at.turn_z(a, by) for by in (3, 2, 1)])
            by_z = lax.dynamic_slice_in_dim(jnp.concatenate([rel, rel]), (4 - at.z) % 4, 4)
            return (by_z[0] + by_z[1]) + (by_z[2] + by_z[3])


VMEM = pltpu.VMEM
SCALAR = pl.BlockSpec(memory_space=pltpu.SMEM)
WHOLE = pl.BlockSpec(memory_space=VMEM)


def params(mib):
    return pltpu.CompilerParams(vmem_limit_bytes=60 * 2**20)


def cost(micros):
    return pl.CostEstimate(flops=int(micros * 1e9), bytes_accessed=int(micros * 1e6), transcendentals=0)


def tdot(a, b):
    return lax.dot_general(a, b, (((0,), (0,)), ((), ())), preferred_element_type=F32)


def dot_t(a, b):
    return lax.dot_general(a, b, (((1,), (1,)), ((), ())), preferred_element_type=F32)


def dot(a, b):
    return jnp.dot(a, b, preferred_element_type=F32)


def parts(a):
    high = a.astype(BF)
    return high, (a - high.astype(F32)).astype(BF)


def left_lanes(shape):
    return lax.broadcasted_iota(jnp.int32, shape, len(shape) - 1) % 128 < 64


def two_heads(a):
    first = left_lanes(a.shape)
    wide = a.astype(F32)
    return jnp.concatenate(
        [jnp.where(first, wide, 0.0), jnp.where(first, 0.0, wide)], axis=0
    ).astype(BF)


def fold(a):
    half = a.shape[0] // 2
    return jnp.where(left_lanes((half, a.shape[1])), a[:half], a[half:])


def head_ones():
    row = lax.broadcasted_iota(jnp.int32, (128, 128), 0) // 64
    col = lax.broadcasted_iota(jnp.int32, (128, 128), 1) // 64
    return jnp.where(row == col, 1.0, 0.0).astype(BF)


def head_sums(a, ones):
    high, low = parts(a)
    return dot(high, ones) + dot(low, ones)


def features(s, g_high, g_low):
    high, low = parts(jnp.concatenate([s, s * s], axis=1))
    return jnp.exp(dot(high, g_high) + dot(high, g_low) + dot(low, g_high)) * 0.125


def features_back(t, s, g_high, g_low, ones, scale):
    high, low = parts(t)
    f_high, f_low = g_high[:128], g_low[:128]
    back = dot_t(high, f_high) + dot_t(high, f_low) + dot_t(low, f_high)
    return ((back - s * (dot(high, ones) + dot(low, ones))) * scale).astype(BF)


def lanes(p):
    return slice(p * 128, (p + 1) * 128)


def key_kernel(c_ref, tok, mine, other, gh, gl, s_out, phi_out, feat_out, v_out, state_out, vec_out):
    first = c_ref[0] == 0
    pairs, block = gh.shape[0], 128
    hw = pairs * 64
    eye = jnp.where(
        lax.broadcasted_iota(jnp.int32, (128, 128), 0) == lax.broadcasted_iota(jnp.int32, (128, 128), 1), 1.0, 0.0
    ).astype(BF)
    vecs = dot_t(eye, mine[:, 3 * hw :])[:16]
    vec_out[...] = vecs
    a = dot(tok[...], mine[:, hw : 3 * hw])
    b = dot(tok[...], other[:, hw : 3 * hw])
    left, right = jnp.where(first, a, b), jnp.where(first, b, a)
    scale = 64 ** (-0.25)
    for p in range(pairs):
        half, at = (left, p * 128) if p < pairs // 2 else (right, p * 128 - hw)
        s = (half[:, at : at + 128] + vecs[1:2, lanes(p)]) * scale
        v = (half[:, hw + at : hw + at + 128] + vecs[2:3, lanes(p)]).astype(BF)
        phi = features(s, gh[p], gl[p])
        k = phi.astype(BF)
        s_out[:, lanes(p)] = s
        phi_out[:, lanes(p)] = phi
        feat_out[:, lanes(p)] = k
        v_out[:, lanes(p)] = v
        for r in range(tok.shape[0] // block):
            rows = slice(r * block, (r + 1) * block)
            state_out[r, :64, lanes(p)] = fold(tdot(k[rows], v[rows])).astype(BF)
            total = jnp.sum(k[rows].astype(F32), axis=0, keepdims=True)
            state_out[r, 64:, lanes(p)] = jnp.broadcast_to(total, (16, 128)).astype(BF)


def query_kernel(c_ref, tok, mine, other, vec, gh, gl, s_out, phi_out, feat_out):
    first = c_ref[0] == 0
    pairs = gh.shape[0]
    hw = pairs * 64
    a, b = dot(tok[...], mine[:, :hw]), dot(tok[...], other[:, :hw])
    left, right = jnp.where(first, a, b), jnp.where(first, b, a)
    for p in range(pairs):
        half, at = (left, p * 128) if p < pairs // 2 else (right, p * 128 - hw)
        s = (half[:, at : at + 128] + vec[0:1, lanes(p)]) * 64 ** (-0.25)
        phi = features(s, gh[p], gl[p])
        s_out[:, lanes(p)] = s
        phi_out[:, lanes(p)] = phi
        feat_out[:, lanes(p)] = phi.astype(BF)


def halo_kernel(c_ref, halo, mine, other, vec, gh, gl, hk_out, hv_out):
    first, inner = c_ref[0] == 0, c_ref[1] > 0
    pairs = gh.shape[0]
    hw = pairs * 64
    a, b = dot(halo[...], mine[:, hw : 3 * hw]), dot(halo[...], other[:, hw : 3 * hw])
    left, right = jnp.where(first, a, b), jnp.where(first, b, a)
    for p in range(pairs):
        half, at = (left, p * 128) if p < pairs // 2 else (right, p * 128 - hw)
        s = (half[:, at : at + 128] + vec[1:2, lanes(p)]) * 64 ** (-0.25)
        v = half[:, hw + at : hw + at + 128] + vec[2:3, lanes(p)]
        hk_out[:, lanes(p)] = jnp.where(inner, features(s, gh[p], gl[p]), 0.0).astype(BF)
        hv_out[:, lanes(p)] = jnp.where(inner, v, 0.0).astype(BF)


def window_weights(base):
    turned = pltpu.roll(jnp.broadcast_to(base, (128, 256)), 0, 1, stride=1, stride_axis=0)
    row = lax.broadcasted_iota(jnp.int32, (128, 256), 0)
    col = lax.broadcasted_iota(jnp.int32, (128, 256), 1)
    return jnp.where(col > row + 128, 0.0, turned - jnp.where(col < 128, base[:, 255:256], 0.0))


def pair_at(step, c, pairs):
    return (step + (pairs // 2) * (1 - c)) % pairs


def block_diagonal(packed):
    return two_heads(packed)


def attention_kernel(q, k, v, hk, hv, table, state, far, context_out, turned_out, ratio_out, denom_out):
    ones = head_ones()
    wmat = jnp.concatenate([window_weights(table[0, 0:1]), window_weights(table[0, 1:2])], axis=0)
    far_row = far[0:1]
    for r in range(q.shape[0] // 128):
        rows = slice(r * 128, (r + 1) * 128)
        qr = q[rows]
        kw = jnp.concatenate([hk[rows], k[rows]], axis=0)
        vw = jnp.concatenate([hv[rows], v[rows]], axis=0)
        weighted = dot_t(two_heads(qr), kw) * wmat
        numer = fold(dot(weighted.astype(BF), vw))
        near = jnp.sum(weighted, axis=1, keepdims=True)
        near = fold(jnp.broadcast_to(near, (256, 128)))
        bd = block_diagonal(state[r, :64])
        total = state[r, 64:80].astype(F32)[0:1]
        numer = numer + far_row * dot(qr, bd)
        denom = near + far_row * head_sums(qr.astype(F32) * total, ones)
        ratio = numer / denom
        context_out[rows] = ratio.astype(BF)
        turned_out[:, rows] = ratio.T.astype(BF)
        ratio_out[rows] = ratio
        denom_out[rows] = denom


def normed(x):
    centred = x - jnp.mean(x, axis=-1, keepdims=True)
    rstd = lax.rsqrt(jnp.mean(centred * centred, axis=-1, keepdims=True) + EPS)
    return centred * rstd, rstd


def norm_back(dy, xhat, rstd, gain):
    d = dy * gain
    return rstd * (
        d - jnp.mean(d, axis=-1, keepdims=True) - xhat * jnp.mean(d * xhat, axis=-1, keepdims=True)
    )


def col_sums(a):
    return jnp.sum(a, axis=0, keepdims=True)


def middle_kernel(
    count, context, tok, cot, vec, bu, ratio, denom, q, state, far, rest_hbm, *more,
):
    blocks_hbm, more = more[:count], more[count:]
    (
        out, dresid_out, dattn_out, dn_out, later_out, sums_out, near_out, du_sums_out, down_hbm, up_hbm,
        w, wd, gp, grads, in_sems, out_sems,
    ) = more
    width, step = tok.shape[1], wd.shape[1]
    hw = width // 2
    loads = []
    for i in range(count):
        loads.append(pltpu.make_async_copy(blocks_hbm[i], w.at[i], in_sems.at[i]))
    for i in range(count):
        wd_block = rest_hbm.at[pl.ds(i * step, step), pl.ds(0, width)]
        loads.append(pltpu.make_async_copy(wd_block, wd.at[i], in_sems.at[count + i]))
    for load in loads:
        load.start()
    for load in loads[:count]:
        load.wait()
    attn = jnp.concatenate([dot(context[...], w[i, :, step:]) for i in range(count)], axis=1)
    xhat, rstd = normed(tok[...].astype(F32) + attn + vec[3:4])
    hidden = xhat * vec[4:5] + vec[5:6]
    h_low = hidden.astype(BF)
    lower = hidden + vec[6:7]
    actives = []
    for i in range(count):
        cols = slice(i * step, (i + 1) * step)
        upper = dot(h_low, w[i, :, :step]) + bu[:, cols]
        cdf = 0.5 * (1.0 + lax.erf(upper * 2.0 ** (-0.5)))
        pdf = jnp.exp(-0.5 * upper * upper) * (2.0 * math.pi) ** (-0.5)
        gp[:, cols] = (cdf + upper * pdf).astype(BF)
        actives.append((upper * cdf).astype(BF))
        loads[count + i].wait()
        lower = lower + dot(actives[-1], wd[i])
    xhat2, rstd2 = normed(lower)
    gain2 = vec[7:8]
    out[...] = xhat2 * gain2 + vec[8:9]
    dy = cot[...].astype(F32)
    d_hidden = norm_back(dy, xhat2, rstd2, gain2)
    d_low = d_hidden.astype(BF)
    sums_out[0:1] = col_sums(d_low.astype(F32))
    sums_out[1:2] = col_sums(dy * xhat2)
    sums_out[2:3] = col_sums(dy)
    stores = []
    for i in range(count):
        cols = slice(i * step, (i + 1) * step)
        d_upper = (dot_t(d_low, wd[i]) * gp[:, cols].astype(F32)).astype(BF)
        du_sums_out[:, cols] = jnp.broadcast_to(col_sums(d_upper.astype(F32)), (8, step))
        d_hidden = d_hidden + dot_t(d_upper, w[i, :, :step])
        grads[2 * i] = tdot(h_low, d_upper).astype(BF)
        stores.append(pltpu.make_async_copy(grads.at[2 * i], up_hbm.at[i], out_sems.at[2 * i]))
        stores[-1].start()
        grads[2 * i + 1] = tdot(actives[i], d_low).astype(BF)
        block = down_hbm.at[pl.ds(i * step, step), pl.ds(0, width)]
        stores.append(pltpu.make_async_copy(grads.at[2 * i + 1], block, out_sems.at[2 * i + 1]))
        stores[-1].start()
    d_resid = norm_back(d_hidden, xhat, rstd, vec[4:5])
    dresid_out[...] = d_resid
    d_attn = d_resid.astype(BF)
    dattn_out[...] = d_attn
    sums_out[3:4] = col_sums(d_attn.astype(F32))
    sums_out[4:5] = col_sums(d_hidden * xhat)
    sums_out[5:6] = col_sums(d_hidden)
    part = width // count
    d_context = sum(dot_t(d_resid[:, i * part : (i + 1) * part].astype(BF), w[i, :, step:]) for i in range(count))
    ones = head_ones()
    pick = jnp.where(
        lax.broadcasted_iota(jnp.int32, (width, 128), 0) == 64 * lax.broadcasted_iota(jnp.int32, (width, 128), 1), 1.0, 0.0
    ).astype(BF)
    all_denoms = []
    for p in range(width // 128):
        dc = d_context[:, lanes(p)]
        inverse = 1.0 / denom[:, lanes(p)]
        dn = (dc * inverse).astype(BF)
        dd = (-head_sums(dc * ratio[:, lanes(p)], ones) * inverse).astype(BF)
        dn_out[:, lanes(p)] = dn
        all_denoms.append(dd)
        near = jnp.zeros((1, 128), F32)
        for r in range(tok.shape[0] // 128):
            rows = slice(r * 128, (r + 1) * 128)
            qr = q[rows, lanes(p)]
            packed = fold(tdot(qr, dn[rows]))
            total = col_sums(qr.astype(F32) * dd[rows].astype(F32))
            far_row = far[0:1, lanes(p)]
            later_out[r, :64, lanes(p)] = (far_row * packed).astype(BF)
            later_out[r, 64:, lanes(p)] = jnp.broadcast_to(far_row * total, (16, 128)).astype(BF)
            held = state[r, :, lanes(p)].astype(F32)
            near = near + col_sums(held[:64] * packed) + held[64:65] * total
        near_out[:, lanes(p)] = jnp.broadcast_to(near, (8, 128))
    dn_out[:, width:] = dot(jnp.concatenate(all_denoms, axis=1), pick).astype(BF)
    for store in stores:
        store.wait()


def spread(dn, p):
    lane = lax.broadcasted_iota(jnp.int32, dn.shape, 1)
    wide = dn.astype(F32)
    return [jnp.sum(jnp.where(lane == 2 * p + h, wide, 0.0), axis=1, keepdims=True) for h in (0, 1)]


def query_back_kernel(
    c_ref, tok, context, dattn, q, k, v, hk, hv, dn, dd, table, state, far, phi, s, gh, gl, near,
    dq_out, keep_out, send_out, pos_out, sums_out,
):
    steps = pl.num_programs(0)
    p = pair_at(pl.program_id(0), c_ref[0], steps)
    ones = head_ones()
    wmat = jnp.concatenate([window_weights(table[0, 0:1]), window_weights(table[0, 1:2])], axis=0)
    far_row = far[0:1]
    first = left_lanes((128, 128))
    pieces = jnp.zeros((256, 256), F32)
    grads = []
    for r in range(q.shape[0] // 128):
        rows = slice(r * 128, (r + 1) * 128)
        kw = jnp.concatenate([hk[rows], k[rows]], axis=0)
        vw = jnp.concatenate([hv[rows], v[rows]], axis=0)
        scores = dot_t(two_heads(q[rows]), kw)
        d0, d1 = spread(dd[rows], p)
        dnr = dn[rows]
        dw = dot_t(two_heads(dnr), vw) + jnp.concatenate([d0, d1], axis=0)
        pieces = pieces + dw * scores
        ds = (dw * wmat).astype(BF)
        bd = block_diagonal(state[r, :64])
        total = state[r, 64:80].astype(F32)[0:1]
        dq = fold(dot(ds, kw)) + far_row * (dot_t(dnr, bd) + jnp.where(first, d0, d1) * total)
        grads.append(
            features_back(dq * phi[rows], s[rows], gh[0], gl[0], ones, 64 ** (-0.25))
        )
    dq = jnp.concatenate(grads, axis=0)
    dq_out[...] = dq
    sums_out[...] = jnp.broadcast_to(col_sums(dq.astype(F32)), sums_out.shape)
    grad = jnp.concatenate([dot(tok[...], dq), dot(context[...], dattn[...])], axis=1).astype(BF)
    place_half(grad, keep_out, send_out)
    row = lax.broadcasted_iota(jnp.int32, (256, 256), 0)
    col = lax.broadcasted_iota(jnp.int32, (256, 256), 1)
    mirror = jnp.where(row + col == 255, 1.0, 0.0).astype(BF)
    high, low = parts(jnp.where(col <= row % 128 + 128, pieces, 0.0))
    mirrored = dot(high, mirror) + dot(low, mirror)
    lane = lax.broadcasted_iota(jnp.int32, (1, 256), 1)
    for h in (0, 1):
        rows = slice(h * 128, (h + 1) * 128)
        by_distance = col_sums(pltpu.roll(mirrored[rows], 129, 1, stride=1, stride_axis=0))
        plain = col_sums(pieces[rows])
        apart = jnp.where(lane >= 128, by_distance, 0.0) - jnp.where(lane < 128, plain, 0.0)
        state_part = jnp.where(lane[:, :128] // 64 == h, near[0:1], 0.0)
        far_sum = jnp.sum(apart, axis=1, keepdims=True) + jnp.sum(state_part, axis=1, keepdims=True)
        pos_out[0, h : h + 1] = jnp.where(lane < 128, by_distance, far_sum)


def place_half(grad, keep_out, send_out):
    early = pl.program_id(0) < pl.num_programs(0) // 2

    @pl.when(early)
    def _():
        send_out[...] = grad

    @pl.when(jnp.logical_not(early))
    def _():
        keep_out[...] = grad


def key_back_kernel(
    c_ref, tok, q, k, v, dn, dd, qn, dnn, ddn, table, later, phi, s, gh, gl, rows_in,
    dk_out, dv_out, keep_out, send_out, small_out,
):
    p = pair_at(pl.program_id(0), c_ref[0], pl.num_programs(0))
    ones = head_ones()
    first, second = window_weights(table[0, 0:1]), window_weights(table[0, 1:2])
    tables = jnp.concatenate([first[:, 128:], second[:, 128:], first[:, :128], second[:, :128]], axis=0)
    dks, dvs = [], []
    for r in range(q.shape[0] // 128):
        rows = slice(r * 128, (r + 1) * 128)
        kr, vr = k[rows], v[rows]
        q4 = jnp.concatenate([two_heads(q[rows]), two_heads(qn[rows])], axis=0)
        dn4 = jnp.concatenate([two_heads(dn[rows]), two_heads(dnn[rows])], axis=0)
        dd4 = jnp.concatenate(spread(dd[rows], p) + spread(ddn[rows], p), axis=0)
        w = (dot_t(q4, kr) * tables).astype(BF)
        ds = ((dot_t(dn4, vr) + dd4) * tables).astype(BF)
        bd = block_diagonal(later[r, :64])
        total = later[r, 64:80].astype(F32)[0:1]
        dk = tdot(ds, q4) + dot_t(vr, bd) + total
        dvs.append((tdot(w, dn4) + dot(kr, bd)).astype(BF))
        dks.append(features_back(dk * phi[rows], s[rows], gh[0], gl[0], ones, 64 ** (-0.25)))
    dk, dv = jnp.concatenate(dks, axis=0), jnp.concatenate(dvs, axis=0)
    dk_out[...] = dk
    dv_out[...] = dv
    place_half(jnp.concatenate([dot(tok[...], dk), dot(tok[...], dv)], axis=1).astype(BF), keep_out, send_out)
    row = lax.broadcasted_iota(jnp.int32, (16, 128), 0)
    lane = lax.broadcasted_iota(jnp.int32, (16, 128), 1)
    late = jnp.where(row == 1, col_sums(dk.astype(F32)), 0.0) + jnp.where(row == 2, col_sums(dv.astype(F32)), 0.0)
    small_out[...] = tdot((rows_in[...] + late).astype(BF), jnp.where(row == lane, 1.0, 0.0).astype(BF)).astype(BF)


def tokens_kernel(c_ref, dresid, dq, dk, dv, mine, other, out):
    first = c_ref[0] == 0
    hw = dq.shape[1] // 2
    total = dresid[...]
    for i, d in enumerate((dq, dk, dv)):
        wide = d[...].astype(F32)
        a = jnp.where(first, wide[:, :hw], wide[:, hw:]).astype(BF)
        b = jnp.where(first, wide[:, hw:], wide[:, :hw]).astype(BF)
        cols = slice(i * hw, (i + 1) * hw)
        total = total + dot_t(a, mine[:, cols]) + dot_t(b, other[:, cols])
    out[...] = total


def unpack_kernel(packed, down_out, up_out):
    own, width = up_out.shape[0], down_out.shape[1]
    step = packed.shape[1] - width
    wide = packed[...].astype(F32)
    down_out[...] = wide[:, :width]
    for i in range(packed.shape[0] // own):
        up_out[:, i * step : (i + 1) * step] = wide[i * own : (i + 1) * own, width:]


def feature_blocks(matrix):
    heads, size, feats = matrix.shape
    zero = jnp.zeros((heads // 2, size, feats), F32)
    even, odd = matrix[0::2], matrix[1::2]
    half = jnp.full(zero.shape, -0.5, F32)
    blocks = jnp.concatenate(
        [
            jnp.concatenate([even, zero], axis=2),
            jnp.concatenate([zero, odd], axis=2),
            jnp.concatenate([half, zero], axis=2),
            jnp.concatenate([zero, half], axis=2),
        ],
        axis=1,
    )
    high = lax.reduce_precision(blocks, 8, 7)
    return high.astype(BF), (blocks - high).astype(BF)


def on_device(
    tokens,
    query_weight,
    query_bias,
    key_weight,
    key_bias,
    value_weight,
    value_bias,
    output_weight,
    output_bias,
    first_gain,
    first_shift,
    up_weight,
    up_bias,
    down_weight,
    down_bias,
    second_gain,
    second_shift,
    position_bias,
    feature_matrix,
    cotangent,
):
    at = Place()
    rows, block, width = tokens.shape
    heads, size, feats = feature_matrix.shape
    window = position_bias.shape[1] - 1
    pairs = heads // 2
    n = rows * block
    hw = width // 2
    ff = up_weight.shape[1]
    hf = ff // 2
    own = query_weight.shape[0]
    up_own = up_bias.shape[0] // own
    tok = tokens.reshape(n, width)
    cot = cotangent.reshape(n, width)
    flags = jnp.stack([at.c, at.s]).astype(jnp.int32)

    def arr(shape, kind):
        return jax.ShapeDtypeStruct(shape, kind)

    halo_tok = at.along(tok, 1)
    tok_t = tok.T

    vectors = (
        query_bias, key_bias, value_bias, output_bias, first_gain, first_shift,
        down_bias, second_gain, second_shift,
    )
    count = len(vectors)
    small = jnp.concatenate(vectors + (up_bias,)).reshape(count + up_own, own).T
    small = jnp.pad(small, ((0, 0), (0, 128 - small.shape[1])))
    slices = down_weight.shape[0] // own
    step, wo_step = ff // slices, width // slices

    def stacked(a):
        return jnp.concatenate(jnp.split(a, slices, axis=1), axis=0)

    rest = lax.all_gather(
        jnp.concatenate([down_weight, stacked(up_weight), stacked(output_weight)], axis=1), BOTH, axis=0, tiled=True
    )
    g1 = Gather(
        at,
        "qkv",
        jnp.concatenate([query_weight[:, :hw], key_weight[:, :hw], value_weight[:, :hw]], axis=1),
        jnp.concatenate([query_weight[:, hw:], key_weight[:, hw:], value_weight[:, hw:]], axis=1),
        small,
    )
    exp_bias = jnp.exp(position_bias)
    table = jnp.concatenate(
        [exp_bias[:, ::-1], jnp.broadcast_to(exp_bias[:, window:], (heads, block - 1))], axis=1
    ).reshape(pairs, 2, window + block)
    table = jnp.pad(table, ((0, 0), (0, 6), (0, 0)))
    far = jnp.broadcast_to(jnp.repeat(exp_bias[:, window], size)[None], (8, width))
    gh, gl = feature_blocks(feature_matrix)

    g1.step_core()
    g1.step_z()
    g1.step_one()
    g1.step_two()
    m1, o1 = g1.step_last(table, far, gh, gl, tok_t)

    wide32, wide16 = arr((n, width), F32), arr((n, width), BF)
    sums = arr((rows, 80, width), BF)
    sk, k_phi, k, v, local, vec = pl.pallas_call(
        key_kernel,
        out_shape=(wide32, wide32, wide16, wide16, sums, arr((16, width), F32)),
        in_specs=[SCALAR] + [WHOLE] * 5,
        out_specs=(WHOLE,) * 6,
        compiler_params=params(48),
        cost_estimate=cost(5),
        name="keys",
    )(flags, tok, m1, o1, gh, gl)
    scan = Before(at, "before", local, False)
    scan.step_beside()
    sq, q_phi, q = pl.pallas_call(
        query_kernel,
        out_shape=(wide32, wide32, wide16),
        in_specs=[SCALAR] + [WHOLE] * 6,
        out_specs=(WHOLE,) * 3,
        compiler_params=params(48),
        cost_estimate=cost(3),
        name="queries",
    )(flags, tok, m1, o1, vec, gh, gl)
    scan.step_z(q)
    hk, hv = pl.pallas_call(
        halo_kernel,
        out_shape=(wide16, wide16),
        in_specs=[SCALAR] + [WHOLE] * 6,
        out_specs=(WHOLE,) * 2,
        compiler_params=params(48),
        cost_estimate=cost(2),
        name="halo",
    )(flags, after(halo_tok, *scan.done), m1, o1, vec, gh, gl)
    q_next = at.along(q, -1)
    before = scan.step_last(hk, q_next)
    b_u = m1[:, 3 * hw + count : 3 * hw + count + up_own].reshape(at.n, own, up_own)
    b_u = jnp.swapaxes(after(b_u, hk), 1, 2).reshape(1, ff).astype(F32)

    def columns(height=n):
        return pl.BlockSpec((height, 128), lambda p, *_: (0, p))

    table_spec = pl.BlockSpec((1, 8, window + block), lambda p, *_: (p, 0, 0))
    sums_spec = pl.BlockSpec((rows, 80, 128), lambda p, *_: (0, 0, p))
    g_spec = pl.BlockSpec((1, 256, 128), lambda p, *_: (p, 0, 0))
    tok_spec = pl.BlockSpec((width, n), lambda p, *_: (0, 0))
    dd_spec = pl.BlockSpec((n, 128), lambda p, *_: (0, pairs))
    context, context_t, ratio, denom = pl.pallas_call(
        attention_kernel,
        grid=(pairs,),
        out_shape=(wide16, arr((width, n), BF), wide32, wide32),
        in_specs=[columns()] * 5 + [table_spec, sums_spec, columns(8)],
        out_specs=(columns(), pl.BlockSpec((128, n), lambda p, *_: (p, 0)), columns(), columns()),
        compiler_params=params(32),
        cost_estimate=cost(5),
        name="attention",
    )(q, k, v, hk, hv, table, before, far)

    split = rest.reshape(at.n, slices, own, rest.shape[1])
    blocks = [split[:, i, :, width:].reshape(width, step + wo_step) for i in range(slices)]
    away = pl.BlockSpec(memory_space=pl.ANY)
    out, d_resid, d_attn, dn, local, sums2, near, du_sums, g_down, g_up = pl.pallas_call(
        functools.partial(middle_kernel, slices),
        out_shape=(
            wide32, wide32, wide16, arr((n, width + 128), BF), sums, arr((8, width), F32), arr((8, width), F32),
            arr((8, ff), F32), arr((ff, width + step), BF), arr((slices, width, step), BF),
        ),
        in_specs=[WHOLE] * 10 + [away] * (1 + slices),
        out_specs=(WHOLE,) * 8 + (away,) * 2,
        scratch_shapes=[
            VMEM((slices, width, step + wo_step), BF),
            VMEM((slices, step, width), BF),
            VMEM((n, ff), BF),
            VMEM((2 * slices, width, step), BF),
            pltpu.SemaphoreType.DMA((2 * slices,)),
            pltpu.SemaphoreType.DMA((2 * slices,)),
        ],
        compiler_params=pltpu.CompilerParams(vmem_limit_bytes=38 * 2**20),
        cost_estimate=cost(20),
        name="middle",
    )(context, tok, cot, vec, b_u, ratio, denom, q, before, far, rest, *blocks)
    g_up = jnp.swapaxes(g_up.reshape(slices, at.n, own, step), 0, 1).reshape(ff, step)
    g_rest = lax.dynamic_update_slice(g_down, g_up, (0, width))
    s_rest = lax.psum_scatter(g_rest, BOTH, scatter_dimension=0, tiled=True)
    if own % 8 == 0:
        s_d, s_u = pl.pallas_call(
            unpack_kernel,
            out_shape=(arr((slices * own, width), F32), arr((own, ff), F32)),
            in_specs=[WHOLE],
            out_specs=(WHOLE,) * 2,
            compiler_params=params(48),
            cost_estimate=cost(1),
            name="unpack",
        )(s_rest)
    else:
        s_d = s_rest[:, :width].astype(F32)
        s_u = jnp.concatenate(jnp.split(s_rest[:, width:].astype(F32), slices, axis=0), axis=1)
    scan = Before(at, "later", local, True)
    scan.step_beside()
    dn_next = at.along(dn, -1)

    def turned(p, c):
        return pair_at(p, c[0], pairs)

    cols = pl.BlockSpec((n, 128), lambda p, c: (0, turned(p, c)))
    cols8 = pl.BlockSpec((8, 128), lambda p, c: (0, turned(p, c)))
    by_pair = pl.BlockSpec((1, 8, window + block), lambda p, c: (turned(p, c), 0, 0))
    sums_by_pair = pl.BlockSpec((rows, 80, 128), lambda p, c: (0, 0, turned(p, c)))
    g_by_pair = pl.BlockSpec((1, 256, 128), lambda p, c: (turned(p, c), 0, 0))
    kept = pl.BlockSpec((width, 256), lambda p, c: (0, jnp.maximum(p - pairs // 2, 0)))
    sent = pl.BlockSpec((width, 256), lambda p, c: (0, jnp.minimum(p, pairs // 2 - 1)))
    half = arr((width, 2 * hw), BF)
    dq, keep1, send1, pos, sums_q = pl.pallas_call(
        query_back_kernel,
        grid_spec=pltpu.PrefetchScalarGridSpec(
            num_scalar_prefetch=1,
            grid=(pairs,),
            in_specs=[tok_spec] * 2 + [cols] * 7 + [dd_spec, by_pair, sums_by_pair, cols8]
            + [cols] * 2 + [g_by_pair] * 2 + [cols8],
            out_specs=(cols, kept, sent, by_pair, cols8),
        ),
        out_shape=(wide16, half, half, arr((pairs, 8, 256), F32), arr((8, width), F32)),
        compiler_params=params(32),
        cost_estimate=cost(0.001),
        name="query_back",
    )(flags, after(tok_t, *scan.done, g_rest), context_t, d_attn, q, k, v, hk, hv, dn, dn, table, before, far, q_phi, sq, gh, gl, near)
    scan.step_z()
    later = scan.step_last(dq, dn_next)
    everywhere = Everywhere(at, exp_bias * pos[:, :2, : window + 1].reshape(heads, window + 1))
    everywhere.step(1)
    du = du_sums[0].reshape(at.n, up_own, own)
    du = jnp.swapaxes(du, 0, 1).reshape(up_own, width)
    nil = jnp.zeros((2, width), F32)
    early = jnp.concatenate([sums_q[:1], nil, sums2[3:6], sums2[:3], du], axis=0)
    early = jnp.pad(early, ((0, 16 - early.shape[0]), (0, 0)))
    dk, dv, keep0, send0, small = pl.pallas_call(
        key_back_kernel,
        grid_spec=pltpu.PrefetchScalarGridSpec(
            num_scalar_prefetch=1,
            grid=(pairs,),
            in_specs=[tok_spec] + [cols] * 4 + [dd_spec] + [cols] * 2
            + [dd_spec, by_pair, sums_by_pair] + [cols] * 2 + [g_by_pair] * 2
            + [pl.BlockSpec((16, 128), lambda p, c: (0, turned(p, c)))],
            out_specs=(cols, cols, kept, sent, pl.BlockSpec((128, 128), lambda p, c: (turned(p, c), 0))),
        ),
        out_shape=(wide16, wide16, half, half, arr((width, 128), BF)),
        compiler_params=params(32),
        cost_estimate=cost(0.001),
        name="key_back",
    )(flags, after(tok_t, *everywhere.done), q, k, v, dn, dn, q_next, dn_next, dn_next, table, later, k_phi, sk, gh, gl, early)

    r0 = Scatter(at, "d_qkv", (keep1, keep0, small), (send1, send0, small))
    r0.step_core()
    everywhere.step(2, dk)
    r0.step_one(*everywhere.done)
    everywhere.step(4, *r0.done)
    r0.step_two(*everywhere.done)
    two0 = r0.done
    r0.step_z()
    position_grad = everywhere.step_z(*two0)
    s_qkv = r0.step_last()
    d_tokens = pl.pallas_call(
        tokens_kernel,
        out_shape=wide32,
        in_specs=[SCALAR] + [WHOLE] * 6,
        out_specs=WHOLE,
        compiler_params=params(40),
        cost_estimate=cost(0.001),
        name="tokens",
    )(flags, d_resid, dq, dk, dv, m1, o1)

    def woven(pair, at):
        return jnp.concatenate(
            [half[:, at + p * 256 : at + p * 256 + 128] for half in pair for p in range(pairs // 2)], axis=1
        )

    s_small = s_qkv[0][:, 4 * hw :]
    bq, bk, bv, bo, sg1, ss1, bd, sg2, ss2 = [s_small[:, i] for i in range(count)]
    bu = s_small[:, count : count + up_own].T.reshape(-1)
    return (
        out.reshape(rows, block, width),
        d_tokens.reshape(rows, block, width),
        woven(s_qkv, 0),
        bq,
        woven(s_qkv, 2 * hw),
        bk,
        woven(s_qkv, 2 * hw + 128),
        bv,
        woven(s_qkv, 128),
        bo,
        sg1,
        ss1,
        s_u,
        bu,
        s_d,
        bd,
        sg2,
        ss2,
        position_grad,
    )


def solution(mesh):
    matrix, vector, split = P(BOTH, None), P(BOTH), P("rows", "seq", None)
    return jax.shard_map(
        on_device,
        mesh=mesh,
        in_specs=(split,)
        + (matrix, vector) * 4
        + (vector, vector)
        + (matrix, vector) * 2
        + (vector, vector)
        + (P(), P(), split),
        out_specs=(split, split)
        + (matrix, vector) * 4
        + (vector, vector)
        + (matrix, vector) * 2
        + (vector, vector)
        + (P(),),
        check_vma=False,
    )
```
